32 devices in a mesh: dp: 4 (over y, x), tensor: 8 (over z, core).
Axes of the slice: x: 2, y: 2, z: 4, core: 2. Of those that a mesh axis runs over, the one named last changes fastest.
Arguments:
- hidden: bfloat16 [512, 53248], P('dp', 'tensor'), may hold values from -0.29882812 to 0.29882812
- upstream: bfloat16 [512, 8192], P('dp'), may hold values from -6 to 6
- weight: bfloat16 [53248, 8192], P('tensor', 'dp'), may hold values from -0.0625 to 0.0625
- scales: float32 [416, 8192], P('tensor', 'dp'), may hold values from 0.3 to 3
- clip_mask: int32 [416, 8192], P('tensor', 'dp'), may hold values 0 or 1
- rot_block: float32 [52, 52], replicated, may hold values from -0.875 to 0.875
Outputs:
- grad_hidden: bfloat16 [512, 53248], P('dp', 'tensor')
- grad_weight: bfloat16 [53248, 8192], P('tensor', 'dp')
- grad_scales: float32 [416, 8192], P('tensor', 'dp')
The draws below stay inside these ranges and needn't reach their ends.
All inputs are finite; a program needn't handle non-finite values. No bound on the sum of `clip_mask` on one device may be relied on, other than what follows from the above.
Results may differ from the reference program's by a relative error of at most 0.023.
Values may be sent and summed in bfloat16 or wider, within the bound.
No kernel may reach another device: no remote copies, remote signals or barrier semaphores. Data moves between devices by JAX's collectives and lax.ppermute only.
A program may use at most 192 MiB of HBM per device.

```python
import math
import jax
import jax.numpy as jnp
from jax import lax

D = 8192
FF = 53248
HB = 128
GROUP = 128
TOKENS = 512
BLOCKS = 52
GROUPS = 416
N_TENSOR = 8


def set_ends(array, rng, least, largest):
    shape = array.shape
    place = [jax.random.randint(jax.random.fold_in(rng, axis), (), 0, shape[axis]) for axis in range(len(shape))]
    array = array.at[tuple(place)].set(least)
    longest = shape.index(max(shape))
    place[longest] = (place[longest] + 1) % shape[longest]
    return array.at[tuple(place)].set(largest)


def block_scale(own_key, shape, shards, low, high):
    def one(dim, blocks):
        steps = jax.random.uniform(jax.random.fold_in(jax.random.fold_in(own_key, 6), dim), (blocks,), jnp.float32, low / len(shards), high / len(shards))
        return jnp.repeat(jnp.exp(steps), shape[dim] // blocks).reshape((-1,) + (1,) * (len(shape) - dim - 1))

    factor_of = one(*shards[0])
    for cut in shards[1:]:
        factor_of = factor_of * one(*cut)
    return factor_of


def gaussian(own_key, shape, scale, bound, shards=(), kind=jnp.bfloat16):
    entries = jax.random.normal(own_key, shape, jnp.float32) * scale
    if len(shards) > 0:
        entries = block_scale(own_key, shape, shards, -0.22, 0.18) * entries
    return jnp.clip(entries, min=-bound, max=bound).astype(kind)


def setup_inputs(seed: int = 0) -> dict:
    key_list = jax.random.split(jax.random.key(seed), 7)
    return {
        "hidden": gaussian(key_list[0], (TOKENS, FF), 0.05, 0.29882812, ((0, 4), (1, 8))),
        "upstream": gaussian(key_list[1], (TOKENS, D), 1.0, 6.0, ((0, 4),)),
        "weight": gaussian(key_list[2], (FF, D), D ** -0.5, 0.0625, ((0, 8), (1, 4))),
        "scales": jnp.clip(jnp.exp(math.log(3.0) - 2.3025851 * jax.random.uniform(key_list[3], (GROUPS, D), jnp.float32) ** block_scale(key_list[3], (GROUPS, D), ((0, 8), (1, 4)), -0.2, 0.2)), 0.3, 3.0),
        "clip_mask": set_ends((jax.random.randint(key_list[4], (GROUPS, D), 0, 4) < 3).astype(jnp.int32), jax.random.fold_in(key_list[4], 1), 0, 1),
        "rot_block": gaussian(key_list[5], (BLOCKS, BLOCKS), BLOCKS ** -0.5, 0.875, (), jnp.float32),
    }


def sign_table(size):
    index = jnp.arange(size, dtype=jnp.int32)
    both = index[:, None] & index[None, :]
    parity = jnp.zeros((size, size), jnp.int32)
    for shift_bit in range(max(size.bit_length() - 1, 0)):
        parity = parity ^ ((both >> shift_bit) & 1)
    return 1.0 - 2.0 * parity.astype(jnp.float32)


def reference(hidden, upstream, weight, scales, clip_mask, rot_block):
    high = lax.Precision.HIGHEST
    blocks = FF // (N_TENSOR * HB)
    width = FF // N_TENSOR
    inner = sign_table(HB)
    cross = sign_table(N_TENSOR)
    shaped = hidden.astype(jnp.float32).reshape(TOKENS, N_TENSOR, blocks, HB)
    first = jnp.einsum('ntkb,bd->ntkd', shaped, inner, precision=high)
    local = (jnp.einsum('ntkd,kc->ntcd', first, rot_block, precision=high) * (HB ** -0.5)).astype(jnp.bfloat16)
    rotated = jnp.einsum('ntcd,ts->nscd', local.astype(jnp.float32), cross, precision=high) * (N_TENSOR ** -0.5)
    rotated = rotated.astype(jnp.bfloat16).reshape(TOKENS, N_TENSOR, width).transpose(1, 0, 2)
    per_group = width // GROUP
    weight_parts = weight.reshape(N_TENSOR, width, D)
    scale_parts = scales.reshape(N_TENSOR, per_group, D)
    mask_parts = clip_mask.reshape(N_TENSOR, per_group, D)

    def one_shard(items):
        rows_rot, w_part, s_part, m_part = items
        w_wide = w_part.astype(jnp.float32).reshape(per_group, GROUP, D)
        quant = (w_wide * s_part[:, None, :]).reshape(width, D).astype(jnp.bfloat16)
        grad = jnp.dot(rows_rot.T, upstream, preferred_element_type=jnp.float32).reshape(per_group, GROUP, D)
        g_weight = (m_part.astype(jnp.float32)[:, None, :] * s_part[:, None, :] * grad).reshape(width, D).astype(jnp.bfloat16)
        g_scale = jnp.sum(grad * w_wide, axis=1)
        g_rot = jnp.dot(upstream, quant.T, preferred_element_type=jnp.float32).astype(jnp.bfloat16)
        return g_weight, g_scale, g_rot

    g_weight, g_scale, g_rot = lax.map(one_shard, (rotated, weight_parts, scale_parts, mask_parts))
    grad_weight = g_weight.reshape(FF, D)
    grad_scales = g_scale.reshape(FF // GROUP, D)
    g_rot = g_rot.transpose(1, 0, 2).reshape(TOKENS, N_TENSOR, blocks, HB).astype(jnp.float32)
    mixed = (jnp.einsum('nscd,ts->ntcd', g_rot, cross, precision=high) * (N_TENSOR ** -0.5)).astype(jnp.bfloat16)
    back = jnp.einsum('ntcd,bd->ntcb', mixed.astype(jnp.float32), inner, precision=high)
    grad_hidden = (jnp.einsum('ntcb,kc->ntkb', back, rot_block, precision=high) * (HB ** -0.5)).astype(jnp.bfloat16)
    return grad_hidden.reshape(TOKENS, FF), grad_weight, grad_scales
```

```python
import functools

import jax
import jax.numpy as jnp
from jax import lax
from jax.experimental import pallas as pl
from jax.experimental.pallas import tpu as pltpu
from jax.sharding import PartitionSpec as P

HB = 128
GROUP = 128
SUB = 16
F32 = jnp.float32
BF16 = jnp.bfloat16


def chunk_plan(groups):
    if groups % 4:
        return (groups,), 1
    units = groups // 4
    count = min(4, units)
    sizes = [units // count + (1 if i < units % count else 0) for i in range(count)]
    return tuple(4 * size for size in sizes), 4


def nt_dot(a, b):
    return lax.dot_general(a, b, (((1,), (1,)), ((), ())), preferred_element_type=F32)


def nn_dot(a, b):
    return lax.dot_general(a, b, (((1,), (0,)), ((), ())), preferred_element_type=F32)


def tn_dot(a, b):
    return lax.dot_general(a, b, (((0,), (0,)), ((), ())), preferred_element_type=F32)


def split2(value):
    high = value.astype(BF16)
    return high, (value - high.astype(F32)).astype(BF16)


def sign_matrix(size):
    both = lax.broadcasted_iota(jnp.int32, (size, size), 0) & lax.broadcasted_iota(
        jnp.int32, (size, size), 1
    )
    parity = jnp.zeros((size, size), jnp.int32)
    for bit in range(size.bit_length() - 1):
        parity = parity ^ ((both >> bit) & 1)
    return (1 - 2 * parity).astype(F32).astype(BF16)


def build_mixing(rot_ref, high_ref, low_ref, sign_ref, transposed):
    blocks = rot_ref.shape[0]
    size = blocks * SUB
    row = lax.broadcasted_iota(jnp.int32, (size, blocks), 0)
    col = lax.broadcasted_iota(jnp.int32, (size, blocks), 1)
    pick = ((row >> 4) == col).astype(F32).astype(BF16)
    rows = lax.broadcasted_iota(jnp.int32, (size, size), 0)
    cols = lax.broadcasted_iota(jnp.int32, (size, size), 1)
    same = (rows & (SUB - 1)) == (cols & (SUB - 1))
    for part, out_ref in zip(split2(rot_ref[...]), (high_ref, low_ref)):
        spread = nt_dot(pick, part) if transposed else nn_dot(pick, part)
        full = nt_dot(spread.astype(BF16), pick)
        out_ref[...] = jnp.where(same, full, 0.0).astype(BF16)
    sign_ref[...] = sign_matrix(HB)


def mix_rows(stacked, high_ref, low_ref, sign_ref):
    mixed = nn_dot(high_ref[...], stacked) + nn_dot(low_ref[...], stacked)
    results = []
    for part in range(stacked.shape[1] // HB):
        high, low = split2(mixed[:, part * HB : (part + 1) * HB])
        both = nn_dot(high, sign_ref[...]) + nn_dot(low, sign_ref[...])
        results.append((both * HB ** (-0.5)).astype(BF16))
    return results


def forward_kernel(sizes, x_ref, rot_ref, *refs):
    outs, (high_ref, low_ref, sign_ref) = refs[: len(sizes)], refs[len(sizes) :]
    blocks = rot_ref.shape[0]

    @pl.when(pl.program_id(0) == 0)
    def _():
        build_mixing(rot_ref, high_ref, low_ref, sign_ref, True)

    parts = x_ref.shape[0] // SUB
    stacked = jnp.concatenate(
        [
            jnp.concatenate(
                [
                    x_ref[j * SUB : (j + 1) * SUB, k * HB : (k + 1) * HB]
                    for k in range(blocks)
                ],
                axis=0,
            )
            for j in range(parts)
        ],
        axis=1,
    )
    for j, result in enumerate(mix_rows(stacked, high_ref, low_ref, sign_ref)):
        start = 0
        for size, out_ref in zip(sizes, outs):
            piece = result[start * SUB : (start + size) * SUB]
            out_ref[:, j * SUB : (j + 1) * SUB, :] = piece.reshape(size, SUB, HB)
            start += size


def backward_kernel(sizes, *refs):
    ins, (rot_ref, out_ref, high_ref, low_ref, sign_ref) = refs[: len(sizes)], refs[len(sizes) :]
    blocks = rot_ref.shape[0]

    @pl.when(pl.program_id(0) == 0)
    def _():
        build_mixing(rot_ref, high_ref, low_ref, sign_ref, False)

    parts = out_ref.shape[0] // SUB
    stacked = jnp.concatenate(
        [
            jnp.concatenate(
                [
                    in_ref[:, j * SUB : (j + 1) * SUB, :].reshape(size * SUB, HB)
                    for size, in_ref in zip(sizes, ins)
                ],
                axis=0,
            )
            for j in range(parts)
        ],
        axis=1,
    )
    for j, result in enumerate(mix_rows(stacked, high_ref, low_ref, sign_ref)):
        for k in range(blocks):
            out_ref[j * SUB : (j + 1) * SUB, k * HB : (k + 1) * HB] = result[
                k * SUB : (k + 1) * SUB
            ]


def local_scratch(blocks):
    return [
        pltpu.VMEM((blocks * SUB, blocks * SUB), BF16),
        pltpu.VMEM((blocks * SUB, blocks * SUB), BF16),
        pltpu.VMEM((HB, HB), BF16),
    ]


def local_cost(rows, blocks):
    size = blocks * SUB
    return pl.CostEstimate(
        flops=4 * size * size * (rows // SUB) * HB,
        bytes_accessed=4 * rows * blocks * HB,
        transcendentals=0,
    )


def local_forward(hidden, rot_block, sizes):
    rows, width = hidden.shape
    blocks = width // HB
    step = 2 * SUB
    return pl.pallas_call(
        functools.partial(forward_kernel, sizes),
        grid=(rows // step,),
        in_specs=[
            pl.BlockSpec((step, width), lambda i: (i, 0)),
            pl.BlockSpec((blocks, blocks), lambda i: (0, 0)),
        ],
        out_specs=[pl.BlockSpec((size, step, HB), lambda i: (0, i, 0)) for size in sizes],
        out_shape=[jax.ShapeDtypeStruct((size, rows, HB), BF16) for size in sizes],
        scratch_shapes=local_scratch(blocks),
        compiler_params=pltpu.CompilerParams(vmem_limit_bytes=32 << 20),
        cost_estimate=local_cost(rows, blocks),
        name="local_forward",
    )(hidden, rot_block)


def local_backward(mixed, rot_block, sizes):
    rows = mixed[0].shape[1]
    blocks = rot_block.shape[0]
    step = 2 * SUB
    return pl.pallas_call(
        functools.partial(backward_kernel, sizes),
        grid=(rows // step,),
        in_specs=[pl.BlockSpec((size, step, HB), lambda i: (0, i, 0)) for size in sizes]
        + [pl.BlockSpec((blocks, blocks), lambda i: (0, 0))],
        out_specs=pl.BlockSpec((step, blocks * HB), lambda i: (i, 0)),
        out_shape=jax.ShapeDtypeStruct((rows, blocks * HB), BF16),
        scratch_shapes=local_scratch(blocks),
        compiler_params=pltpu.CompilerParams(vmem_limit_bytes=32 << 20),
        cost_estimate=local_cost(rows, blocks),
        name="local_backward",
    )(*mixed, rot_block)


def units_kernel(first, per, up_ref, w_ref, s_ref, out_ref, quant_ref):
    base = first + pl.program_id(0) * per
    for g in range(per):
        rows = slice(g * GROUP, (g + 1) * GROUP)
        quant_ref[rows, :] = (w_ref[rows, :].astype(F32) * s_ref[pl.ds(base + g, 1), :]).astype(
            BF16
        )
    result = nt_dot(up_ref[...], quant_ref[...]).astype(BF16)
    tokens = out_ref.shape[2]
    for p in range(out_ref.shape[0]):
        for g in range(per):
            out_ref[p, g] = result[p * tokens : (p + 1) * tokens, g * GROUP : (g + 1) * GROUP]


def unit_grads(up, weight, scales, first, size, per, parts):
    tokens, cols = up.shape
    rows = tokens // parts
    offset = first // per
    return pl.pallas_call(
        functools.partial(units_kernel, first, per),
        grid=(size // per,),
        in_specs=[
            pl.BlockSpec((tokens, cols), lambda i: (0, 0)),
            pl.BlockSpec((per * GROUP, cols), lambda i: (offset + i, 0)),
            pl.BlockSpec(scales.shape, lambda i: (0, 0)),
        ],
        out_specs=pl.BlockSpec((parts, per, rows, HB), lambda i: (0, i, 0, 0)),
        out_shape=jax.ShapeDtypeStruct((parts, size, rows, HB), BF16),
        scratch_shapes=[pltpu.VMEM((per * GROUP, cols), BF16)],
        compiler_params=pltpu.CompilerParams(vmem_limit_bytes=40 << 20),
        cost_estimate=pl.CostEstimate(
            flops=2 * tokens * cols * size * GROUP,
            bytes_accessed=2 * cols * size * GROUP + 2 * tokens * (cols + size * GROUP),
            transcendentals=0,
        ),
        name="unit_grads",
    )(up, weight, scales)


def weights_kernel(first, per, rot_ref, up_ref, w_ref, s_ref, m_ref, *refs):
    gw_ref, gs_ref = refs[-2:]
    step = pl.program_id(0)
    base = first + step * per
    parts = rot_ref.shape[0]
    left = jnp.concatenate(
        [jnp.concatenate([rot_ref[p, g] for p in range(parts)], axis=0) for g in range(per)], axis=1
    )
    cols = up_ref.shape[1]
    tile = min(512, cols)
    for e in range(cols // tile):
        span = slice(e * tile, (e + 1) * tile)
        grad = tn_dot(left, up_ref[:, span])
        for g in range(per):
            rows = slice(g * GROUP, (g + 1) * GROUP)
            piece = grad[rows]
            scale = s_ref[pl.ds(base + g, 1), span]
            kept = m_ref[pl.ds(base + g, 1), span].astype(F32) * scale
            gw_ref[rows, span] = (piece * kept).astype(BF16)
            gs_ref[pl.ds(step * per + g, 1), span] = jnp.sum(
                piece * w_ref[rows, span].astype(F32), axis=0, keepdims=True
            )


def weight_grads(rotated, up, weight, scales, mask, buffer, first, size, per):
    parts, _, rows, _ = rotated.shape
    tokens, cols = up.shape
    offset = first // per
    specs = [
        pl.BlockSpec((parts, per, rows, HB), lambda i: (0, i, 0, 0)),
        pl.BlockSpec((tokens, cols), lambda i: (0, 0)),
        pl.BlockSpec((per * GROUP, cols), lambda i: (offset + i, 0)),
        pl.BlockSpec(scales.shape, lambda i: (0, 0)),
        pl.BlockSpec(scales.shape, lambda i: (0, 0)),
    ]
    args = [rotated, up, weight, scales, mask]
    aliases = {}
    if buffer is not None:
        aliases = {len(args): 0}
        args.append(buffer)
        specs.append(pl.BlockSpec(memory_space=pl.ANY))
    return pl.pallas_call(
        functools.partial(weights_kernel, first, per),
        grid=(size // per,),
        in_specs=specs,
        out_specs=[
            pl.BlockSpec((per * GROUP, cols), lambda i: (offset + i, 0)),
            pl.BlockSpec((size, cols), lambda i: (0, 0)),
        ],
        out_shape=[
            jax.ShapeDtypeStruct(weight.shape, BF16),
            jax.ShapeDtypeStruct((size, cols), F32),
        ],
        input_output_aliases=aliases,
        compiler_params=pltpu.CompilerParams(vmem_limit_bytes=40 << 20),
        cost_estimate=pl.CostEstimate(
            flops=2 * tokens * cols * size * GROUP,
            bytes_accessed=4 * cols * size * GROUP + 2 * tokens * (cols + size * GROUP),
            transcendentals=0,
        ),
        name="weight_grads",
    )(*args)


def partner(value, mask):
    size = lax.axis_size("tensor")
    return lax.ppermute(value, "tensor", [(i, i ^ mask) for i in range(size)])


def mix_across(value, masks):
    size = lax.axis_size("tensor")
    index = lax.axis_index("tensor")
    for place, mask in enumerate(masks):
        other = partner(value, mask).astype(F32)
        sign = jnp.where((index & mask) != 0, -1.0, 1.0).astype(F32)
        total = other + sign * value.astype(F32)
        if place == len(masks) - 1:
            total = total * size ** (-0.5)
        value = total.astype(BF16)
    return value


def gather_upstream(upstream):
    rows = upstream.shape[0]
    parts = lax.axis_size("dp")
    half = rows // 2
    core = lax.axis_index("tensor") & 1
    mine = lax.dynamic_slice_in_dim(upstream, core * half, half, axis=0)
    mine = lax.all_to_all(mine, "dp", split_axis=1, concat_axis=0, tiled=True)
    other = partner(mine, 1)
    cols = mine.shape[1]
    mine = mine.reshape(parts, half, cols)
    other = other.reshape(parts, half, cols)
    low = jnp.where(core == 0, mine, other)
    high = jnp.where(core == 0, other, mine)
    return jnp.concatenate([low, high], axis=1).reshape(parts * rows, cols)


def shards(hidden, upstream, weight, scales, clip_mask, rot_block):
    groups = scales.shape[0]
    parts = lax.axis_size("dp")
    size = lax.axis_size("tensor")
    sizes, per = chunk_plan(groups)
    starts = [sum(sizes[:i]) for i in range(len(sizes))]
    bits = [1 << i for i in range(size.bit_length() - 1)]
    down = bits[::-1]
    up_first = bits[1:] + bits[:1]

    up = gather_upstream(upstream)
    local = local_forward(hidden, rot_block, sizes)
    rotated = [mix_across(value, down) for value in local]
    gathered = [lax.all_gather(value, "dp", axis=0, tiled=False) for value in rotated]

    sums = []
    for start, count in zip(starts, sizes):
        full = unit_grads(up, weight, scales, start, count, per, parts)
        sums.append(
            lax.psum_scatter(full, "dp", scatter_dimension=0, tiled=False)
        )
    mixed = [mix_across(value, up_first) for value in sums]

    buffer = None
    scale_grads = []
    for value, start, count in zip(gathered, starts, sizes):
        buffer, scale_grad = weight_grads(
            value, up, weight, scales, clip_mask, buffer, start, count, per
        )
        scale_grads.append(scale_grad)
    grad_hidden = local_backward(mixed, rot_block, sizes)
    return (grad_hidden, buffer, jnp.concatenate(scale_grads, axis=0))


def solution(mesh):
    return jax.shard_map(
        shards,
        mesh=mesh,
        in_specs=(
            P("dp", "tensor"),
            P("dp", None),
            P("tensor", "dp"),
            P("tensor", "dp"),
            P("tensor", "dp"),
            P(),
        ),
        out_specs=(P("dp", "tensor"), P("tensor", "dp"), P("tensor", "dp")),
        check_vma=False,
    )
```

```python
import functools

import jax
import jax.numpy as jnp
from jax import lax
from jax.experimental import pallas as pl
from jax.experimental.pallas import tpu as pltpu
from jax.sharding import PartitionSpec as P

HB = 128
GROUP = 128
SUB = 16
F32 = jnp.float32
BF16 = jnp.bfloat16


def nt_dot(a, b):
    return lax.dot_general(a, b, (((1,), (1,)), ((), ())), preferred_element_type=F32)


def nn_dot(a, b):
    return lax.dot_general(a, b, (((1,), (0,)), ((), ())), preferred_element_type=F32)


def tn_dot(a, b):
    return lax.dot_general(a, b, (((0,), (0,)), ((), ())), preferred_element_type=F32)


def split2(value):
    high = value.astype(BF16)
    return high, (value - high.astype(F32)).astype(BF16)


def sign_matrix(size):
    both = lax.broadcasted_iota(jnp.int32, (size, size), 0) & lax.broadcasted_iota(
        jnp.int32, (size, size), 1
    )
    parity = jnp.zeros((size, size), jnp.int32)
    for bit in range(size.bit_length() - 1):
        parity = parity ^ ((both >> bit) & 1)
    return (1 - 2 * parity).astype(F32).astype(BF16)


def build_mixing(rot_ref, high_ref, low_ref, sign_ref, transposed):
    blocks = rot_ref.shape[0]
    size = blocks * SUB
    row = lax.broadcasted_iota(jnp.int32, (size, blocks), 0)
    col = lax.broadcasted_iota(jnp.int32, (size, blocks), 1)
    pick = ((row >> 4) == col).astype(F32).astype(BF16)
    rows = lax.broadcasted_iota(jnp.int32, (size, size), 0)
    cols = lax.broadcasted_iota(jnp.int32, (size, size), 1)
    same = (rows & (SUB - 1)) == (cols & (SUB - 1))
    for part, out_ref in zip(split2(rot_ref[...]), (high_ref, low_ref)):
        spread = nt_dot(pick, part) if transposed else nn_dot(pick, part)
        full = nt_dot(spread.astype(BF16), pick)
        out_ref[...] = jnp.where(same, full, 0.0).astype(BF16)
    sign_ref[...] = sign_matrix(HB)


def mix_rows(stacked, high_ref, low_ref, sign_ref):
    mixed = nn_dot(high_ref[...], stacked) + nn_dot(low_ref[...], stacked)
    results = []
    for part in range(stacked.shape[1] // HB):
        high, low = split2(mixed[:, part * HB : (part + 1) * HB])
        both = nn_dot(high, sign_ref[...]) + nn_dot(low, sign_ref[...])
        results.append((both * HB ** (-0.5)).astype(BF16))
    return results


def forward_kernel(sizes, x_ref, rot_ref, *refs):
    outs, (high_ref, low_ref, sign_ref) = refs[: len(sizes)], refs[len(sizes) :]
    blocks = rot_ref.shape[0]

    @pl.when(pl.program_id(0) == 0)
    def _():
        build_mixing(rot_ref, high_ref, low_ref, sign_ref, True)

    parts = x_ref.shape[0] // SUB
    stacked = jnp.concatenate(
        [
            jnp.concatenate(
                [
                    x_ref[j * SUB : (j + 1) * SUB, k * HB : (k + 1) * HB]
                    for k in range(blocks)
                ],
                axis=0,
            )
            for j in range(parts)
        ],
        axis=1,
    )
    for j, result in enumerate(mix_rows(stacked, high_ref, low_ref, sign_ref)):
        start = 0
        for size, out_ref in zip(sizes, outs):
            piece = result[start * SUB : (start + size) * SUB]
            out_ref[j] = piece.reshape(size, SUB, HB)
            start += size


def backward_kernel(sizes, *refs):
    ins, (rot_ref, out_ref, high_ref, low_ref, sign_ref) = refs[: len(sizes)], refs[len(sizes) :]
    blocks = rot_ref.shape[0]

    @pl.when(pl.program_id(0) == 0)
    def _():
        build_mixing(rot_ref, high_ref, low_ref, sign_ref, False)

    parts = out_ref.shape[0] // SUB
    stacked = jnp.concatenate(
        [
            jnp.concatenate(
                [in_ref[j].reshape(size * SUB, HB) for size, in_ref in zip(sizes, ins)], axis=0
            )
            for j in range(parts)
        ],
        axis=1,
    )
    for j, result in enumerate(mix_rows(stacked, high_ref, low_ref, sign_ref)):
        for k in range(blocks):
            out_ref[j * SUB : (j + 1) * SUB, k * HB : (k + 1) * HB] = result[
                k * SUB : (k + 1) * SUB
            ]


def local_scratch(blocks):
    return [
        pltpu.VMEM((blocks * SUB, blocks * SUB), BF16),
        pltpu.VMEM((blocks * SUB, blocks * SUB), BF16),
        pltpu.VMEM((HB, HB), BF16),
    ]


def local_cost(rows, blocks):
    size = blocks * SUB
    return pl.CostEstimate(
        flops=4 * size * size * (rows // SUB) * HB,
        bytes_accessed=4 * rows * blocks * HB,
        transcendentals=0,
    )


ANYWHERE = pl.BlockSpec(memory_space=pl.ANY)


def drop_inputs(kernel, start, count):
    def run(*refs):
        kernel(*refs[:start], *refs[start + count :])

    return run


def local_forward(hidden, rot_block, sizes):
    rows, width = hidden.shape
    blocks = width // HB
    parts = 2
    return pl.pallas_call(
        functools.partial(forward_kernel, sizes),
        grid=(rows // (SUB * parts),),
        in_specs=[
            pl.BlockSpec((SUB * parts, width), lambda i: (i, 0)),
            pl.BlockSpec((blocks, blocks), lambda i: (0, 0)),
        ],
        out_specs=[pl.BlockSpec((parts, size, SUB, HB), lambda i: (i, 0, 0, 0)) for size in sizes],
        out_shape=[jax.ShapeDtypeStruct((rows // SUB, size, SUB, HB), BF16) for size in sizes],
        scratch_shapes=local_scratch(blocks),
        compiler_params=pltpu.CompilerParams(vmem_limit_bytes=32 << 20),
        cost_estimate=local_cost(rows, blocks),
        name="local_forward",
    )(hidden, rot_block)


def local_backward(mixed, rot_block, sizes, after=()):
    count = mixed[0].shape[0]
    rows = count * SUB
    blocks = rot_block.shape[0]
    parts = 2
    return pl.pallas_call(
        drop_inputs(functools.partial(backward_kernel, sizes), len(sizes) + 1, len(after)),
        grid=(count // parts,),
        in_specs=[pl.BlockSpec((parts, size, SUB, HB), lambda i: (i, 0, 0, 0)) for size in sizes]
        + [pl.BlockSpec((blocks, blocks), lambda i: (0, 0))]
        + [ANYWHERE] * len(after),
        out_specs=pl.BlockSpec((parts * SUB, blocks * HB), lambda i: (i, 0)),
        out_shape=jax.ShapeDtypeStruct((rows, blocks * HB), BF16),
        scratch_shapes=local_scratch(blocks),
        compiler_params=pltpu.CompilerParams(vmem_limit_bytes=32 << 20),
        cost_estimate=local_cost(rows, blocks),
        name="local_backward",
    )(*mixed, rot_block, *after)


def units_kernel(first, per, up_ref, w_ref, s_ref, *refs):
    outs, quant_ref = refs[:-1], refs[-1]
    base = first + pl.program_id(0) * per
    for g in range(per):
        rows = slice(g * GROUP, (g + 1) * GROUP)
        quant_ref[rows, :] = (w_ref[rows, :].astype(F32) * s_ref[pl.ds(base + g, 1), :]).astype(
            BF16
        )
    result = nt_dot(up_ref[...], quant_ref[...]).astype(BF16)
    token = 0
    for out_ref in outs:
        for q in range(out_ref.shape[0]):
            for g in range(per):
                out_ref[q, g] = result[token : token + SUB, g * GROUP : (g + 1) * GROUP]
            token += SUB


def unit_grads(up, weight, scales, first, size, per, counts, after=()):
    tokens, cols = up.shape
    offset = first // per
    return pl.pallas_call(
        drop_inputs(functools.partial(units_kernel, first, per), 3, len(after)),
        grid=(size // per,),
        in_specs=[
            pl.BlockSpec((tokens, cols), lambda i: (0, 0)),
            pl.BlockSpec((per * GROUP, cols), lambda i: (offset + i, 0)),
            pl.BlockSpec(scales.shape, lambda i: (0, 0)),
        ]
        + [ANYWHERE] * len(after),
        out_specs=[pl.BlockSpec((count, per, SUB, HB), lambda i: (0, i, 0, 0)) for count in counts],
        out_shape=[jax.ShapeDtypeStruct((count, size, SUB, HB), BF16) for count in counts],
        scratch_shapes=[pltpu.VMEM((per * GROUP, cols), BF16)],
        compiler_params=pltpu.CompilerParams(vmem_limit_bytes=40 << 20),
        cost_estimate=pl.CostEstimate(
            flops=2 * tokens * cols * size * GROUP,
            bytes_accessed=2 * cols * size * GROUP + 2 * tokens * (cols + size * GROUP),
            transcendentals=0,
        ),
        name="unit_grads",
    )(up, weight, scales, *after)


def weights_kernel(first, per, pieces, *refs):
    rots = refs[:pieces]
    up_ref, w_ref, s_ref, m_ref = refs[pieces : pieces + 4]
    gw_ref, gs_ref = refs[-2:]
    step = pl.program_id(0)
    base = first + step * per
    left = jnp.concatenate(
        [
            jnp.concatenate(
                [rot_ref[q, g] for rot_ref in rots for q in range(rot_ref.shape[0])], axis=0
            )
            for g in range(per)
        ],
        axis=1,
    )
    cols = up_ref.shape[1]
    tile = min(512, cols)
    for e in range(cols // tile):
        span = slice(e * tile, (e + 1) * tile)
        grad = tn_dot(left, up_ref[:, span])
        for g in range(per):
            rows = slice(g * GROUP, (g + 1) * GROUP)
            piece = grad[rows]
            scale = s_ref[pl.ds(base + g, 1), span]
            kept = m_ref[pl.ds(base + g, 1), span].astype(F32) * scale
            gw_ref[rows, span] = (piece * kept).astype(BF16)
            gs_ref[pl.ds(step * per + g, 1), span] = jnp.sum(
                piece * w_ref[rows, span].astype(F32), axis=0, keepdims=True
            )


def weight_grads(rotated, up, weight, scales, mask, buffer, first, size, per, after=()):
    tokens, cols = up.shape
    offset = first // per
    specs = [
        pl.BlockSpec((piece.shape[0], per, SUB, HB), lambda i: (0, i, 0, 0)) for piece in rotated
    ] + [
        pl.BlockSpec((tokens, cols), lambda i: (0, 0)),
        pl.BlockSpec((per * GROUP, cols), lambda i: (offset + i, 0)),
        pl.BlockSpec(scales.shape, lambda i: (0, 0)),
        pl.BlockSpec(scales.shape, lambda i: (0, 0)),
    ]
    args = [*rotated, up, weight, scales, mask]
    aliases = {}
    if buffer is not None:
        aliases = {len(args): 0}
        args.append(buffer)
        specs.append(ANYWHERE)
    return pl.pallas_call(
        functools.partial(weights_kernel, first, per, len(rotated)),
        grid=(size // per,),
        in_specs=specs + [ANYWHERE] * len(after),
        out_specs=[
            pl.BlockSpec((per * GROUP, cols), lambda i: (offset + i, 0)),
            pl.BlockSpec((size, cols), lambda i: (0, 0)),
        ],
        out_shape=[
            jax.ShapeDtypeStruct(weight.shape, BF16),
            jax.ShapeDtypeStruct((size, cols), F32),
        ],
        input_output_aliases=aliases,
        compiler_params=pltpu.CompilerParams(vmem_limit_bytes=40 << 20),
        cost_estimate=pl.CostEstimate(
            flops=2 * tokens * cols * size * GROUP,
            bytes_accessed=4 * cols * size * GROUP + 2 * tokens * (cols + size * GROUP),
            transcendentals=0,
        ),
        name="weight_grads",
    )(*args, *after)


def small_call(kernel, name, ins, outs, steps, after=()):
    def spec(shape, dim):
        block = tuple(n // steps if d == dim else n for d, n in enumerate(shape))
        return pl.BlockSpec(
            block, lambda i: tuple(i if d == dim else 0 for d in range(len(shape)))
        )

    return pl.pallas_call(
        drop_inputs(kernel, len(ins), len(after)),
        grid=(steps,),
        in_specs=[spec(value.shape, 1) for value in ins] + [ANYWHERE] * len(after),
        out_specs=[spec(shape, 1) for shape in outs],
        out_shape=[jax.ShapeDtypeStruct(shape, BF16) for shape in outs],
        compiler_params=pltpu.CompilerParams(vmem_limit_bytes=32 << 20),
        cost_estimate=pl.CostEstimate(
            flops=0,
            bytes_accessed=2 * sum(v.size for v in ins) * 2,
            transcendentals=0,
        ),
        name=name,
    )(*ins, *after)


def transform_kernel(x_ref, out_ref):
    count = x_ref.shape[0]
    values = [x_ref[t].astype(F32) for t in range(count)]
    stride = 1
    while stride < count:
        for t in range(count):
            if not t & stride:
                a, b = values[t], values[t | stride]
                values[t], values[t | stride] = a + b, a - b
        stride *= 2
    for t in range(count):
        out_ref[t] = (values[t] * count ** (-0.5)).astype(BF16)


def transform(value, after=()):
    steps = 4 if value.shape[1] % 4 == 0 else 1
    return small_call(
        transform_kernel, "transform", [value], [value.shape], steps, after
    )[0]


def exchange(value):
    return lax.all_to_all(value, "tensor", split_axis=0, concat_axis=0, tiled=True)


def partner(value, axis, mask):
    size = lax.axis_size(axis)
    return lax.ppermute(value, axis, [(i, i ^ mask) for i in range(size)])


def mix_across(value):
    size = lax.axis_size("tensor")
    index = lax.axis_index("tensor")
    masks = [1 << i for i in range(size.bit_length() - 1)]
    for place, mask in enumerate(masks):
        other = partner(value, "tensor", mask).astype(F32)
        sign = jnp.where((index & mask) != 0, -1.0, 1.0).astype(F32)
        total = other + sign * value.astype(F32)
        if place == len(masks) - 1:
            total = total * size ** (-0.5)
        value = total.astype(BF16)
    return value


def gather_upstream(upstream):
    rows, width = upstream.shape
    parts = lax.axis_size("dp")
    cols = width // parts
    half = rows // 2
    index = lax.axis_index("dp")
    core = lax.axis_index("tensor") & 1
    own = lax.dynamic_slice(upstream, (0, index * cols), (rows, cols))
    mine = [
        partner(
            lax.dynamic_slice(upstream, (core * half, (index ^ m) * cols), (half, cols)), "dp", m
        )
        for m in range(1, parts)
    ]
    mine = jnp.stack(mine)
    other = partner(mine, "tensor", 1)
    low = jnp.where(core == 0, mine, other)
    high = jnp.where(core == 0, other, mine)
    far = jnp.concatenate([low, high], axis=1).reshape((parts - 1) * rows, cols)
    return jnp.concatenate([own, far], axis=0)


def relay_kernel(x_ref, y_ref, a_ref, b_ref, x_out, y_out):
    half = a_ref.shape[0]
    x_out[:half] = x_ref[:half]
    x_out[half:] = (x_ref[half:].astype(F32) + b_ref[...].astype(F32)).astype(BF16)
    y_out[:half] = (y_ref[:half].astype(F32) + a_ref[...].astype(F32)).astype(BF16)
    y_out[half:] = y_ref[half:]


def total_kernel(own_ref, x_ref, y_ref, out_ref):
    out_ref[...] = (
        own_ref[...].astype(F32) + x_ref[...].astype(F32) + y_ref[...].astype(F32)
    ).astype(BF16)


def general_shards(hidden, upstream, weight, scales, clip_mask, rot_block):
    groups = scales.shape[0]
    rows = hidden.shape[0]
    parts = lax.axis_size("dp")
    subs = rows // SUB
    index = lax.axis_index("dp")

    up = gather_upstream(upstream)
    (local,) = local_forward(hidden, rot_block, (groups,))
    rotated = lax.all_gather(mix_across(local), "dp", axis=0, tiled=False)
    order = index ^ jnp.arange(parts)
    rotated = rotated[order].reshape((parts * subs,) + local.shape[1:])
    per = 4 if groups % 4 == 0 else 1
    (full,) = unit_grads(up, weight, scales, 0, groups, per, (parts * subs,))
    full = full.reshape((parts,) + local.shape)[order]
    mixed = mix_across(lax.psum_scatter(full, "dp", scatter_dimension=0, tiled=False))
    grad_weight, grad_scales = weight_grads(
        [rotated], up, weight, scales, clip_mask, None, 0, groups, per
    )
    grad_hidden = local_backward([mixed], rot_block, (groups,))
    return grad_hidden, grad_weight, grad_scales


def shards(hidden, upstream, weight, scales, clip_mask, rot_block):
    groups = scales.shape[0]
    subs = hidden.shape[0] // SUB
    if lax.axis_size("dp") != 4 or lax.axis_size("tensor") != subs or groups % 8 != 4:
        return general_shards(hidden, upstream, weight, scales, clip_mask, rot_block)
    per = 4
    units = groups // per
    sizes = (per * (units - units // 2), per * (units // 2))
    starts = (0, sizes[0])
    half = subs // 2
    counts = (subs, subs, subs, half, half)

    def scatter_first(parts_of):
        return partner(parts_of[3], "dp", 1), partner(parts_of[4], "dp", 2)

    def scatter_second(parts_of, received, after):
        x_part, y_part = small_call(
            relay_kernel,
            "relay",
            [parts_of[1], parts_of[2], *received],
            [parts_of[1].shape] * 2,
            2,
            after,
        )
        return partner(x_part, "dp", 1), partner(y_part, "dp", 2)

    def scatter_last(parts_of, received, after):
        return small_call(
            total_kernel, "total", [parts_of[0], *received], [parts_of[0].shape], 2, after
        )[0]

    def gather(value):
        x_part, y_part = partner(value, "dp", 1), partner(value, "dp", 2)
        return value, x_part, y_part, partner(y_part[:half], "dp", 1), partner(
            x_part[half:], "dp", 2
        )

    up = gather_upstream(upstream)
    local = local_forward(hidden, rot_block, sizes)
    forth = [exchange(value) for value in local]
    unit0 = unit_grads(up, weight, scales, starts[0], sizes[0], per, counts, after=(local[0],))
    first0 = scatter_first(unit0)
    turned0 = transform(forth[0], after=(unit0[0],))
    rotated0 = exchange(turned0)
    unit1 = unit_grads(up, weight, scales, starts[1], sizes[1], per, counts, after=(turned0,))
    first1 = scatter_first(unit1)
    second0 = scatter_second(unit0, first0, after=(unit1[0],))
    turned1 = transform(forth[1], after=(unit1[0],))
    rotated1 = exchange(turned1)
    second1 = scatter_second(unit1, first1, after=(turned1,))
    sum0 = scatter_last(unit0, second0, after=(turned1,))
    back0 = exchange(sum0)
    sum1 = scatter_last(unit1, second1, after=(sum0,))
    back1 = exchange(sum1)
    gathered0 = gather(rotated0)
    gathered1 = gather(rotated1)
    mixed0 = transform(back0, after=(sum1,))
    final0 = exchange(mixed0)
    buffer, scale0 = weight_grads(
        gathered0, up, weight, scales, clip_mask, None, starts[0], sizes[0], per, after=(mixed0,)
    )
    mixed1 = transform(back1, after=(scale0,))
    final1 = exchange(mixed1)
    buffer, scale1 = weight_grads(
        gathered1, up, weight, scales, clip_mask, buffer, starts[1], sizes[1], per, after=(mixed1,)
    )
    grad_hidden = local_backward([final0, final1], rot_block, sizes, after=(scale1,))
    return grad_hidden, buffer, jnp.concatenate([scale0, scale1], axis=0)


def solution(mesh):
    return jax.shard_map(
        shards,
        mesh=mesh,
        in_specs=(
            P("dp", "tensor"),
            P("dp", None),
            P("tensor", "dp"),
            P("tensor", "dp"),
            P("tensor", "dp"),
            P(),
        ),
        out_specs=(P("dp", "tensor"), P("tensor", "dp"), P("tensor", "dp")),
        check_vma=False,
    )
```

```python
import functools

import jax
import jax.numpy as jnp
from jax import lax
from jax.experimental import pallas as pl
from jax.experimental.pallas import tpu as pltpu
from jax.sharding import PartitionSpec as P

HB = 128
GROUP = 128
SUB = 16
F32 = jnp.float32
BF16 = jnp.bfloat16


def nt_dot(a, b):
    return lax.dot_general(a, b, (((1,), (1,)), ((), ())), preferred_element_type=F32)


def nn_dot(a, b):
    return lax.dot_general(a, b, (((1,), (0,)), ((), ())), preferred_element_type=F32)


def tn_dot(a, b):
    return lax.dot_general(a, b, (((0,), (0,)), ((), ())), preferred_element_type=F32)


def split2(value):
    high = value.astype(BF16)
    return high, (value - high.astype(F32)).astype(BF16)


def sign_matrix(size):
    both = lax.broadcasted_iota(jnp.int32, (size, size), 0) & lax.broadcasted_iota(
        jnp.int32, (size, size), 1
    )
    parity = jnp.zeros((size, size), jnp.int32)
    for bit in range(size.bit_length() - 1):
        parity = parity ^ ((both >> bit) & 1)
    return (1 - 2 * parity).astype(F32).astype(BF16)


def build_mixing(rot_ref, high_ref, low_ref, sign_ref, transposed):
    blocks = rot_ref.shape[0]
    size = blocks * SUB
    row = lax.broadcasted_iota(jnp.int32, (size, blocks), 0)
    col = lax.broadcasted_iota(jnp.int32, (size, blocks), 1)
    pick = ((row >> 4) == col).astype(F32).astype(BF16)
    rows = lax.broadcasted_iota(jnp.int32, (size, size), 0)
    cols = lax.broadcasted_iota(jnp.int32, (size, size), 1)
    same = (rows & (SUB - 1)) == (cols & (SUB - 1))
    for part, out_ref in zip(split2(rot_ref[...]), (high_ref, low_ref)):
        spread = nt_dot(pick, part) if transposed else nn_dot(pick, part)
        full = nt_dot(spread.astype(BF16), pick)
        out_ref[...] = jnp.where(same, full, 0.0).astype(BF16)
    sign_ref[...] = sign_matrix(HB)


def mix_rows(stacked, high_ref, low_ref, sign_ref):
    mixed = nn_dot(high_ref[...], stacked) + nn_dot(low_ref[...], stacked)
    results = []
    for part in range(stacked.shape[1] // HB):
        high, low = split2(mixed[:, part * HB : (part + 1) * HB])
        both = nn_dot(high, sign_ref[...]) + nn_dot(low, sign_ref[...])
        results.append((both * HB ** (-0.5)).astype(BF16))
    return results


def forward_kernel(sizes, x_ref, rot_ref, *refs):
    outs, (high_ref, low_ref, sign_ref) = refs[: len(sizes)], refs[len(sizes) :]
    blocks = rot_ref.shape[0]

    @pl.when(pl.program_id(0) == 0)
    def _():
        build_mixing(rot_ref, high_ref, low_ref, sign_ref, True)

    parts = x_ref.shape[0] // SUB
    stacked = jnp.concatenate(
        [
            jnp.concatenate(
                [
                    x_ref[j * SUB : (j + 1) * SUB, k * HB : (k + 1) * HB]
                    for k in range(blocks)
                ],
                axis=0,
            )
            for j in range(parts)
        ],
        axis=1,
    )
    for j, result in enumerate(mix_rows(stacked, high_ref, low_ref, sign_ref)):
        start = 0
        for size, out_ref in zip(sizes, outs):
            piece = result[start * SUB : (start + size) * SUB]
            out_ref[j] = piece.reshape(size, SUB, HB)
            start += size


def backward_kernel(sizes, *refs):
    ins, (rot_ref, out_ref, high_ref, low_ref, sign_ref) = refs[: len(sizes)], refs[len(sizes) :]
    blocks = rot_ref.shape[0]

    @pl.when(pl.program_id(0) == 0)
    def _():
        build_mixing(rot_ref, high_ref, low_ref, sign_ref, False)

    parts = out_ref.shape[0] // SUB
    stacked = jnp.concatenate(
        [
            jnp.concatenate(
                [in_ref[j].reshape(size * SUB, HB) for size, in_ref in zip(sizes, ins)], axis=0
            )
            for j in range(parts)
        ],
        axis=1,
    )
    for j, result in enumerate(mix_rows(stacked, high_ref, low_ref, sign_ref)):
        for k in range(blocks):
            out_ref[j * SUB : (j + 1) * SUB, k * HB : (k + 1) * HB] = result[
                k * SUB : (k + 1) * SUB
            ]


def local_scratch(blocks):
    return [
        pltpu.VMEM((blocks * SUB, blocks * SUB), BF16),
        pltpu.VMEM((blocks * SUB, blocks * SUB), BF16),
        pltpu.VMEM((HB, HB), BF16),
    ]


FREE = pl.CostEstimate(flops=0, bytes_accessed=0, transcendentals=0)


def cost(size, cols):
    return pl.CostEstimate(
        flops=0, bytes_accessed=4 * size * GROUP * cols, transcendentals=0
    )
ANYWHERE = pl.BlockSpec(memory_space=pl.ANY)


def in_hbm(*values):
    return [pltpu.with_memory_space_constraint(value, pltpu.HBM) for value in values]


def drop_inputs(kernel, start, count):
    def run(*refs):
        kernel(*refs[:start], *refs[start + count :])

    return run


def local_forward(hidden, rot_block, sizes):
    rows, width = hidden.shape
    blocks = width // HB
    parts = 2
    return pl.pallas_call(
        functools.partial(forward_kernel, sizes),
        grid=(rows // (SUB * parts),),
        in_specs=[
            pl.BlockSpec((SUB * parts, width), lambda i: (i, 0)),
            pl.BlockSpec((blocks, blocks), lambda i: (0, 0)),
        ],
        out_specs=[pl.BlockSpec((parts, size, SUB, HB), lambda i: (i, 0, 0, 0)) for size in sizes],
        out_shape=[jax.ShapeDtypeStruct((rows // SUB, size, SUB, HB), BF16) for size in sizes],
        scratch_shapes=local_scratch(blocks),
        compiler_params=pltpu.CompilerParams(vmem_limit_bytes=16 << 20),
        cost_estimate=FREE,
        name="local_forward",
    )(*in_hbm(hidden), rot_block)


def local_backward(mixed, rot_block, sizes, after=()):
    count = mixed[0].shape[0]
    rows = count * SUB
    blocks = rot_block.shape[0]
    parts = 2
    return pl.pallas_call(
        drop_inputs(functools.partial(backward_kernel, sizes), len(sizes) + 1, len(after)),
        grid=(count // parts,),
        in_specs=[pl.BlockSpec((parts, size, SUB, HB), lambda i: (i, 0, 0, 0)) for size in sizes]
        + [pl.BlockSpec((blocks, blocks), lambda i: (0, 0))]
        + [ANYWHERE] * len(after),
        out_specs=pl.BlockSpec((parts * SUB, blocks * HB), lambda i: (i, 0)),
        out_shape=pltpu.HBM((rows, blocks * HB), BF16),
        scratch_shapes=local_scratch(blocks),
        compiler_params=pltpu.CompilerParams(vmem_limit_bytes=16 << 20),
        cost_estimate=FREE,
        name="local_backward",
    )(*mixed, rot_block, *after)


def units_kernel(first, per, up_ref, w_ref, s_ref, *refs):
    outs, quant_ref = refs[:-1], refs[-1]
    base = first + pl.program_id(0) * per
    for g in range(per):
        rows = slice(g * GROUP, (g + 1) * GROUP)
        quant_ref[rows, :] = (w_ref[rows, :].astype(F32) * s_ref[pl.ds(base + g, 1), :]).astype(
            BF16
        )
    result = nt_dot(up_ref[...], quant_ref[...]).astype(BF16)
    token = 0
    for out_ref in outs:
        for q in range(out_ref.shape[0]):
            for g in range(per):
                out_ref[q, g] = result[token : token + SUB, g * GROUP : (g + 1) * GROUP]
            token += SUB


def unit_grads(up, weight, scales, first, size, per, counts, after=()):
    tokens, cols = up.shape
    offset = first // per
    return pl.pallas_call(
        drop_inputs(functools.partial(units_kernel, first, per), 3, len(after)),
        grid=(size // per,),
        in_specs=[
            pl.BlockSpec((tokens, cols), lambda i: (0, 0)),
            pl.BlockSpec((per * GROUP, cols), lambda i: (offset + i, 0)),
            pl.BlockSpec(scales.shape, lambda i: (0, 0)),
        ]
        + [ANYWHERE] * len(after),
        out_specs=[pl.BlockSpec((count, per, SUB, HB), lambda i: (0, i, 0, 0)) for count in counts],
        out_shape=[jax.ShapeDtypeStruct((count, size, SUB, HB), BF16) for count in counts],
        scratch_shapes=[pltpu.VMEM((per * GROUP, cols), BF16)],
        compiler_params=pltpu.CompilerParams(vmem_limit_bytes=26 << 20),
        cost_estimate=FREE,
        name="unit_grads",
    )(up, *in_hbm(weight, scales), *after)


def weights_kernel(first, per, pieces, *refs):
    rots = refs[:pieces]
    up_ref, w_ref, s_ref, m_ref = refs[pieces : pieces + 4]
    gw_ref, gs_ref = refs[-2:]
    step = pl.program_id(0)
    base = first + step * per
    left = jnp.concatenate(
        [
            jnp.concatenate(
                [rot_ref[q, g] for rot_ref in rots for q in range(rot_ref.shape[0])], axis=0
            )
            for g in range(per)
        ],
        axis=1,
    )
    cols = up_ref.shape[1]
    tile = min(512, cols)
    for e in range(cols // tile):
        span = slice(e * tile, (e + 1) * tile)
        grad = tn_dot(left, up_ref[:, span])
        for g in range(per):
            rows = slice(g * GROUP, (g + 1) * GROUP)
            piece = grad[rows]
            scale = s_ref[pl.ds(base + g, 1), span]
            kept = m_ref[pl.ds(base + g, 1), span].astype(F32) * scale
            gw_ref[rows, span] = (piece * kept).astype(BF16)
            gs_ref[pl.ds(step * per + g, 1), span] = jnp.sum(
                piece * w_ref[rows, span].astype(F32), axis=0, keepdims=True
            )


def weight_grads(rotated, up, weight, scales, mask, buffer, first, size, per, after=()):
    tokens, cols = up.shape
    offset = first // per
    specs = [
        pl.BlockSpec((piece.shape[0], per, SUB, HB), lambda i: (0, offset + i, 0, 0))
        for piece in rotated
    ] + [
        pl.BlockSpec((tokens, cols), lambda i: (0, 0)),
        pl.BlockSpec((per * GROUP, cols), lambda i: (offset + i, 0)),
        pl.BlockSpec(scales.shape, lambda i: (0, 0)),
        pl.BlockSpec(scales.shape, lambda i: (0, 0)),
    ]
    args = [*rotated, up, *in_hbm(weight, scales, mask)]
    aliases = {}
    if buffer is not None:
        aliases = {len(args): 0}
        args.append(buffer)
        specs.append(ANYWHERE)
    return pl.pallas_call(
        functools.partial(weights_kernel, first, per, len(rotated)),
        grid=(size // per,),
        in_specs=specs + [ANYWHERE] * len(after),
        out_specs=[
            pl.BlockSpec((per * GROUP, cols), lambda i: (offset + i, 0)),
            pl.BlockSpec((size, cols), lambda i: (0, 0)),
        ],
        out_shape=[
            pltpu.HBM(weight.shape, BF16),
            jax.ShapeDtypeStruct((size, cols), F32),
        ],
        input_output_aliases=aliases,
        compiler_params=pltpu.CompilerParams(vmem_limit_bytes=26 << 20),
        cost_estimate=FREE,
        name="weight_grads",
    )(*args, *after)


def small_call(kernel, name, ins, outs, steps, after=()):
    def spec(shape, dim):
        block = tuple(n // steps if d == dim else n for d, n in enumerate(shape))
        return pl.BlockSpec(
            block, lambda i: tuple(i if d == dim else 0 for d in range(len(shape)))
        )

    return pl.pallas_call(
        drop_inputs(kernel, len(ins), len(after)),
        grid=(steps,),
        in_specs=[spec(value.shape, 1) for value in ins] + [ANYWHERE] * len(after),
        out_specs=[spec(shape, 1) for shape in outs],
        out_shape=[jax.ShapeDtypeStruct(shape, BF16) for shape in outs],
        compiler_params=pltpu.CompilerParams(vmem_limit_bytes=16 << 20),
        cost_estimate=FREE,
        name=name,
    )(*ins, *after)


def transform_kernel(x_ref, out_ref):
    count = x_ref.shape[0]
    values = [x_ref[t].astype(F32) for t in range(count)]
    stride = 1
    while stride < count:
        for t in range(count):
            if not t & stride:
                a, b = values[t], values[t | stride]
                values[t], values[t | stride] = a + b, a - b
        stride *= 2
    for t in range(count):
        out_ref[t] = (values[t] * count ** (-0.5)).astype(BF16)


def transform(value, after=()):
    steps = 4 if value.shape[1] % 4 == 0 else 1
    return small_call(
        transform_kernel, "transform", [value], [value.shape], steps, after
    )[0]


def exchange(value):
    return lax.all_to_all(value, "tensor", split_axis=0, concat_axis=0, tiled=True)


def partner(value, axis, mask):
    size = lax.axis_size(axis)
    return lax.ppermute(value, axis, [(i, i ^ mask) for i in range(size)])


def mix_across(value):
    size = lax.axis_size("tensor")
    index = lax.axis_index("tensor")
    masks = [1 << i for i in range(size.bit_length() - 1)]
    for place, mask in enumerate(masks):
        other = partner(value, "tensor", mask).astype(F32)
        sign = jnp.where((index & mask) != 0, -1.0, 1.0).astype(F32)
        total = other + sign * value.astype(F32)
        if place == len(masks) - 1:
            total = total * size ** (-0.5)
        value = total.astype(BF16)
    return value


def gather_upstream(upstream):
    rows, width = upstream.shape
    parts = lax.axis_size("dp")
    cols = width // parts
    half = rows // 2
    index = lax.axis_index("dp")
    core = lax.axis_index("tensor") & 1
    own = lax.dynamic_slice(upstream, (0, index * cols), (rows, cols))
    mine = [
        partner(
            lax.dynamic_slice(upstream, (core * half, (index ^ m) * cols), (half, cols)), "dp", m
        )
        for m in range(1, parts)
    ]
    mine = jnp.stack(mine)
    other = partner(mine, "tensor", 1)
    low = jnp.where(core == 0, mine, other)
    high = jnp.where(core == 0, other, mine)
    far = jnp.concatenate([low, high], axis=1).reshape((parts - 1) * rows, cols)
    return jnp.concatenate([own, far], axis=0)


def relay_kernel(x_ref, y_ref, a_ref, b_ref, x_out, y_out):
    half = a_ref.shape[0]
    x_out[:half] = x_ref[:half]
    x_out[half:] = (x_ref[half:].astype(F32) + b_ref[...].astype(F32)).astype(BF16)
    y_out[:half] = (y_ref[:half].astype(F32) + a_ref[...].astype(F32)).astype(BF16)
    y_out[half:] = y_ref[half:]


def total_kernel(own_ref, x_ref, y_ref, *refs):
    refs[-1][...] = (
        own_ref[...].astype(F32) + x_ref[...].astype(F32) + y_ref[...].astype(F32)
    ).astype(BF16)


def total(ins, buffer, first, groups, per, after=()):
    count, size = ins[0].shape[:2]
    offset = first // per
    args = list(ins)
    specs = [pl.BlockSpec((count, per, SUB, HB), lambda i: (0, i, 0, 0))] * 3
    aliases = {}
    if buffer is not None:
        aliases = {3: 0}
        args.append(buffer)
        specs.append(ANYWHERE)
    return pl.pallas_call(
        total_kernel,
        grid=(size // per,),
        in_specs=specs + [ANYWHERE] * len(after),
        out_specs=pl.BlockSpec((count, per, SUB, HB), lambda i: (0, offset + i, 0, 0)),
        out_shape=jax.ShapeDtypeStruct((count, groups, SUB, HB), BF16),
        input_output_aliases=aliases,
        compiler_params=pltpu.CompilerParams(vmem_limit_bytes=16 << 20),
        cost_estimate=FREE,
        name="total",
    )(*args, *after)


def general_shards(hidden, upstream, weight, scales, clip_mask, rot_block):
    groups = scales.shape[0]
    rows = hidden.shape[0]
    parts = lax.axis_size("dp")
    subs = rows // SUB
    index = lax.axis_index("dp")

    up = gather_upstream(upstream)
    (local,) = local_forward(hidden, rot_block, (groups,))
    rotated = lax.all_gather(mix_across(local), "dp", axis=0, tiled=False)
    order = index ^ jnp.arange(parts)
    rotated = rotated[order].reshape((parts * subs,) + local.shape[1:])
    per = 4 if groups % 4 == 0 else 1
    (full,) = unit_grads(up, weight, scales, 0, groups, per, (parts * subs,))
    full = full.reshape((parts,) + local.shape)[order]
    mixed = mix_across(lax.psum_scatter(full, "dp", scatter_dimension=0, tiled=False))
    grad_weight, grad_scales = weight_grads(
        [rotated], up, weight, scales, clip_mask, None, 0, groups, per
    )
    grad_hidden = local_backward([mixed], rot_block, (groups,))
    return grad_hidden, grad_weight, grad_scales


def shards(hidden, upstream, weight, scales, clip_mask, rot_block):
    groups = scales.shape[0]
    subs = hidden.shape[0] // SUB
    if lax.axis_size("dp") != 4 or lax.axis_size("tensor") != subs or groups % 8 != 4:
        return general_shards(hidden, upstream, weight, scales, clip_mask, rot_block)
    per = 4
    units = groups // per
    sizes = (per * (units - units // 2), per * (units // 2))
    starts = (0, sizes[0])
    half = subs // 2
    counts = (subs, subs, subs, half, half)

    def scatter_first(parts_of):
        return partner(parts_of[3], "dp", 1), partner(parts_of[4], "dp", 2)

    def scatter_second(parts_of, received, after):
        x_part, y_part = small_call(
            relay_kernel,
            "relay",
            [parts_of[1], parts_of[2], *received],
            [parts_of[1].shape] * 2,
            2,
            after,
        )
        return x_part, partner(x_part, "dp", 1), partner(y_part, "dp", 2)

    def gather(value):
        x_part, y_part = partner(value, "dp", 1), partner(value, "dp", 2)
        return value, x_part, y_part, partner(y_part[:half], "dp", 1), partner(
            x_part[half:], "dp", 2
        )

    up = gather_upstream(upstream)
    (local,) = local_forward(hidden, rot_block, (groups,))
    forth = exchange(local)
    unit0 = unit_grads(up, weight, scales, starts[0], sizes[0], per, counts, after=(local,))
    first0 = scatter_first(unit0)
    unit1 = unit_grads(up, weight, scales, starts[1], sizes[1], per, counts, after=(unit0[0],))
    first1 = scatter_first(unit1)
    relayed0, *second0 = scatter_second(unit0, first0, after=(unit1[0],))
    turned = transform(forth, after=(relayed0,))
    rotated = exchange(turned)
    relayed1, *second1 = scatter_second(unit1, first1, after=(turned,))
    summed = total((unit0[0], *second0), None, starts[0], groups, per, after=(turned,))
    summed = total((unit1[0], *second1), summed, starts[1], groups, per, after=(rotated,))
    back = exchange(summed)
    gathered = gather(rotated)
    mixed = transform(back, after=gathered[1:3])
    final = exchange(mixed)
    buffer, scale0 = weight_grads(
        gathered, up, weight, scales, clip_mask, None, starts[0], sizes[0], per, after=(mixed,)
    )
    buffer, scale1 = weight_grads(
        gathered, up, weight, scales, clip_mask, buffer, starts[1], sizes[1], per
    )
    grad_hidden = local_backward([final], rot_block, (groups,), after=(scale1,))
    return grad_hidden, buffer, jnp.concatenate([scale0, scale1], axis=0)


def solution(mesh):
    return jax.shard_map(
        shards,
        mesh=mesh,
        in_specs=(
            P("dp", "tensor"),
            P("dp", None),
            P("tensor", "dp"),
            P("tensor", "dp"),
            P("tensor", "dp"),
            P(),
        ),
        out_specs=(P("dp", "tensor"), P("tensor", "dp"), P("tensor", "dp")),
        check_vma=False,
    )
```

```python
import functools

import jax
import jax.numpy as jnp
from jax import lax
from jax.experimental import pallas as pl
from jax.experimental.pallas import tpu as pltpu
from jax.sharding import PartitionSpec as P

HB = 128
GROUP = 128
SUB = 16
ROWS = 8
F32 = jnp.float32
BF16 = jnp.bfloat16


def nt_dot(a, b):
    return lax.dot_general(a, b, (((1,), (1,)), ((), ())), preferred_element_type=F32)


def nn_dot(a, b):
    return lax.dot_general(a, b, (((1,), (0,)), ((), ())), preferred_element_type=F32)


def tn_dot(a, b):
    return lax.dot_general(a, b, (((0,), (0,)), ((), ())), preferred_element_type=F32)


def split2(value):
    high = value.astype(BF16)
    return high, (value - high.astype(F32)).astype(BF16)


def sign_matrix(size):
    both = lax.broadcasted_iota(jnp.int32, (size, size), 0) & lax.broadcasted_iota(
        jnp.int32, (size, size), 1
    )
    parity = jnp.zeros((size, size), jnp.int32)
    for bit in range(size.bit_length() - 1):
        parity = parity ^ ((both >> bit) & 1)
    return (1 - 2 * parity).astype(F32).astype(BF16)


def build_mixing(rot_ref, high_ref, low_ref, sign_ref, transposed):
    blocks = rot_ref.shape[0]
    size = blocks * ROWS
    row = lax.broadcasted_iota(jnp.int32, (size, blocks), 0)
    col = lax.broadcasted_iota(jnp.int32, (size, blocks), 1)
    pick = ((row >> 3) == col).astype(F32).astype(BF16)
    rows = lax.broadcasted_iota(jnp.int32, (size, size), 0)
    cols = lax.broadcasted_iota(jnp.int32, (size, size), 1)
    same = (rows & (ROWS - 1)) == (cols & (ROWS - 1))
    for part, out_ref in zip(split2(rot_ref[...]), (high_ref, low_ref)):
        spread = nt_dot(pick, part) if transposed else nn_dot(pick, part)
        full = nt_dot(spread.astype(BF16), pick)
        out_ref[...] = jnp.where(same, full, 0.0).astype(BF16)
    sign_ref[...] = sign_matrix(HB)


def mix_rows(tiles, high_ref, low_ref, sign_ref):
    blocks = len(tiles[0])
    stacked = jnp.concatenate([jnp.concatenate(one, axis=0).astype(BF16) for one in tiles], axis=1)
    mixed = nn_dot(high_ref[...], stacked) + nn_dot(low_ref[...], stacked)
    results = []
    for j in range(len(tiles)):
        part = nn_dot(mixed[:, j * HB : (j + 1) * HB].astype(BF16), sign_ref[...])
        results.append((part * HB ** (-0.5)).reshape(blocks, ROWS, HB))
    return results


def forward_kernel(sizes, x_ref, rot_ref, *refs):
    outs, (high_ref, low_ref, sign_ref) = refs[: len(sizes)], refs[len(sizes) :]
    blocks = rot_ref.shape[0]

    @pl.when(pl.program_id(0) == 0)
    def _():
        build_mixing(rot_ref, high_ref, low_ref, sign_ref, True)

    rows = x_ref.shape[0]
    wide = [x_ref[:, k * HB : (k + 1) * HB].astype(F32) for k in range(blocks)]
    tiles = [[one[j : j + ROWS] for one in wide] for j in range(0, rows, ROWS)]
    results = mix_rows(tiles, high_ref, low_ref, sign_ref)
    for j in range(rows // SUB):
        both = jnp.concatenate([results[2 * j], results[2 * j + 1]], axis=1).astype(BF16)
        start = 0
        for size, out_ref in zip(sizes, outs):
            out_ref[j] = both[start : start + size]
            start += size


def backward_kernel(sizes, *refs):
    ins, (rot_ref, out_ref, high_ref, low_ref, sign_ref) = refs[: len(sizes)], refs[len(sizes) :]
    blocks = rot_ref.shape[0]

    @pl.when(pl.program_id(0) == 0)
    def _():
        build_mixing(rot_ref, high_ref, low_ref, sign_ref, False)

    rows = out_ref.shape[0]
    tiles = []
    for j in range(rows // SUB):
        wide = [
            in_ref[j, c].astype(F32) for size, in_ref in zip(sizes, ins) for c in range(size)
        ]
        tiles += [[one[:ROWS] for one in wide], [one[ROWS:] for one in wide]]
    results = mix_rows(tiles, high_ref, low_ref, sign_ref)
    for j in range(rows // SUB):
        both = jnp.concatenate([results[2 * j], results[2 * j + 1]], axis=1).astype(BF16)
        for k in range(blocks):
            out_ref[j * SUB : (j + 1) * SUB, k * HB : (k + 1) * HB] = both[k]


def local_scratch(blocks):
    return [
        pltpu.VMEM((blocks * ROWS, blocks * ROWS), BF16),
        pltpu.VMEM((blocks * ROWS, blocks * ROWS), BF16),
        pltpu.VMEM((HB, HB), BF16),
    ]


FREE = pl.CostEstimate(flops=0, bytes_accessed=0, transcendentals=0)


def cost(size, cols):
    return pl.CostEstimate(
        flops=0, bytes_accessed=4 * size * GROUP * cols, transcendentals=0
    )
ANYWHERE = pl.BlockSpec(memory_space=pl.ANY)


def in_hbm(*values):
    return [pltpu.with_memory_space_constraint(value, pltpu.HBM) for value in values]


def drop_inputs(kernel, start, count):
    def run(*refs):
        kernel(*refs[:start], *refs[start + count :])

    return run


def local_forward(hidden, rot_block, sizes):
    rows, width = hidden.shape
    blocks = width // HB
    parts = 2
    return pl.pallas_call(
        functools.partial(forward_kernel, sizes),
        grid=(rows // (SUB * parts),),
        in_specs=[
            pl.BlockSpec((SUB * parts, width), lambda i: (i, 0)),
            pl.BlockSpec((blocks, blocks), lambda i: (0, 0)),
        ],
        out_specs=[pl.BlockSpec((parts, size, SUB, HB), lambda i: (i, 0, 0, 0)) for size in sizes],
        out_shape=[jax.ShapeDtypeStruct((rows // SUB, size, SUB, HB), BF16) for size in sizes],
        scratch_shapes=local_scratch(blocks),
        compiler_params=pltpu.CompilerParams(vmem_limit_bytes=60 << 20),
        cost_estimate=FREE,
        name="local_forward",
    )(*in_hbm(hidden), rot_block)


def local_backward(mixed, rot_block, sizes, after=()):
    count = mixed[0].shape[0]
    rows = count * SUB
    blocks = rot_block.shape[0]
    parts = 2
    return pl.pallas_call(
        drop_inputs(functools.partial(backward_kernel, sizes), len(sizes) + 1, len(after)),
        grid=(count // parts,),
        in_specs=[pl.BlockSpec((parts, size, SUB, HB), lambda i: (i, 0, 0, 0)) for size in sizes]
        + [pl.BlockSpec((blocks, blocks), lambda i: (0, 0))]
        + [ANYWHERE] * len(after),
        out_specs=pl.BlockSpec((parts * SUB, blocks * HB), lambda i: (i, 0)),
        out_shape=pltpu.HBM((rows, blocks * HB), BF16),
        scratch_shapes=local_scratch(blocks),
        compiler_params=pltpu.CompilerParams(vmem_limit_bytes=60 << 20),
        cost_estimate=FREE,
        name="local_backward",
    )(*mixed, rot_block, *after)


def units_kernel(first, per, up_ref, w_ref, s_ref, *refs):
    outs, quant_ref = refs[:-1], refs[-1]
    base = first + pl.program_id(0) * per
    for g in range(per):
        rows = slice(g * GROUP, (g + 1) * GROUP)
        quant_ref[rows, :] = (w_ref[rows, :].astype(F32) * s_ref[pl.ds(base + g, 1), :]).astype(
            BF16
        )
    result = nt_dot(up_ref[...], quant_ref[...]).astype(BF16)
    token = 0
    for out_ref in outs:
        for q in range(out_ref.shape[0]):
            for g in range(per):
                out_ref[q, g] = result[token : token + SUB, g * GROUP : (g + 1) * GROUP]
            token += SUB


def unit_grads(up, weight, scales, first, size, per, counts, after=()):
    tokens, cols = up.shape
    offset = first // per
    return pl.pallas_call(
        drop_inputs(functools.partial(units_kernel, first, per), 3, len(after)),
        grid=(size // per,),
        in_specs=[
            pl.BlockSpec((tokens, cols), lambda i: (0, 0)),
            pl.BlockSpec((per * GROUP, cols), lambda i: (offset + i, 0)),
            pl.BlockSpec(scales.shape, lambda i: (0, 0)),
        ]
        + [ANYWHERE] * len(after),
        out_specs=[pl.BlockSpec((count, per, SUB, HB), lambda i: (0, i, 0, 0)) for count in counts],
        out_shape=[jax.ShapeDtypeStruct((count, size, SUB, HB), BF16) for count in counts],
        scratch_shapes=[pltpu.VMEM((per * GROUP, cols), BF16)],
        compiler_params=pltpu.CompilerParams(vmem_limit_bytes=26 << 20),
        cost_estimate=FREE,
        name="unit_grads",
    )(up, *in_hbm(weight, scales), *after)


def weights_kernel(first, per, pieces, *refs):
    rots = refs[:pieces]
    up_ref, w_ref, s_ref, m_ref = refs[pieces : pieces + 4]
    gw_ref, gs_ref = refs[-2:]
    step = pl.program_id(0)
    base = first + step * per
    left = jnp.concatenate(
        [
            jnp.concatenate(
                [rot_ref[q, g] for rot_ref in rots for q in range(rot_ref.shape[0])], axis=0
            )
            for g in range(per)
        ],
        axis=1,
    )
    cols = up_ref.shape[1]
    tile = min(512, cols)
    for e in range(cols // tile):
        span = slice(e * tile, (e + 1) * tile)
        grad = tn_dot(left, up_ref[:, span])
        for g in range(per):
            rows = slice(g * GROUP, (g + 1) * GROUP)
            piece = grad[rows]
            scale = s_ref[pl.ds(base + g, 1), span]
            kept = m_ref[pl.ds(base + g, 1), span].astype(F32) * scale
            gw_ref[rows, span] = (piece * kept).astype(BF16)
            gs_ref[pl.ds(step * per + g, 1), span] = jnp.sum(
                piece * w_ref[rows, span].astype(F32), axis=0, keepdims=True
            )


def weight_grads(rotated, up, weight, scales, mask, buffer, first, size, per, after=()):
    tokens, cols = up.shape
    offset = first // per
    specs = [
        pl.BlockSpec((piece.shape[0], per, SUB, HB), lambda i: (0, offset + i, 0, 0))
        for piece in rotated
    ] + [
        pl.BlockSpec((tokens, cols), lambda i: (0, 0)),
        pl.BlockSpec((per * GROUP, cols), lambda i: (offset + i, 0)),
        pl.BlockSpec(scales.shape, lambda i: (0, 0)),
        pl.BlockSpec(scales.shape, lambda i: (0, 0)),
    ]
    args = [*rotated, up, *in_hbm(weight, scales, mask)]
    aliases = {}
    if buffer is not None:
        aliases = {len(args): 0}
        args.append(buffer)
        specs.append(ANYWHERE)
    return pl.pallas_call(
        functools.partial(weights_kernel, first, per, len(rotated)),
        grid=(size // per,),
        in_specs=specs + [ANYWHERE] * len(after),
        out_specs=[
            pl.BlockSpec((per * GROUP, cols), lambda i: (offset + i, 0)),
            pl.BlockSpec((size, cols), lambda i: (0, 0)),
        ],
        out_shape=[
            pltpu.HBM(weight.shape, BF16),
            jax.ShapeDtypeStruct((size, cols), F32),
        ],
        input_output_aliases=aliases,
        compiler_params=pltpu.CompilerParams(vmem_limit_bytes=26 << 20),
        cost_estimate=FREE,
        name="weight_grads",
    )(*args, *after)


def small_call(kernel, name, ins, outs, steps, after=()):
    def spec(shape, dim):
        block = tuple(n // steps if d == dim else n for d, n in enumerate(shape))
        return pl.BlockSpec(
            block, lambda i: tuple(i if d == dim else 0 for d in range(len(shape)))
        )

    return pl.pallas_call(
        drop_inputs(kernel, len(ins), len(after)),
        grid=(steps,),
        in_specs=[spec(value.shape, 1) for value in ins] + [ANYWHERE] * len(after),
        out_specs=[spec(shape, 1) for shape in outs],
        out_shape=[jax.ShapeDtypeStruct(shape, BF16) for shape in outs],
        compiler_params=pltpu.CompilerParams(vmem_limit_bytes=60 << 20),
        cost_estimate=FREE,
        name=name,
    )(*ins, *after)


def transform_kernel(x_ref, out_ref):
    count = x_ref.shape[0]
    values = [x_ref[t].astype(F32) for t in range(count)]
    stride = 1
    while stride < count:
        for t in range(count):
            if not t & stride:
                a, b = values[t], values[t | stride]
                values[t], values[t | stride] = a + b, a - b
        stride *= 2
    for t in range(count):
        out_ref[t] = (values[t] * count ** (-0.5)).astype(BF16)


def transform(value, after=()):
    steps = 4 if value.shape[1] % 4 == 0 else 1
    return small_call(
        transform_kernel, "transform", [value], [value.shape], steps, after
    )[0]


def exchange(value):
    return lax.all_to_all(value, "tensor", split_axis=0, concat_axis=0, tiled=True)


def partner(value, axis, mask):
    size = lax.axis_size(axis)
    return lax.ppermute(value, axis, [(i, i ^ mask) for i in range(size)])


def mix_across(value):
    size = lax.axis_size("tensor")
    index = lax.axis_index("tensor")
    masks = [1 << i for i in range(size.bit_length() - 1)]
    for place, mask in enumerate(masks):
        other = partner(value, "tensor", mask).astype(F32)
        sign = jnp.where((index & mask) != 0, -1.0, 1.0).astype(F32)
        total = other + sign * value.astype(F32)
        if place == len(masks) - 1:
            total = total * size ** (-0.5)
        value = total.astype(BF16)
    return value


def gather_upstream(upstream):
    rows, width = upstream.shape
    parts = lax.axis_size("dp")
    cols = width // parts
    half = rows // 2
    index = lax.axis_index("dp")
    core = lax.axis_index("tensor") & 1
    own = lax.dynamic_slice(upstream, (0, index * cols), (rows, cols))
    mine = [
        partner(
            lax.dynamic_slice(upstream, (core * half, (index ^ m) * cols), (half, cols)), "dp", m
        )
        for m in range(1, parts)
    ]
    mine = jnp.stack(mine)
    other = partner(mine, "tensor", 1)
    low = jnp.where(core == 0, mine, other)
    high = jnp.where(core == 0, other, mine)
    far = jnp.concatenate([low, high], axis=1).reshape((parts - 1) * rows, cols)
    return jnp.concatenate([own, far], axis=0)


def relay_kernel(x_ref, y_ref, a_ref, b_ref, x_out, y_out):
    half = a_ref.shape[0]
    x_out[:half] = x_ref[:half]
    x_out[half:] = (x_ref[half:].astype(F32) + b_ref[...].astype(F32)).astype(BF16)
    y_out[:half] = (y_ref[:half].astype(F32) + a_ref[...].astype(F32)).astype(BF16)
    y_out[half:] = y_ref[half:]


def total_kernel(own_ref, x_ref, y_ref, *refs):
    refs[-1][...] = (
        own_ref[...].astype(F32) + x_ref[...].astype(F32) + y_ref[...].astype(F32)
    ).astype(BF16)


def total(ins, buffer, first, groups, per, after=()):
    count, size = ins[0].shape[:2]
    offset = first // per
    args = list(ins)
    specs = [pl.BlockSpec((count, per, SUB, HB), lambda i: (0, i, 0, 0))] * 3
    aliases = {}
    if buffer is not None:
        aliases = {3: 0}
        args.append(buffer)
        specs.append(ANYWHERE)
    return pl.pallas_call(
        total_kernel,
        grid=(size // per,),
        in_specs=specs + [ANYWHERE] * len(after),
        out_specs=pl.BlockSpec((count, per, SUB, HB), lambda i: (0, offset + i, 0, 0)),
        out_shape=jax.ShapeDtypeStruct((count, groups, SUB, HB), BF16),
        input_output_aliases=aliases,
        compiler_params=pltpu.CompilerParams(vmem_limit_bytes=60 << 20),
        cost_estimate=FREE,
        name="total",
    )(*args, *after)


def general_shards(hidden, upstream, weight, scales, clip_mask, rot_block):
    groups = scales.shape[0]
    rows = hidden.shape[0]
    parts = lax.axis_size("dp")
    subs = rows // SUB
    index = lax.axis_index("dp")

    up = gather_upstream(upstream)
    (local,) = local_forward(hidden, rot_block, (groups,))
    rotated = lax.all_gather(mix_across(local), "dp", axis=0, tiled=False)
    order = index ^ jnp.arange(parts)
    rotated = rotated[order].reshape((parts * subs,) + local.shape[1:])
    per = 4 if groups % 4 == 0 else 1
    (full,) = unit_grads(up, weight, scales, 0, groups, per, (parts * subs,))
    full = full.reshape((parts,) + local.shape)[order]
    mixed = mix_across(lax.psum_scatter(full, "dp", scatter_dimension=0, tiled=False))
    grad_weight, grad_scales = weight_grads(
        [rotated], up, weight, scales, clip_mask, None, 0, groups, per
    )
    grad_hidden = local_backward([mixed], rot_block, (groups,))
    return grad_hidden, grad_weight, grad_scales


def shards(hidden, upstream, weight, scales, clip_mask, rot_block):
    groups = scales.shape[0]
    subs = hidden.shape[0] // SUB
    if lax.axis_size("dp") != 4 or lax.axis_size("tensor") != subs or groups % 8 != 4:
        return general_shards(hidden, upstream, weight, scales, clip_mask, rot_block)
    per = 4
    units = groups // per
    sizes = (per * (units - 2 * units // 5), per * (2 * units // 5))
    starts = (0, sizes[0])
    half = subs // 2
    counts = (subs, subs, subs, half, half)

    def scatter_first(parts_of):
        return partner(parts_of[3], "dp", 1), partner(parts_of[4], "dp", 2)

    def scatter_second(parts_of, received, after):
        x_part, y_part = small_call(
            relay_kernel,
            "relay",
            [parts_of[1], parts_of[2], *received],
            [parts_of[1].shape] * 2,
            2,
            after,
        )
        return x_part, partner(x_part, "dp", 1), partner(y_part, "dp", 2)

    def gather(value):
        x_part, y_part = partner(value, "dp", 1), partner(value, "dp", 2)
        return value, x_part, y_part, partner(y_part[:half], "dp", 1), partner(
            x_part[half:], "dp", 2
        )

    up = gather_upstream(upstream)
    (local,) = local_forward(hidden, rot_block, (groups,))
    forth = exchange(local)
    unit0 = unit_grads(up, weight, scales, starts[0], sizes[0], per, counts, after=(local,))
    first0 = scatter_first(unit0)
    turned = transform(forth, after=(unit0[0],))
    rotated = exchange(turned)
    unit1 = unit_grads(up, weight, scales, starts[1], sizes[1], per, counts, after=(turned,))
    first1 = scatter_first(unit1)
    relayed0, *second0 = scatter_second(unit0, first0, after=(unit1[0],))
    relayed1, *second1 = scatter_second(unit1, first1, after=(relayed0,))
    summed = total((unit0[0], *second0), None, starts[0], groups, per, after=(turned,))
    summed = total((unit1[0], *second1), summed, starts[1], groups, per, after=(rotated,))
    back = exchange(summed)
    gathered = gather(rotated)
    mixed = transform(back, after=gathered[1:3])
    final = exchange(mixed)
    buffer, scale0 = weight_grads(
        gathered, up, weight, scales, clip_mask, None, starts[0], sizes[0], per, after=(mixed,)
    )
    buffer, scale1 = weight_grads(
        gathered, up, weight, scales, clip_mask, buffer, starts[1], sizes[1], per
    )
    grad_hidden = local_backward([final], rot_block, (groups,), after=(scale1,))
    return grad_hidden, buffer, jnp.concatenate([scale0, scale1], axis=0)


def solution(mesh):
    return jax.shard_map(
        shards,
        mesh=mesh,
        in_specs=(
            P("dp", "tensor"),
            P("dp", None),
            P("tensor", "dp"),
            P("tensor", "dp"),
            P("tensor", "dp"),
            P(),
        ),
        out_specs=(P("dp", "tensor"), P("tensor", "dp"), P("tensor", "dp")),
        check_vma=False,
    )
```

```python
import functools

import jax
import jax.numpy as jnp
from jax import lax
from jax.experimental import pallas as pl
from jax.experimental.pallas import tpu as pltpu
from jax.sharding import PartitionSpec as P

HB = 128
GROUP = 128
SUB = 16
ROWS = 8
F32 = jnp.float32
BF16 = jnp.bfloat16


def nt_dot(a, b):
    return lax.dot_general(a, b, (((1,), (1,)), ((), ())), preferred_element_type=F32)


def nn_dot(a, b):
    return lax.dot_general(a, b, (((1,), (0,)), ((), ())), preferred_element_type=F32)


def tn_dot(a, b):
    return lax.dot_general(a, b, (((0,), (0,)), ((), ())), preferred_element_type=F32)


def split2(value):
    high = value.astype(BF16)
    return high, (value - high.astype(F32)).astype(BF16)


def sign_matrix(size):
    both = lax.broadcasted_iota(jnp.int32, (size, size), 0) & lax.broadcasted_iota(
        jnp.int32, (size, size), 1
    )
    parity = jnp.zeros((size, size), jnp.int32)
    for bit in range(size.bit_length() - 1):
        parity = parity ^ ((both >> bit) & 1)
    return (1 - 2 * parity).astype(F32).astype(BF16)


def build_mixing(rot_ref, high_ref, low_ref, sign_ref, transposed):
    blocks = rot_ref.shape[0]
    size = blocks * ROWS
    row = lax.broadcasted_iota(jnp.int32, (size, blocks), 0)
    col = lax.broadcasted_iota(jnp.int32, (size, blocks), 1)
    pick = ((row >> 3) == col).astype(F32).astype(BF16)
    rows = lax.broadcasted_iota(jnp.int32, (size, size), 0)
    cols = lax.broadcasted_iota(jnp.int32, (size, size), 1)
    same = (rows & (ROWS - 1)) == (cols & (ROWS - 1))
    for part, out_ref in zip(split2(rot_ref[...]), (high_ref, low_ref)):
        spread = nt_dot(pick, part) if transposed else nn_dot(pick, part)
        full = nt_dot(spread.astype(BF16), pick)
        out_ref[...] = jnp.where(same, full, 0.0).astype(BF16)
    sign_ref[...] = sign_matrix(HB)


def mix_rows(tiles, high_ref, low_ref, sign_ref):
    blocks = len(tiles[0])
    stacked = jnp.concatenate([jnp.concatenate(one, axis=0).astype(BF16) for one in tiles], axis=1)
    mixed = nn_dot(high_ref[...], stacked) + nn_dot(low_ref[...], stacked)
    results = []
    for j in range(len(tiles)):
        part = nn_dot(mixed[:, j * HB : (j + 1) * HB].astype(BF16), sign_ref[...])
        results.append((part * HB ** (-0.5)).reshape(blocks, ROWS, HB))
    return results


def forward_kernel(sizes, x_ref, rot_ref, *refs):
    outs, (high_ref, low_ref, sign_ref) = refs[: len(sizes)], refs[len(sizes) :]
    blocks = rot_ref.shape[0]

    @pl.when(pl.program_id(0) == 0)
    def _():
        build_mixing(rot_ref, high_ref, low_ref, sign_ref, True)

    rows = x_ref.shape[0]
    wide = [x_ref[:, k * HB : (k + 1) * HB].astype(F32) for k in range(blocks)]
    tiles = [[one[j : j + ROWS] for one in wide] for j in range(0, rows, ROWS)]
    results = mix_rows(tiles, high_ref, low_ref, sign_ref)
    for j in range(rows // SUB):
        both = jnp.concatenate([results[2 * j], results[2 * j + 1]], axis=1).astype(BF16)
        start = 0
        for size, out_ref in zip(sizes, outs):
            out_ref[j] = both[start : start + size]
            start += size


def backward_kernel(sizes, *refs):
    ins, (rot_ref, out_ref, high_ref, low_ref, sign_ref) = refs[: len(sizes)], refs[len(sizes) :]
    blocks = rot_ref.shape[0]

    @pl.when(pl.program_id(0) == 0)
    def _():
        build_mixing(rot_ref, high_ref, low_ref, sign_ref, False)

    rows = out_ref.shape[0]
    tiles = []
    for j in range(rows // SUB):
        wide = [
            in_ref[j, c].astype(F32) for size, in_ref in zip(sizes, ins) for c in range(size)
        ]
        tiles += [[one[:ROWS] for one in wide], [one[ROWS:] for one in wide]]
    results = mix_rows(tiles, high_ref, low_ref, sign_ref)
    for j in range(rows // SUB):
        both = jnp.concatenate([results[2 * j], results[2 * j + 1]], axis=1).astype(BF16)
        for k in range(blocks):
            out_ref[j * SUB : (j + 1) * SUB, k * HB : (k + 1) * HB] = both[k]


def local_scratch(blocks):
    return [
        pltpu.VMEM((blocks * ROWS, blocks * ROWS), BF16),
        pltpu.VMEM((blocks * ROWS, blocks * ROWS), BF16),
        pltpu.VMEM((HB, HB), BF16),
    ]


FREE = pl.CostEstimate(flops=0, bytes_accessed=0, transcendentals=0)
LONG = pl.CostEstimate(flops=10**12, bytes_accessed=0, transcendentals=0)
SMALL = 12 << 20

ANYWHERE = pl.BlockSpec(memory_space=pl.ANY)


def in_hbm(*values):
    return [pltpu.with_memory_space_constraint(value, pltpu.HBM) for value in values]


def drop_inputs(kernel, start, count):
    def run(*refs):
        kernel(*refs[:start], *refs[start + count :])

    return run


def local_forward(hidden, rot_block, sizes):
    rows, width = hidden.shape
    blocks = width // HB
    parts = 2
    return pl.pallas_call(
        functools.partial(forward_kernel, sizes),
        grid=(rows // (SUB * parts),),
        in_specs=[
            pl.BlockSpec((SUB * parts, width), lambda i: (i, 0)),
            pl.BlockSpec((blocks, blocks), lambda i: (0, 0)),
        ],
        out_specs=[pl.BlockSpec((parts, size, SUB, HB), lambda i: (i, 0, 0, 0)) for size in sizes],
        out_shape=[pltpu.HBM((rows // SUB, size, SUB, HB), BF16) for size in sizes],
        scratch_shapes=local_scratch(blocks),
        compiler_params=pltpu.CompilerParams(vmem_limit_bytes=60 << 20),
        cost_estimate=FREE,
        name="local_forward",
    )(*in_hbm(hidden), rot_block)


def local_backward(mixed, rot_block, sizes, after=()):
    count = mixed[0].shape[0]
    rows = count * SUB
    blocks = rot_block.shape[0]
    parts = 2
    return pl.pallas_call(
        drop_inputs(functools.partial(backward_kernel, sizes), len(sizes) + 1, len(after)),
        grid=(count // parts,),
        in_specs=[pl.BlockSpec((parts, size, SUB, HB), lambda i: (i, 0, 0, 0)) for size in sizes]
        + [pl.BlockSpec((blocks, blocks), lambda i: (0, 0))]
        + [ANYWHERE] * len(after),
        out_specs=pl.BlockSpec((parts * SUB, blocks * HB), lambda i: (i, 0)),
        out_shape=pltpu.HBM((rows, blocks * HB), BF16),
        scratch_shapes=local_scratch(blocks),
        compiler_params=pltpu.CompilerParams(vmem_limit_bytes=60 << 20),
        cost_estimate=FREE,
        name="local_backward",
    )(*mixed, rot_block, *in_hbm(*after))


def units_kernel(first, per, up_ref, w_ref, s_ref, *outs):
    base = first + pl.program_id(0) * per
    pair = 2 if per % 2 == 0 else 1
    for start in range(0, per, pair):
        quant = jnp.concatenate(
            [
                (
                    w_ref[g * GROUP : (g + 1) * GROUP, :].astype(F32) * s_ref[pl.ds(base + g, 1), :]
                ).astype(BF16)
                for g in range(start, start + pair)
            ],
            axis=0,
        )
        result = nt_dot(up_ref[...], quant).astype(BF16)
        token = 0
        for out_ref in outs:
            for q in range(out_ref.shape[0]):
                for g in range(pair):
                    out_ref[q, start + g] = result[token : token + SUB, g * GROUP : (g + 1) * GROUP]
                token += SUB


def unit_grads(up, weight, scales, first, size, per, counts, after=()):
    tokens, cols = up.shape
    offset = first // per
    return pl.pallas_call(
        drop_inputs(functools.partial(units_kernel, first, per), 3, len(after)),
        grid=(size // per,),
        in_specs=[
            pl.BlockSpec((tokens, cols), lambda i: (0, 0)),
            pl.BlockSpec((per * GROUP, cols), lambda i: (offset + i, 0)),
            pl.BlockSpec(scales.shape, lambda i: (0, 0)),
        ]
        + [ANYWHERE] * len(after),
        out_specs=[pl.BlockSpec((count, per, SUB, HB), lambda i: (0, i, 0, 0)) for count in counts],
        out_shape=[pltpu.HBM((count, size, SUB, HB), BF16) for count in counts],
        compiler_params=pltpu.CompilerParams(vmem_limit_bytes=26 << 20),
        cost_estimate=FREE,
        name="unit_grads",
    )(up, *in_hbm(weight, scales), *in_hbm(*after))


def weights_kernel(first, per, pieces, *refs):
    rots = refs[:pieces]
    up_ref, w_ref, s_ref, m_ref = refs[pieces : pieces + 4]
    gw_ref, gs_ref = refs[-2:]
    step = pl.program_id(0)
    base = first + step * per
    left = jnp.concatenate(
        [
            jnp.concatenate(
                [rot_ref[q, g] for rot_ref in rots for q in range(rot_ref.shape[0])], axis=0
            )
            for g in range(per)
        ],
        axis=1,
    )
    cols = up_ref.shape[1]
    tile = min(256, cols)
    for e in range(cols // tile):
        span = slice(e * tile, (e + 1) * tile)
        grad = tn_dot(left, up_ref[:, span])
        for g in range(per):
            rows = slice(g * GROUP, (g + 1) * GROUP)
            piece = grad[rows]
            scale = s_ref[pl.ds(base + g, 1), span]
            kept = m_ref[pl.ds(base + g, 1), span].astype(F32) * scale
            gw_ref[rows, span] = (piece * kept).astype(BF16)
            gs_ref[pl.ds(step * per + g, 1), span] = jnp.sum(
                piece * w_ref[rows, span].astype(F32), axis=0, keepdims=True
            )


def weight_grads(rotated, up, weight, scales, mask, buffer, first, size, per, after=()):
    tokens, cols = up.shape
    offset = first // per
    specs = [
        pl.BlockSpec((piece.shape[0], per, SUB, HB), lambda i: (0, offset + i, 0, 0))
        for piece in rotated
    ] + [
        pl.BlockSpec((tokens, cols), lambda i: (0, 0)),
        pl.BlockSpec((per * GROUP, cols), lambda i: (offset + i, 0)),
        pl.BlockSpec(scales.shape, lambda i: (0, 0)),
        pl.BlockSpec(scales.shape, lambda i: (0, 0)),
    ]
    args = [*rotated, up, *in_hbm(weight, scales, mask)]
    aliases = {}
    if buffer is not None:
        aliases = {len(args): 0}
        args.append(buffer)
        specs.append(ANYWHERE)
    return pl.pallas_call(
        functools.partial(weights_kernel, first, per, len(rotated)),
        grid=(size // per,),
        in_specs=specs + [ANYWHERE] * len(after),
        out_specs=[
            pl.BlockSpec((per * GROUP, cols), lambda i: (offset + i, 0)),
            pl.BlockSpec((size, cols), lambda i: (0, 0)),
        ],
        out_shape=[
            pltpu.HBM(weight.shape, BF16),
            jax.ShapeDtypeStruct((size, cols), F32),
        ],
        input_output_aliases=aliases,
        compiler_params=pltpu.CompilerParams(vmem_limit_bytes=26 << 20),
        cost_estimate=LONG,
        name="weight_grads",
    )(*args, *in_hbm(*after))


def small_call(kernel, name, ins, outs, steps, after=(), cost=FREE):
    def spec(shape, dim):
        block = tuple(n // steps if d == dim else n for d, n in enumerate(shape))
        return pl.BlockSpec(
            block, lambda i: tuple(i if d == dim else 0 for d in range(len(shape)))
        )

    return pl.pallas_call(
        drop_inputs(kernel, len(ins), len(after)),
        grid=(steps,),
        in_specs=[spec(value.shape, 1) for value in ins] + [ANYWHERE] * len(after),
        out_specs=[spec(shape, 1) for shape in outs],
        out_shape=[pltpu.HBM(shape, BF16) for shape in outs],
        compiler_params=pltpu.CompilerParams(vmem_limit_bytes=SMALL),
        cost_estimate=cost,
        name=name,
    )(*ins, *in_hbm(*after))


def transform_kernel(x_ref, out_ref):
    count = x_ref.shape[0]
    values = [x_ref[t].astype(F32) for t in range(count)]
    stride = 1
    while stride < count:
        for t in range(count):
            if not t & stride:
                a, b = values[t], values[t | stride]
                values[t], values[t | stride] = a + b, a - b
        stride *= 2
    for t in range(count):
        out_ref[t] = (values[t] * count ** (-0.5)).astype(BF16)


def transform(value, after=(), cost=FREE):
    steps = 4 if value.shape[1] % 4 == 0 else 1
    return small_call(
        transform_kernel, "transform", [value], [value.shape], steps, after, cost
    )[0]


def exchange(value):
    return lax.all_to_all(value, "tensor", split_axis=0, concat_axis=0, tiled=True)


def partner(value, axis, mask):
    size = lax.axis_size(axis)
    return lax.ppermute(value, axis, [(i, i ^ mask) for i in range(size)])


def mix_across(value):
    size = lax.axis_size("tensor")
    index = lax.axis_index("tensor")
    masks = [1 << i for i in range(size.bit_length() - 1)]
    for place, mask in enumerate(masks):
        other = partner(value, "tensor", mask).astype(F32)
        sign = jnp.where((index & mask) != 0, -1.0, 1.0).astype(F32)
        total = other + sign * value.astype(F32)
        if place == len(masks) - 1:
            total = total * size ** (-0.5)
        value = total.astype(BF16)
    return value


def gather_upstream(upstream):
    rows, width = upstream.shape
    parts = lax.axis_size("dp")
    cols = width // parts
    half = rows // 2
    index = lax.axis_index("dp")
    core = lax.axis_index("tensor") & 1
    own = lax.dynamic_slice(upstream, (0, index * cols), (rows, cols))
    mine = [
        partner(
            lax.dynamic_slice(upstream, (core * half, (index ^ m) * cols), (half, cols)), "dp", m
        )
        for m in range(1, parts)
    ]
    mine = jnp.stack(mine)
    other = partner(mine, "tensor", 1)
    low = jnp.where(core == 0, mine, other)
    high = jnp.where(core == 0, other, mine)
    far = jnp.concatenate([low, high], axis=1).reshape((parts - 1) * rows, cols)
    return jnp.concatenate([own, far], axis=0)


def relay_kernel(x_ref, y_ref, a_ref, b_ref, x_out, y_out):
    half = a_ref.shape[0]
    x_out[:half] = x_ref[:half]
    x_out[half:] = (x_ref[half:].astype(F32) + b_ref[...].astype(F32)).astype(BF16)
    y_out[:half] = (y_ref[:half].astype(F32) + a_ref[...].astype(F32)).astype(BF16)
    y_out[half:] = y_ref[half:]


def total_kernel(count, *refs):
    out_ref = refs[-1]
    start = 0
    for i in range(count):
        own_ref, x_ref, y_ref = refs[3 * i : 3 * i + 3]
        size = own_ref.shape[1]
        out_ref[:, start : start + size] = (
            own_ref[...].astype(F32) + x_ref[...].astype(F32) + y_ref[...].astype(F32)
        ).astype(BF16)
        start += size


def total(chunks, after=()):
    ins = [value for own, *far in chunks for value in (*in_hbm(own), *far)]
    subs = ins[0].shape[0]
    groups = sum(chunk[0].shape[1] for chunk in chunks)
    step = 2
    return pl.pallas_call(
        drop_inputs(functools.partial(total_kernel, len(chunks)), len(ins), len(after)),
        grid=(subs // step,),
        in_specs=[pl.BlockSpec((step,) + v.shape[1:], lambda i: (i, 0, 0, 0)) for v in ins]
        + [ANYWHERE] * len(after),
        out_specs=pl.BlockSpec((step, groups, SUB, HB), lambda i: (i, 0, 0, 0)),
        out_shape=pltpu.HBM((subs, groups, SUB, HB), BF16),
        compiler_params=pltpu.CompilerParams(vmem_limit_bytes=SMALL),
        cost_estimate=FREE,
        name="total",
    )(*ins, *in_hbm(*after))


def general_shards(hidden, upstream, weight, scales, clip_mask, rot_block):
    groups = scales.shape[0]
    rows = hidden.shape[0]
    parts = lax.axis_size("dp")
    subs = rows // SUB
    index = lax.axis_index("dp")

    up = gather_upstream(upstream)
    (local,) = local_forward(hidden, rot_block, (groups,))
    rotated = lax.all_gather(mix_across(local), "dp", axis=0, tiled=False)
    order = index ^ jnp.arange(parts)
    rotated = rotated[order].reshape((parts * subs,) + local.shape[1:])
    per = 4 if groups % 4 == 0 else 1
    (full,) = unit_grads(up, weight, scales, 0, groups, per, (parts * subs,))
    full = full.reshape((parts,) + local.shape)[order]
    mixed = mix_across(lax.psum_scatter(full, "dp", scatter_dimension=0, tiled=False))
    grad_weight, grad_scales = weight_grads(
        [rotated], up, weight, scales, clip_mask, None, 0, groups, per
    )
    grad_hidden = local_backward([mixed], rot_block, (groups,))
    return grad_hidden, grad_weight, grad_scales


def shards(hidden, upstream, weight, scales, clip_mask, rot_block):
    groups = scales.shape[0]
    subs = hidden.shape[0] // SUB
    if lax.axis_size("dp") != 4 or lax.axis_size("tensor") != subs or groups % 8 != 4:
        return general_shards(hidden, upstream, weight, scales, clip_mask, rot_block)
    per = 4
    units = groups // per
    sizes = (per * (units - units // 2), per * (units // 2))
    starts = (0, sizes[0])
    half = subs // 2
    counts = (subs, subs, subs, half, half)

    def scatter_first(parts_of):
        return partner(parts_of[3], "dp", 1), partner(parts_of[4], "dp", 2)

    def scatter_second(parts_of, received, after, cost=FREE):
        x_part, y_part = small_call(
            relay_kernel,
            "relay",
            [*in_hbm(parts_of[1], parts_of[2]), *received],
            [parts_of[1].shape] * 2,
            2,
            after,
            cost,
        )
        return x_part, partner(x_part, "dp", 1), partner(y_part, "dp", 2)

    def gather(value):
        x_part, y_part = partner(value, "dp", 1), partner(value, "dp", 2)
        return value, x_part, y_part, partner(y_part[:half], "dp", 1), partner(
            x_part[half:], "dp", 2
        )

    up = gather_upstream(upstream)
    (local,) = local_forward(hidden, rot_block, (groups,))
    forth = exchange(local)
    unit0 = unit_grads(up, weight, scales, starts[0], sizes[0], per, counts, after=(local,))
    first0 = scatter_first(unit0)
    unit1 = unit_grads(up, weight, scales, starts[1], sizes[1], per, counts, after=(unit0[0],))
    first1 = scatter_first(unit1)
    relayed0, *second0 = scatter_second(unit0, first0, after=(unit1[0],))
    turned = transform(forth, after=(relayed0,), cost=LONG)
    rotated = exchange(turned)
    relayed1, *second1 = scatter_second(unit1, first1, after=(turned,), cost=LONG)
    summed = total(((unit0[0], *second0), (unit1[0], *second1)), after=(rotated,))
    back = exchange(summed)
    gathered = gather(rotated)
    mixed = transform(back, cost=LONG)
    final = exchange(mixed)
    buffer, scale0 = weight_grads(
        gathered, up, weight, scales, clip_mask, None, starts[0], sizes[0], per, after=(mixed,)
    )
    buffer, scale1 = weight_grads(
        gathered, up, weight, scales, clip_mask, buffer, starts[1], sizes[1], per
    )
    grad_hidden = local_backward([final], rot_block, (groups,), after=(scale1,))
    return grad_hidden, buffer, jnp.concatenate([scale0, scale1], axis=0)


def solution(mesh):
    return jax.shard_map(
        shards,
        mesh=mesh,
        in_specs=(
            P("dp", "tensor"),
            P("dp", None),
            P("tensor", "dp"),
            P("tensor", "dp"),
            P("tensor", "dp"),
            P(),
        ),
        out_specs=(P("dp", "tensor"), P("tensor", "dp"), P("tensor", "dp")),
        check_vma=False,
    )
```

```python
import functools

import jax
import jax.numpy as jnp
from jax import lax
from jax.experimental import pallas as pl
from jax.experimental.pallas import tpu as pltpu
from jax.sharding import PartitionSpec as P

HB = 128
GROUP = 128
SUB = 16
ROWS = 8
F32 = jnp.float32
BF16 = jnp.bfloat16


def nt_dot(a, b):
    return lax.dot_general(a, b, (((1,), (1,)), ((), ())), preferred_element_type=F32)


def nn_dot(a, b):
    return lax.dot_general(a, b, (((1,), (0,)), ((), ())), preferred_element_type=F32)


def tn_dot(a, b):
    return lax.dot_general(a, b, (((0,), (0,)), ((), ())), preferred_element_type=F32)


def split2(value):
    high = value.astype(BF16)
    return high, (value - high.astype(F32)).astype(BF16)


def sign_matrix(size):
    both = lax.broadcasted_iota(jnp.int32, (size, size), 0) & lax.broadcasted_iota(
        jnp.int32, (size, size), 1
    )
    parity = jnp.zeros((size, size), jnp.int32)
    for bit in range(size.bit_length() - 1):
        parity = parity ^ ((both >> bit) & 1)
    return (1 - 2 * parity).astype(F32).astype(BF16)


def build_mixing(rot_ref, high_ref, low_ref, sign_ref, transposed):
    blocks = rot_ref.shape[0]
    size = blocks * ROWS
    row = lax.broadcasted_iota(jnp.int32, (size, blocks), 0)
    col = lax.broadcasted_iota(jnp.int32, (size, blocks), 1)
    pick = ((row >> 3) == col).astype(F32).astype(BF16)
    rows = lax.broadcasted_iota(jnp.int32, (size, size), 0)
    cols = lax.broadcasted_iota(jnp.int32, (size, size), 1)
    same = (rows & (ROWS - 1)) == (cols & (ROWS - 1))
    for part, out_ref in zip(split2(rot_ref[...]), (high_ref, low_ref)):
        spread = nt_dot(pick, part) if transposed else nn_dot(pick, part)
        full = nt_dot(spread.astype(BF16), pick)
        out_ref[...] = jnp.where(same, full, 0.0).astype(BF16)
    sign_ref[...] = sign_matrix(HB)


def mix_rows(tiles, high_ref, low_ref, sign_ref):
    blocks = len(tiles[0])
    stacked = jnp.concatenate([jnp.concatenate(one, axis=0).astype(BF16) for one in tiles], axis=1)
    mixed = nn_dot(high_ref[...], stacked) + nn_dot(low_ref[...], stacked)
    results = []
    for j in range(len(tiles)):
        part = nn_dot(mixed[:, j * HB : (j + 1) * HB].astype(BF16), sign_ref[...])
        results.append((part * HB ** (-0.5)).reshape(blocks, ROWS, HB))
    return results


def forward_kernel(sizes, x_ref, rot_ref, *refs):
    outs, (high_ref, low_ref, sign_ref) = refs[: len(sizes)], refs[len(sizes) :]
    blocks = rot_ref.shape[0]

    @pl.when(pl.program_id(0) == 0)
    def _():
        build_mixing(rot_ref, high_ref, low_ref, sign_ref, True)

    rows = x_ref.shape[0]
    wide = [x_ref[:, k * HB : (k + 1) * HB].astype(F32) for k in range(blocks)]
    tiles = [[one[j : j + ROWS] for one in wide] for j in range(0, rows, ROWS)]
    results = mix_rows(tiles, high_ref, low_ref, sign_ref)
    for j in range(rows // SUB):
        both = jnp.concatenate([results[2 * j], results[2 * j + 1]], axis=1).astype(BF16)
        start = 0
        for size, out_ref in zip(sizes, outs):
            out_ref[j] = both[start : start + size]
            start += size


def backward_kernel(sizes, *refs):
    ins, (rot_ref, out_ref, high_ref, low_ref, sign_ref) = refs[: len(sizes)], refs[len(sizes) :]
    blocks = rot_ref.shape[0]

    @pl.when(pl.program_id(0) == 0)
    def _():
        build_mixing(rot_ref, high_ref, low_ref, sign_ref, False)

    rows = out_ref.shape[0]
    tiles = []
    for j in range(rows // SUB):
        wide = [
            in_ref[j, c].astype(F32) for size, in_ref in zip(sizes, ins) for c in range(size)
        ]
        tiles += [[one[:ROWS] for one in wide], [one[ROWS:] for one in wide]]
    results = mix_rows(tiles, high_ref, low_ref, sign_ref)
    for j in range(rows // SUB):
        both = jnp.concatenate([results[2 * j], results[2 * j + 1]], axis=1).astype(BF16)
        for k in range(blocks):
            out_ref[j * SUB : (j + 1) * SUB, k * HB : (k + 1) * HB] = both[k]


def local_scratch(blocks):
    return [
        pltpu.VMEM((blocks * ROWS, blocks * ROWS), BF16),
        pltpu.VMEM((blocks * ROWS, blocks * ROWS), BF16),
        pltpu.VMEM((HB, HB), BF16),
    ]


FREE = pl.CostEstimate(flops=0, bytes_accessed=0, transcendentals=0)
LONG = pl.CostEstimate(flops=10**12, bytes_accessed=0, transcendentals=0)
SOME = pl.CostEstimate(flops=5_000_000_000, bytes_accessed=0, transcendentals=0)
SMALL = 12 << 20

ANYWHERE = pl.BlockSpec(memory_space=pl.ANY)


def in_hbm(*values):
    return [pltpu.with_memory_space_constraint(value, pltpu.HBM) for value in values]


def drop_inputs(kernel, start, count):
    def run(*refs):
        kernel(*refs[:start], *refs[start + count :])

    return run


def local_forward(hidden, rot_block, sizes):
    rows, width = hidden.shape
    blocks = width // HB
    parts = 2
    return pl.pallas_call(
        functools.partial(forward_kernel, sizes),
        grid=(rows // (SUB * parts),),
        in_specs=[
            pl.BlockSpec((SUB * parts, width), lambda i: (i, 0)),
            pl.BlockSpec((blocks, blocks), lambda i: (0, 0)),
        ],
        out_specs=[pl.BlockSpec((parts, size, SUB, HB), lambda i: (i, 0, 0, 0)) for size in sizes],
        out_shape=[pltpu.HBM((rows // SUB, size, SUB, HB), BF16) for size in sizes],
        scratch_shapes=local_scratch(blocks),
        compiler_params=pltpu.CompilerParams(vmem_limit_bytes=60 << 20),
        cost_estimate=FREE,
        name="local_forward",
    )(*in_hbm(hidden), rot_block)


def local_backward(mixed, rot_block, sizes, after=()):
    count = mixed[0].shape[0]
    rows = count * SUB
    blocks = rot_block.shape[0]
    parts = 2
    return pl.pallas_call(
        drop_inputs(functools.partial(backward_kernel, sizes), len(sizes) + 1, len(after)),
        grid=(count // parts,),
        in_specs=[pl.BlockSpec((parts, size, SUB, HB), lambda i: (i, 0, 0, 0)) for size in sizes]
        + [pl.BlockSpec((blocks, blocks), lambda i: (0, 0))]
        + [ANYWHERE] * len(after),
        out_specs=pl.BlockSpec((parts * SUB, blocks * HB), lambda i: (i, 0)),
        out_shape=pltpu.HBM((rows, blocks * HB), BF16),
        scratch_shapes=local_scratch(blocks),
        compiler_params=pltpu.CompilerParams(vmem_limit_bytes=60 << 20),
        cost_estimate=FREE,
        name="local_backward",
    )(*mixed, rot_block, *in_hbm(*after))


def units_kernel(first, per, up_ref, w_ref, s_ref, *refs):
    outs, quant_ref = refs[:-1], refs[-1]
    base = first + pl.program_id(0) * per
    for g in range(per):
        rows = slice(g * GROUP, (g + 1) * GROUP)
        quant_ref[rows, :] = (w_ref[rows, :].astype(F32) * s_ref[pl.ds(base + g, 1), :]).astype(
            BF16
        )
    result = nt_dot(up_ref[...], quant_ref[...]).astype(BF16)
    token = 0
    for out_ref in outs:
        for q in range(out_ref.shape[0]):
            for g in range(per):
                out_ref[q, g] = result[token : token + SUB, g * GROUP : (g + 1) * GROUP]
            token += SUB


def unit_grads(up, weight, scales, first, size, per, counts, after=(), cost=FREE):
    tokens, cols = up.shape
    offset = first // per
    return pl.pallas_call(
        drop_inputs(functools.partial(units_kernel, first, per), 3, len(after)),
        grid=(size // per,),
        in_specs=[
            pl.BlockSpec((tokens, cols), lambda i: (0, 0)),
            pl.BlockSpec((per * GROUP, cols), lambda i: (offset + i, 0)),
            pl.BlockSpec(scales.shape, lambda i: (0, 0)),
        ]
        + [ANYWHERE] * len(after),
        out_specs=[pl.BlockSpec((count, per, SUB, HB), lambda i: (0, i, 0, 0)) for count in counts],
        out_shape=[pltpu.HBM((count, size, SUB, HB), BF16) for count in counts],
        scratch_shapes=[pltpu.VMEM((per * GROUP, cols), BF16)],
        compiler_params=pltpu.CompilerParams(vmem_limit_bytes=26 << 20),
        cost_estimate=cost,
        name="unit_grads",
    )(up, *in_hbm(weight, scales), *in_hbm(*after))


def weights_kernel(first, per, pieces, *refs):
    rots = refs[:pieces]
    up_ref, w_ref, s_ref, m_ref = refs[pieces : pieces + 4]
    gw_ref, gs_ref = refs[-2:]
    step = pl.program_id(0)
    base = first + step * per
    left = jnp.concatenate(
        [
            jnp.concatenate(
                [rot_ref[q, g] for rot_ref in rots for q in range(rot_ref.shape[0])], axis=0
            )
            for g in range(per)
        ],
        axis=1,
    )
    cols = up_ref.shape[1]
    tile = min(256, cols)
    for e in range(cols // tile):
        span = slice(e * tile, (e + 1) * tile)
        grad = tn_dot(left, up_ref[:, span])
        for g in range(per):
            rows = slice(g * GROUP, (g + 1) * GROUP)
            piece = grad[rows]
            scale = s_ref[pl.ds(base + g, 1), span]
            kept = m_ref[pl.ds(base + g, 1), span].astype(F32) * scale
            gw_ref[rows, span] = (piece * kept).astype(BF16)
            gs_ref[pl.ds(step * per + g, 1), span] = jnp.sum(
                piece * w_ref[rows, span].astype(F32), axis=0, keepdims=True
            )


def weight_grads(rotated, up, weight, scales, mask, buffer, first, size, per, after=()):
    tokens, cols = up.shape
    offset = first // per
    specs = [
        pl.BlockSpec((piece.shape[0], per, SUB, HB), lambda i: (0, offset + i, 0, 0))
        for piece in rotated
    ] + [
        pl.BlockSpec((tokens, cols), lambda i: (0, 0)),
        pl.BlockSpec((per * GROUP, cols), lambda i: (offset + i, 0)),
        pl.BlockSpec(scales.shape, lambda i: (0, 0)),
        pl.BlockSpec(scales.shape, lambda i: (0, 0)),
    ]
    args = [*rotated, up, *in_hbm(weight, scales, mask)]
    aliases = {}
    if buffer is not None:
        aliases = {len(args): 0}
        args.append(buffer)
        specs.append(ANYWHERE)
    return pl.pallas_call(
        functools.partial(weights_kernel, first, per, len(rotated)),
        grid=(size // per,),
        in_specs=specs + [ANYWHERE] * len(after),
        out_specs=[
            pl.BlockSpec((per * GROUP, cols), lambda i: (offset + i, 0)),
            pl.BlockSpec((size, cols), lambda i: (0, 0)),
        ],
        out_shape=[
            pltpu.HBM(weight.shape, BF16),
            jax.ShapeDtypeStruct((size, cols), F32),
        ],
        input_output_aliases=aliases,
        compiler_params=pltpu.CompilerParams(vmem_limit_bytes=26 << 20),
        cost_estimate=LONG,
        name="weight_grads",
    )(*args, *in_hbm(*after))


def small_call(kernel, name, ins, outs, steps, after=(), cost=FREE):
    def spec(shape, dim):
        block = tuple(n // steps if d == dim else n for d, n in enumerate(shape))
        return pl.BlockSpec(
            block, lambda i: tuple(i if d == dim else 0 for d in range(len(shape)))
        )

    return pl.pallas_call(
        drop_inputs(kernel, len(ins), len(after)),
        grid=(steps,),
        in_specs=[spec(value.shape, 1) for value in ins] + [ANYWHERE] * len(after),
        out_specs=[spec(shape, 1) for shape in outs],
        out_shape=[pltpu.HBM(shape, BF16) for shape in outs],
        compiler_params=pltpu.CompilerParams(vmem_limit_bytes=SMALL),
        cost_estimate=cost,
        name=name,
    )(*ins, *in_hbm(*after))


def gate(value, after):
    return pl.pallas_call(
        drop_inputs(lambda x_ref, out_ref: None, 1, len(after)),
        in_specs=[ANYWHERE] * (1 + len(after)),
        out_specs=ANYWHERE,
        out_shape=pltpu.HBM(value.shape, value.dtype),
        input_output_aliases={0: 0},
        cost_estimate=FREE,
        name="gate",
    )(*in_hbm(value, *after))


def transform_kernel(x_ref, out_ref):
    count = x_ref.shape[0]
    values = [x_ref[t].astype(F32) for t in range(count)]
    stride = 1
    while stride < count:
        for t in range(count):
            if not t & stride:
                a, b = values[t], values[t | stride]
                values[t], values[t | stride] = a + b, a - b
        stride *= 2
    for t in range(count):
        out_ref[t] = (values[t] * count ** (-0.5)).astype(BF16)


def transform(value, after=(), cost=FREE):
    steps = 4 if value.shape[1] % 4 == 0 else 1
    return small_call(
        transform_kernel, "transform", [value], [value.shape], steps, after, cost
    )[0]


def exchange(value):
    return lax.all_to_all(value, "tensor", split_axis=0, concat_axis=0, tiled=True)


def partner(value, axis, mask):
    size = lax.axis_size(axis)
    return lax.ppermute(value, axis, [(i, i ^ mask) for i in range(size)])


def mix_across(value):
    size = lax.axis_size("tensor")
    index = lax.axis_index("tensor")
    masks = [1 << i for i in range(size.bit_length() - 1)]
    for place, mask in enumerate(masks):
        other = partner(value, "tensor", mask).astype(F32)
        sign = jnp.where((index & mask) != 0, -1.0, 1.0).astype(F32)
        total = other + sign * value.astype(F32)
        if place == len(masks) - 1:
            total = total * size ** (-0.5)
        value = total.astype(BF16)
    return value


def gather_upstream(upstream):
    rows, width = upstream.shape
    parts = lax.axis_size("dp")
    cols = width // parts
    half = rows // 2
    index = lax.axis_index("dp")
    core = lax.axis_index("tensor") & 1
    own = lax.dynamic_slice(upstream, (0, index * cols), (rows, cols))
    mine = [
        partner(
            lax.dynamic_slice(upstream, (core * half, (index ^ m) * cols), (half, cols)), "dp", m
        )
        for m in range(1, parts)
    ]
    mine = jnp.stack(mine)
    other = partner(mine, "tensor", 1)
    low = jnp.where(core == 0, mine, other)
    high = jnp.where(core == 0, other, mine)
    far = jnp.concatenate([low, high], axis=1).reshape((parts - 1) * rows, cols)
    return jnp.concatenate([own, far], axis=0)


def relay_kernel(x_ref, y_ref, a_ref, b_ref, x_out, y_out):
    half = a_ref.shape[0]
    x_out[:half] = x_ref[:half]
    x_out[half:] = (x_ref[half:].astype(F32) + b_ref[...].astype(F32)).astype(BF16)
    y_out[:half] = (y_ref[:half].astype(F32) + a_ref[...].astype(F32)).astype(BF16)
    y_out[half:] = y_ref[half:]


def total_kernel(count, *refs):
    out_ref = refs[-1]
    start = 0
    for i in range(count):
        own_ref, x_ref, y_ref = refs[3 * i : 3 * i + 3]
        size = own_ref.shape[1]
        out_ref[:, start : start + size] = (
            own_ref[...].astype(F32) + x_ref[...].astype(F32) + y_ref[...].astype(F32)
        ).astype(BF16)
        start += size


def total(chunks, after=()):
    ins = [value for own, *far in chunks for value in (*in_hbm(own), *far)]
    subs = ins[0].shape[0]
    groups = sum(chunk[0].shape[1] for chunk in chunks)
    step = 2
    return pl.pallas_call(
        drop_inputs(functools.partial(total_kernel, len(chunks)), len(ins), len(after)),
        grid=(subs // step,),
        in_specs=[pl.BlockSpec((step,) + v.shape[1:], lambda i: (i, 0, 0, 0)) for v in ins]
        + [ANYWHERE] * len(after),
        out_specs=pl.BlockSpec((step, groups, SUB, HB), lambda i: (i, 0, 0, 0)),
        out_shape=pltpu.HBM((subs, groups, SUB, HB), BF16),
        compiler_params=pltpu.CompilerParams(vmem_limit_bytes=SMALL),
        cost_estimate=FREE,
        name="total",
    )(*ins, *in_hbm(*after))


def general_shards(hidden, upstream, weight, scales, clip_mask, rot_block):
    groups = scales.shape[0]
    rows = hidden.shape[0]
    parts = lax.axis_size("dp")
    subs = rows // SUB
    index = lax.axis_index("dp")

    up = gather_upstream(upstream)
    (local,) = local_forward(hidden, rot_block, (groups,))
    rotated = lax.all_gather(mix_across(local), "dp", axis=0, tiled=False)
    order = index ^ jnp.arange(parts)
    rotated = rotated[order].reshape((parts * subs,) + local.shape[1:])
    per = 4 if groups % 4 == 0 else 1
    (full,) = unit_grads(up, weight, scales, 0, groups, per, (parts * subs,))
    full = full.reshape((parts,) + local.shape)[order]
    mixed = mix_across(lax.psum_scatter(full, "dp", scatter_dimension=0, tiled=False))
    grad_weight, grad_scales = weight_grads(
        [rotated], up, weight, scales, clip_mask, None, 0, groups, per
    )
    grad_hidden = local_backward([mixed], rot_block, (groups,))
    return grad_hidden, grad_weight, grad_scales


def shards(hidden, upstream, weight, scales, clip_mask, rot_block):
    groups = scales.shape[0]
    subs = hidden.shape[0] // SUB
    if lax.axis_size("dp") != 4 or lax.axis_size("tensor") != subs or groups % 8 != 4:
        return general_shards(hidden, upstream, weight, scales, clip_mask, rot_block)
    per = 4
    units = groups // per
    sizes = (per * (units - units // 2), per * (units // 2))
    starts = (0, sizes[0])
    half = subs // 2
    counts = (subs, subs, subs, half, half)

    def scatter_first(parts_of):
        return partner(parts_of[3], "dp", 1), partner(parts_of[4], "dp", 2)

    def scatter_second(parts_of, received, after, cost=FREE):
        x_part, y_part = small_call(
            relay_kernel,
            "relay",
            [*in_hbm(parts_of[1], parts_of[2]), *received],
            [parts_of[1].shape] * 2,
            2,
            after,
            cost,
        )
        return x_part, partner(x_part, "dp", 1), partner(y_part, "dp", 2)

    def gather(value):
        x_part, y_part = partner(value, "dp", 1), partner(value, "dp", 2)
        return value, x_part, y_part, partner(y_part[:half], "dp", 1), partner(
            x_part[half:], "dp", 2
        )

    up = gather_upstream(upstream)
    (local,) = local_forward(hidden, rot_block, (groups,))
    forth = exchange(local)
    unit0 = unit_grads(
        up, weight, scales, starts[0], sizes[0], per, counts, after=(local,), cost=SOME
    )
    first0 = scatter_first(unit0)
    unit1 = unit_grads(up, weight, scales, starts[1], sizes[1], per, counts, after=(unit0[0],))
    first1 = scatter_first(unit1)
    relayed0, *second0 = scatter_second(unit0, first0, after=(unit1[0],))
    turned = transform(forth, after=(relayed0,), cost=LONG)
    rotated = exchange(turned)
    relayed1, *second1 = scatter_second(unit1, first1, after=(turned,), cost=LONG)
    summed = gate(total(((unit0[0], *second0), (unit1[0], *second1))), after=(rotated,))
    back = exchange(summed)
    gathered = gather(rotated)
    mixed = transform(back, cost=LONG)
    final = exchange(mixed)
    buffer, scale0 = weight_grads(
        gathered, up, weight, scales, clip_mask, None, starts[0], sizes[0], per, after=(mixed,)
    )
    buffer, scale1 = weight_grads(
        gathered, up, weight, scales, clip_mask, buffer, starts[1], sizes[1], per
    )
    grad_hidden = local_backward([final], rot_block, (groups,), after=(scale1,))
    return grad_hidden, buffer, jnp.concatenate([scale0, scale1], axis=0)


def solution(mesh):
    return jax.shard_map(
        shards,
        mesh=mesh,
        in_specs=(
            P("dp", "tensor"),
            P("dp", None),
            P("tensor", "dp"),
            P("tensor", "dp"),
            P("tensor", "dp"),
            P(),
        ),
        out_specs=(P("dp", "tensor"), P("tensor", "dp"), P("tensor", "dp")),
        check_vma=False,
    )
```

```python
import functools

import jax
import jax.numpy as jnp
from jax import lax
from jax.experimental import pallas as pl
from jax.experimental.pallas import tpu as pltpu
from jax.sharding import PartitionSpec as P

HB = 128
GROUP = 128
SUB = 16
ROWS = 8
SIDE = 8
F32 = jnp.float32
BF16 = jnp.bfloat16


def nt_dot(a, b):
    return lax.dot_general(a, b, (((1,), (1,)), ((), ())), preferred_element_type=F32)


def nn_dot(a, b):
    return lax.dot_general(a, b, (((1,), (0,)), ((), ())), preferred_element_type=F32)


def tn_dot(a, b):
    return lax.dot_general(a, b, (((0,), (0,)), ((), ())), preferred_element_type=F32)


def split2(value):
    high = value.astype(BF16)
    return high, (value - high.astype(F32)).astype(BF16)


def sign_matrix(size):
    both = lax.broadcasted_iota(jnp.int32, (size, size), 0) & lax.broadcasted_iota(
        jnp.int32, (size, size), 1
    )
    parity = jnp.zeros((size, size), jnp.int32)
    for bit in range(size.bit_length() - 1):
        parity = parity ^ ((both >> bit) & 1)
    return (1 - 2 * parity).astype(F32).astype(BF16)


def build_mixing(rot_ref, high_ref, low_ref, sign_ref, transposed):
    blocks = rot_ref.shape[0]
    size = blocks * ROWS
    row = lax.broadcasted_iota(jnp.int32, (size, blocks), 0)
    col = lax.broadcasted_iota(jnp.int32, (size, blocks), 1)
    pick = ((row >> 3) == col).astype(F32).astype(BF16)
    rows = lax.broadcasted_iota(jnp.int32, (size, size), 0)
    cols = lax.broadcasted_iota(jnp.int32, (size, size), 1)
    same = (rows & (ROWS - 1)) == (cols & (ROWS - 1))
    for part, out_ref in zip(split2(rot_ref[...]), (high_ref, low_ref)):
        spread = nt_dot(pick, part) if transposed else nn_dot(pick, part)
        full = nt_dot(spread.astype(BF16), pick)
        out_ref[...] = jnp.where(same, full, 0.0).astype(BF16)
    sign_ref[...] = sign_matrix(HB)


def mix_rows(tiles, high_ref, low_ref, sign_ref):
    blocks = len(tiles[0])
    stacked = jnp.concatenate([jnp.concatenate(one, axis=0).astype(BF16) for one in tiles], axis=1)
    mixed = nn_dot(high_ref[...], stacked) + nn_dot(low_ref[...], stacked)
    results = []
    for j in range(len(tiles)):
        part = nn_dot(mixed[:, j * HB : (j + 1) * HB].astype(BF16), sign_ref[...])
        results.append((part * HB ** (-0.5)).reshape(blocks, ROWS, HB))
    return results


def forward_kernel(sizes, x_ref, rot_ref, *refs):
    outs, (high_ref, low_ref, sign_ref) = refs[: len(sizes)], refs[len(sizes) :]
    blocks = rot_ref.shape[0]

    @pl.when(pl.program_id(0) == 0)
    def _():
        build_mixing(rot_ref, high_ref, low_ref, sign_ref, True)

    rows = x_ref.shape[0]
    wide = [x_ref[:, k * HB : (k + 1) * HB].astype(F32) for k in range(blocks)]
    tiles = [[one[j : j + ROWS] for one in wide] for j in range(0, rows, ROWS)]
    results = mix_rows(tiles, high_ref, low_ref, sign_ref)
    for j in range(rows // SUB):
        both = jnp.concatenate([results[2 * j], results[2 * j + 1]], axis=1).astype(BF16)
        start = 0
        for size, out_ref in zip(sizes, outs):
            out_ref[j] = both[start : start + size]
            start += size


def backward_kernel(sizes, *refs):
    ins, (rot_ref, out_ref, high_ref, low_ref, sign_ref) = refs[: len(sizes)], refs[len(sizes) :]
    blocks = rot_ref.shape[0]

    @pl.when(pl.program_id(0) == 0)
    def _():
        build_mixing(rot_ref, high_ref, low_ref, sign_ref, False)

    rows = out_ref.shape[0]
    tiles = []
    for j in range(rows // SUB):
        wide = [
            in_ref[j, c].astype(F32) for size, in_ref in zip(sizes, ins) for c in range(size)
        ]
        tiles += [[one[:ROWS] for one in wide], [one[ROWS:] for one in wide]]
    results = mix_rows(tiles, high_ref, low_ref, sign_ref)
    for j in range(rows // SUB):
        both = jnp.concatenate([results[2 * j], results[2 * j + 1]], axis=1).astype(BF16)
        for k in range(blocks):
            out_ref[j * SUB : (j + 1) * SUB, k * HB : (k + 1) * HB] = both[k]


def local_scratch(blocks):
    return [
        pltpu.VMEM((blocks * ROWS, blocks * ROWS), BF16),
        pltpu.VMEM((blocks * ROWS, blocks * ROWS), BF16),
        pltpu.VMEM((HB, HB), BF16),
    ]


FREE = pl.CostEstimate(flops=0, bytes_accessed=0, transcendentals=0)
LONG = pl.CostEstimate(flops=10**12, bytes_accessed=0, transcendentals=0)
SOME = pl.CostEstimate(flops=5_000_000_000, bytes_accessed=0, transcendentals=0)
SMALL = 12 << 20

ANYWHERE = pl.BlockSpec(memory_space=pl.ANY)


def in_hbm(*values):
    return [pltpu.with_memory_space_constraint(value, pltpu.HBM) for value in values]


def drop_inputs(kernel, start, count):
    def run(*refs):
        kernel(*refs[:start], *refs[start + count :])

    return run


def local_forward(hidden, rot_block, sizes):
    rows, width = hidden.shape
    blocks = width // HB
    parts = 2
    return pl.pallas_call(
        functools.partial(forward_kernel, sizes),
        grid=(rows // (SUB * parts),),
        in_specs=[
            pl.BlockSpec((SUB * parts, width), lambda i: (i, 0)),
            pl.BlockSpec((blocks, blocks), lambda i: (0, 0)),
        ],
        out_specs=[pl.BlockSpec((parts, size, SUB, HB), lambda i: (i, 0, 0, 0)) for size in sizes],
        out_shape=[pltpu.HBM((rows // SUB, size, SUB, HB), BF16) for size in sizes],
        scratch_shapes=local_scratch(blocks),
        compiler_params=pltpu.CompilerParams(vmem_limit_bytes=60 << 20),
        cost_estimate=FREE,
        name="local_forward",
    )(*in_hbm(hidden), rot_block)


def local_backward(mixed, rot_block, sizes, after=()):
    count = mixed[0].shape[0]
    rows = count * SUB
    blocks = rot_block.shape[0]
    parts = 2
    return pl.pallas_call(
        drop_inputs(functools.partial(backward_kernel, sizes), len(sizes) + 1, len(after)),
        grid=(count // parts,),
        in_specs=[pl.BlockSpec((parts, size, SUB, HB), lambda i: (i, 0, 0, 0)) for size in sizes]
        + [pl.BlockSpec((blocks, blocks), lambda i: (0, 0))]
        + [ANYWHERE] * len(after),
        out_specs=pl.BlockSpec((parts * SUB, blocks * HB), lambda i: (i, 0)),
        out_shape=pltpu.HBM((rows, blocks * HB), BF16),
        scratch_shapes=local_scratch(blocks),
        compiler_params=pltpu.CompilerParams(vmem_limit_bytes=60 << 20),
        cost_estimate=FREE,
        name="local_backward",
    )(*mixed, rot_block, *in_hbm(*after))


def units_kernel(first, per, up_ref, w_ref, s_ref, *refs):
    outs, quant_ref = refs[:-1], refs[-1]
    base = first + pl.program_id(0) * per
    for g in range(per):
        rows = slice(g * GROUP, (g + 1) * GROUP)
        quant_ref[rows, :] = (w_ref[rows, :].astype(F32) * s_ref[pl.ds(base + g, 1), :]).astype(
            BF16
        )
    result = nt_dot(up_ref[...], quant_ref[...]).astype(BF16)
    token = 0
    for out_ref in outs:
        for q in range(out_ref.shape[0]):
            for g in range(per):
                out_ref[q, g] = result[token : token + SUB, g * GROUP : (g + 1) * GROUP]
            token += SUB


def unit_grads(up, weight, scales, first, size, per, counts, after=(), cost=FREE):
    tokens, cols = up.shape
    offset = first // per
    return pl.pallas_call(
        drop_inputs(functools.partial(units_kernel, first, per), 3, len(after)),
        grid=(size // per,),
        in_specs=[
            pl.BlockSpec((tokens, cols), lambda i: (0, 0)),
            pl.BlockSpec((per * GROUP, cols), lambda i: (offset + i, 0)),
            pl.BlockSpec(scales.shape, lambda i: (0, 0)),
        ]
        + [ANYWHERE] * len(after),
        out_specs=[pl.BlockSpec((count, per, SUB, HB), lambda i: (0, i, 0, 0)) for count in counts],
        out_shape=[pltpu.HBM((count, size, SUB, HB), BF16) for count in counts],
        scratch_shapes=[pltpu.VMEM((per * GROUP, cols), BF16)],
        compiler_params=pltpu.CompilerParams(vmem_limit_bytes=26 << 20),
        cost_estimate=cost,
        name="unit_grads",
    )(up, *in_hbm(weight, scales), *in_hbm(*after))


def weights_kernel(first, per, pieces, *refs):
    rots = refs[:pieces]
    up_ref, w_ref, s_ref, m_ref = refs[pieces : pieces + 4]
    gw_ref, gs_ref = refs[-2:]
    step = pl.program_id(0)
    base = first + step * per
    left = jnp.concatenate(
        [
            jnp.concatenate(
                [rot_ref[q, g] for rot_ref in rots for q in range(rot_ref.shape[0])], axis=0
            )
            for g in range(per)
        ],
        axis=1,
    )
    cols = up_ref.shape[1]
    tile = min(256, cols)
    for e in range(cols // tile):
        span = slice(e * tile, (e + 1) * tile)
        grad = tn_dot(left, up_ref[:, span])
        for g in range(per):
            rows = slice(g * GROUP, (g + 1) * GROUP)
            piece = grad[rows]
            scale = s_ref[pl.ds(base + g, 1), span]
            kept = m_ref[pl.ds(base + g, 1), span].astype(F32) * scale
            gw_ref[rows, span] = (piece * kept).astype(BF16)
            gs_ref[pl.ds(step * per + g, 1), span] = jnp.sum(
                piece * w_ref[rows, span].astype(F32), axis=0, keepdims=True
            )


def weight_grads(rotated, up, weight, scales, mask, buffer, first, size, per, after=(), cost=FREE):
    tokens, cols = up.shape
    offset = first // per
    specs = [
        pl.BlockSpec((piece.shape[0], per, SUB, HB), lambda i: (0, i, 0, 0))
        for piece in rotated
    ] + [
        pl.BlockSpec((tokens, cols), lambda i: (0, 0)),
        pl.BlockSpec((per * GROUP, cols), lambda i: (offset + i, 0)),
        pl.BlockSpec(scales.shape, lambda i: (0, 0)),
        pl.BlockSpec(scales.shape, lambda i: (0, 0)),
    ]
    args = [*rotated, up, *in_hbm(weight, scales, mask)]
    aliases = {}
    if buffer is not None:
        aliases = {len(args): 0}
        args.append(buffer)
        specs.append(ANYWHERE)
    return pl.pallas_call(
        functools.partial(weights_kernel, first, per, len(rotated)),
        grid=(size // per,),
        in_specs=specs + [ANYWHERE] * len(after),
        out_specs=[
            pl.BlockSpec((per * GROUP, cols), lambda i: (offset + i, 0)),
            pl.BlockSpec((size, cols), lambda i: (0, 0)),
        ],
        out_shape=[
            pltpu.HBM(weight.shape, BF16),
            jax.ShapeDtypeStruct((size, cols), F32),
        ],
        input_output_aliases=aliases,
        compiler_params=pltpu.CompilerParams(vmem_limit_bytes=26 << 20),
        cost_estimate=cost,
        name="weight_grads",
    )(*args, *in_hbm(*after))


def small_call(kernel, name, ins, outs, steps, after=(), cost=FREE):
    def spec(shape, dim):
        block = tuple(n // steps if d == dim else n for d, n in enumerate(shape))
        return pl.BlockSpec(
            block, lambda i: tuple(i if d == dim else 0 for d in range(len(shape)))
        )

    return pl.pallas_call(
        drop_inputs(kernel, len(ins), len(after)),
        grid=(steps,),
        in_specs=[spec(value.shape, 1) for value in ins] + [ANYWHERE] * len(after),
        out_specs=[spec(shape, 1) for shape in outs],
        out_shape=[pltpu.HBM(shape, BF16) for shape in outs],
        compiler_params=pltpu.CompilerParams(vmem_limit_bytes=SMALL),
        cost_estimate=cost,
        name=name,
    )(*ins, *in_hbm(*after))


def gate(value, after):
    return pl.pallas_call(
        drop_inputs(lambda x_ref, out_ref: None, 1, len(after)),
        in_specs=[ANYWHERE] * (1 + len(after)),
        out_specs=ANYWHERE,
        out_shape=pltpu.HBM(value.shape, value.dtype),
        input_output_aliases={0: 0},
        cost_estimate=FREE,
        name="gate",
    )(*in_hbm(value), *after)


def transform_kernel(x_ref, out_ref):
    count = x_ref.shape[0]
    values = [x_ref[t].astype(F32) for t in range(count)]
    stride = 1
    while stride < count:
        for t in range(count):
            if not t & stride:
                a, b = values[t], values[t | stride]
                values[t], values[t | stride] = a + b, a - b
        stride *= 2
    for t in range(count):
        out_ref[t] = (values[t] * count ** (-0.5)).astype(BF16)


def transform(value, after=(), cost=FREE):
    steps = 4 if value.shape[1] % 4 == 0 else 1
    return small_call(
        transform_kernel, "transform", [value], [value.shape], steps, after, cost
    )[0]


def exchange(value):
    return lax.all_to_all(value, "tensor", split_axis=0, concat_axis=0, tiled=True)


def partner(value, axis, mask):
    size = lax.axis_size(axis)
    return lax.ppermute(value, axis, [(i, i ^ mask) for i in range(size)])


def mix_across(value):
    size = lax.axis_size("tensor")
    index = lax.axis_index("tensor")
    masks = [1 << i for i in range(size.bit_length() - 1)]
    for place, mask in enumerate(masks):
        other = partner(value, "tensor", mask).astype(F32)
        sign = jnp.where((index & mask) != 0, -1.0, 1.0).astype(F32)
        total = other + sign * value.astype(F32)
        if place == len(masks) - 1:
            total = total * size ** (-0.5)
        value = total.astype(BF16)
    return value


def gather_upstream(upstream):
    rows, width = upstream.shape
    parts = lax.axis_size("dp")
    cols = width // parts
    half = rows // 2
    index = lax.axis_index("dp")
    core = lax.axis_index("tensor") & 1
    own = lax.dynamic_slice(upstream, (0, index * cols), (rows, cols))
    mine = [
        partner(
            lax.dynamic_slice(upstream, (core * half, (index ^ m) * cols), (half, cols)), "dp", m
        )
        for m in range(1, parts)
    ]
    mine = jnp.stack(mine)
    other = partner(mine, "tensor", 1)
    low = jnp.where(core == 0, mine, other)
    high = jnp.where(core == 0, other, mine)
    far = jnp.concatenate([low, high], axis=1).reshape((parts - 1) * rows, cols)
    return jnp.concatenate([own, far], axis=0)


def relay_kernel(x_ref, y_ref, a_ref, b_ref, x_out, y_out):
    half = a_ref.shape[0]
    x_out[:half] = x_ref[:half]
    x_out[half:] = (x_ref[half:].astype(F32) + b_ref[...].astype(F32)).astype(BF16)
    y_out[:half] = (y_ref[:half].astype(F32) + a_ref[...].astype(F32)).astype(BF16)
    y_out[half:] = y_ref[half:]


def total_kernel(count, *refs):
    outs = refs[3 * count :]
    place = 0
    for i in range(count):
        own_ref, x_ref, y_ref = refs[3 * i : 3 * i + 3]
        value = own_ref[...].astype(F32) + x_ref[...].astype(F32) + y_ref[...].astype(F32)
        value = value.astype(BF16)
        size = own_ref.shape[1]
        start = 0
        for out_ref in outs:
            first, last = max(place, start), min(place + size, start + out_ref.shape[1])
            if first < last:
                out_ref[:, first - start : last - start] = value[:, first - place : last - place]
            start += out_ref.shape[1]
        place += size


def total(chunks, sizes, after=()):
    ins = [value for own, *far in chunks for value in (*in_hbm(own), *far)]
    subs = ins[0].shape[0]
    step = 2
    return pl.pallas_call(
        drop_inputs(functools.partial(total_kernel, len(chunks)), len(ins), len(after)),
        grid=(subs // step,),
        in_specs=[pl.BlockSpec((step,) + v.shape[1:], lambda i: (i, 0, 0, 0)) for v in ins]
        + [ANYWHERE] * len(after),
        out_specs=[pl.BlockSpec((step, size, SUB, HB), lambda i: (i, 0, 0, 0)) for size in sizes],
        out_shape=[pltpu.HBM((subs, size, SUB, HB), BF16) for size in sizes],
        compiler_params=pltpu.CompilerParams(vmem_limit_bytes=SMALL),
        cost_estimate=FREE,
        name="total",
    )(*ins, *in_hbm(*after))


def butterfly_kernel(scale, x_ref, other_ref, sign_ref, out_ref):
    value = other_ref[...].astype(F32) + sign_ref[0] * x_ref[...].astype(F32)
    out_ref[...] = (value * scale).astype(BF16)


def butterfly(value, mask, scale, after):
    other = partner(value, "tensor", mask)
    sign = jnp.where((lax.axis_index("tensor") & mask) != 0, -1.0, 1.0).astype(F32).reshape(1)
    count = value.shape[0]
    step = min(4, count)
    spec = pl.BlockSpec((step,) + value.shape[1:], lambda i: (i, 0, 0, 0))
    return pl.pallas_call(
        drop_inputs(functools.partial(butterfly_kernel, scale), 3, len(after)),
        grid=(count // step,),
        in_specs=[spec, spec, pl.BlockSpec(memory_space=pltpu.SMEM)] + [ANYWHERE] * len(after),
        out_specs=spec,
        out_shape=pltpu.HBM(value.shape, BF16),
        compiler_params=pltpu.CompilerParams(vmem_limit_bytes=SMALL),
        cost_estimate=FREE,
        name="butterfly",
    )(*in_hbm(value), other, sign, *in_hbm(*after))


def general_shards(hidden, upstream, weight, scales, clip_mask, rot_block):
    groups = scales.shape[0]
    rows = hidden.shape[0]
    parts = lax.axis_size("dp")
    subs = rows // SUB
    index = lax.axis_index("dp")

    up = gather_upstream(upstream)
    (local,) = local_forward(hidden, rot_block, (groups,))
    rotated = lax.all_gather(mix_across(local), "dp", axis=0, tiled=False)
    order = index ^ jnp.arange(parts)
    rotated = rotated[order].reshape((parts * subs,) + local.shape[1:])
    per = 4 if groups % 4 == 0 else 1
    (full,) = unit_grads(up, weight, scales, 0, groups, per, (parts * subs,))
    full = full.reshape((parts,) + local.shape)[order]
    mixed = mix_across(lax.psum_scatter(full, "dp", scatter_dimension=0, tiled=False))
    grad_weight, grad_scales = weight_grads(
        [rotated], up, weight, scales, clip_mask, None, 0, groups, per
    )
    grad_hidden = local_backward([mixed], rot_block, (groups,))
    return grad_hidden, grad_weight, grad_scales


def shards(hidden, upstream, weight, scales, clip_mask, rot_block):
    groups = scales.shape[0]
    subs = hidden.shape[0] // SUB
    if lax.axis_size("dp") != 4 or lax.axis_size("tensor") != subs or groups % 8 != 4 or subs != 8:
        return general_shards(hidden, upstream, weight, scales, clip_mask, rot_block)
    per = 4
    units = groups // per
    sizes = (per * (units - units // 2), per * (units // 2))
    starts = (0, sizes[0])
    half = subs // 2
    counts = (subs, subs, subs, half, half)

    def scatter_first(parts_of):
        return partner(parts_of[3], "dp", 1), partner(parts_of[4], "dp", 2)

    def scatter_second(parts_of, received, after, cost=FREE):
        x_part, y_part = small_call(
            relay_kernel,
            "relay",
            [*in_hbm(parts_of[1], parts_of[2]), *received],
            [parts_of[1].shape] * 2,
            2,
            after,
            cost,
        )
        return x_part, partner(x_part, "dp", 1), partner(y_part, "dp", 2)

    def gather_first(value):
        return value, partner(value, "dp", 1), partner(value, "dp", 2)

    def gather_second(value, x_part, y_part):
        return value, x_part, y_part, partner(y_part[:half], "dp", 1), partner(
            x_part[half:], "dp", 2
        )

    up = gather_upstream(upstream)
    (local,) = local_forward(hidden, rot_block, (groups,))
    forth = exchange(local)
    unit0 = unit_grads(
        up, weight, scales, starts[0], sizes[0], per, counts, after=(local,), cost=SOME
    )
    first0 = scatter_first(unit0)
    unit1 = unit_grads(up, weight, scales, starts[1], sizes[1], per, counts, after=(unit0[0],))
    first1 = scatter_first(unit1)
    relayed0, *second0 = scatter_second(unit0, first0, after=(unit1[0],))
    turned = transform(forth, after=(relayed0,), cost=LONG)
    rotated = exchange(turned)
    relayed1, *second1 = scatter_second(unit1, first1, after=(turned,), cost=LONG)
    side, summed = total(
        ((unit0[0], *second0), (unit1[0], *second1)), (SIDE, groups - SIDE)
    )
    summed = gate(summed, after=(rotated,))
    back = exchange(summed)
    gathered0 = gather_second(*gather_first(rotated[:, : sizes[0]]))
    near = gather_first(gate(rotated, after=gathered0[1:3])[:, sizes[0] :])
    mixed = transform(back, cost=LONG)
    final = exchange(mixed)
    buffer, scale0 = weight_grads(
        gathered0,
        up,
        weight,
        scales,
        clip_mask,
        None,
        starts[0],
        sizes[0],
        per,
        after=(mixed,),
        cost=LONG,
    )
    gathered1 = gather_second(near[0], *(gate(value, after=(scale0,)) for value in near[1:]))
    side = gate(side, after=gathered0[1:3])
    side = butterfly(side, 4, 1.0, after=(scale0,))
    side = butterfly(side, 2, 1.0, after=())
    buffer, scale1 = weight_grads(
        gathered1, up, weight, scales, clip_mask, buffer, starts[1], sizes[1], per, after=(side,)
    )
    side = butterfly(side, 1, subs ** (-0.5), after=(scale1,))
    grad_hidden = local_backward([side, final], rot_block, (SIDE, groups - SIDE))
    return grad_hidden, buffer, jnp.concatenate([scale0, scale1], axis=0)


def solution(mesh):
    return jax.shard_map(
        shards,
        mesh=mesh,
        in_specs=(
            P("dp", "tensor"),
            P("dp", None),
            P("tensor", "dp"),
            P("tensor", "dp"),
            P("tensor", "dp"),
            P(),
        ),
        out_specs=(P("dp", "tensor"), P("tensor", "dp"), P("tensor", "dp")),
        check_vma=False,
    )
```

```python
import functools

import jax
import jax.numpy as jnp
from jax import lax
from jax.experimental import pallas as pl
from jax.experimental.pallas import tpu as pltpu
from jax.sharding import PartitionSpec as P

HB = 128
GROUP = 128
SUB = 16
ROWS = 8
SIDE = 8
F32 = jnp.float32
BF16 = jnp.bfloat16


def nt_dot(a, b):
    return lax.dot_general(a, b, (((1,), (1,)), ((), ())), preferred_element_type=F32)


def nn_dot(a, b):
    return lax.dot_general(a, b, (((1,), (0,)), ((), ())), preferred_element_type=F32)


def tn_dot(a, b):
    return lax.dot_general(a, b, (((0,), (0,)), ((), ())), preferred_element_type=F32)


def split2(value):
    high = value.astype(BF16)
    return high, (value - high.astype(F32)).astype(BF16)


def sign_matrix(size):
    both = lax.broadcasted_iota(jnp.int32, (size, size), 0) & lax.broadcasted_iota(
        jnp.int32, (size, size), 1
    )
    parity = jnp.zeros((size, size), jnp.int32)
    for bit in range(size.bit_length() - 1):
        parity = parity ^ ((both >> bit) & 1)
    return (1 - 2 * parity).astype(F32).astype(BF16)


def build_mixing(rot_ref, high_ref, low_ref, sign_ref, transposed):
    blocks = rot_ref.shape[0]
    size = blocks * ROWS
    row = lax.broadcasted_iota(jnp.int32, (size, blocks), 0)
    col = lax.broadcasted_iota(jnp.int32, (size, blocks), 1)
    pick = ((row >> 3) == col).astype(F32).astype(BF16)
    rows = lax.broadcasted_iota(jnp.int32, (size, size), 0)
    cols = lax.broadcasted_iota(jnp.int32, (size, size), 1)
    same = (rows & (ROWS - 1)) == (cols & (ROWS - 1))
    for part, out_ref in zip(split2(rot_ref[...]), (high_ref, low_ref)):
        spread = nt_dot(pick, part) if transposed else nn_dot(pick, part)
        full = nt_dot(spread.astype(BF16), pick)
        out_ref[...] = jnp.where(same, full, 0.0).astype(BF16)
    sign_ref[...] = sign_matrix(HB)


def mix_rows(tiles, high_ref, low_ref, sign_ref):
    blocks = len(tiles[0])
    stacked = jnp.concatenate([jnp.concatenate(one, axis=0).astype(BF16) for one in tiles], axis=1)
    mixed = nn_dot(high_ref[...], stacked) + nn_dot(low_ref[...], stacked)
    results = []
    for j in range(len(tiles)):
        part = nn_dot(mixed[:, j * HB : (j + 1) * HB].astype(BF16), sign_ref[...])
        results.append((part * HB ** (-0.5)).reshape(blocks, ROWS, HB))
    return results


def forward_kernel(sizes, x_ref, rot_ref, *refs):
    outs, (high_ref, low_ref, sign_ref) = refs[: len(sizes)], refs[len(sizes) :]
    blocks = rot_ref.shape[0]

    @pl.when(pl.program_id(0) == 0)
    def _():
        build_mixing(rot_ref, high_ref, low_ref, sign_ref, True)

    rows = x_ref.shape[0]
    wide = [x_ref[:, k * HB : (k + 1) * HB].astype(F32) for k in range(blocks)]
    tiles = [[one[j : j + ROWS] for one in wide] for j in range(0, rows, ROWS)]
    results = mix_rows(tiles, high_ref, low_ref, sign_ref)
    for j in range(rows // SUB):
        both = jnp.concatenate([results[2 * j], results[2 * j + 1]], axis=1).astype(BF16)
        start = 0
        for size, out_ref in zip(sizes, outs):
            out_ref[j] = both[start : start + size]
            start += size


def backward_kernel(sizes, *refs):
    ins, (rot_ref, out_ref, high_ref, low_ref, sign_ref) = refs[: len(sizes)], refs[len(sizes) :]
    blocks = rot_ref.shape[0]

    @pl.when(pl.program_id(0) == 0)
    def _():
        build_mixing(rot_ref, high_ref, low_ref, sign_ref, False)

    rows = out_ref.shape[0]
    tiles = []
    for j in range(rows // SUB):
        wide = [
            in_ref[j, c].astype(F32) for size, in_ref in zip(sizes, ins) for c in range(size)
        ]
        tiles += [[one[:ROWS] for one in wide], [one[ROWS:] for one in wide]]
    results = mix_rows(tiles, high_ref, low_ref, sign_ref)
    for j in range(rows // SUB):
        both = jnp.concatenate([results[2 * j], results[2 * j + 1]], axis=1).astype(BF16)
        for k in range(blocks):
            out_ref[j * SUB : (j + 1) * SUB, k * HB : (k + 1) * HB] = both[k]


def local_scratch(blocks):
    return [
        pltpu.VMEM((blocks * ROWS, blocks * ROWS), BF16),
        pltpu.VMEM((blocks * ROWS, blocks * ROWS), BF16),
        pltpu.VMEM((HB, HB), BF16),
    ]


FREE = pl.CostEstimate(flops=0, bytes_accessed=0, transcendentals=0)
LONG = pl.CostEstimate(flops=10**12, bytes_accessed=0, transcendentals=0)
SOME = pl.CostEstimate(flops=2_000_000_000, bytes_accessed=0, transcendentals=0)
MORE = pl.CostEstimate(flops=26_000_000_000, bytes_accessed=0, transcendentals=0)
SMALL = 12 << 20

ANYWHERE = pl.BlockSpec(memory_space=pl.ANY)


def in_hbm(*values):
    return [pltpu.with_memory_space_constraint(value, pltpu.HBM) for value in values]


def drop_inputs(kernel, start, count):
    def run(*refs):
        kernel(*refs[:start], *refs[start + count :])

    return run


def local_forward(hidden, rot_block, sizes):
    rows, width = hidden.shape
    blocks = width // HB
    parts = 2
    return pl.pallas_call(
        functools.partial(forward_kernel, sizes),
        grid=(rows // (SUB * parts),),
        in_specs=[
            pl.BlockSpec((SUB * parts, width), lambda i: (i, 0)),
            pl.BlockSpec((blocks, blocks), lambda i: (0, 0)),
        ],
        out_specs=[pl.BlockSpec((parts, size, SUB, HB), lambda i: (i, 0, 0, 0)) for size in sizes],
        out_shape=[pltpu.HBM((rows // SUB, size, SUB, HB), BF16) for size in sizes],
        scratch_shapes=local_scratch(blocks),
        compiler_params=pltpu.CompilerParams(vmem_limit_bytes=60 << 20),
        cost_estimate=FREE,
        name="local_forward",
    )(*in_hbm(hidden), rot_block)


def local_backward(mixed, rot_block, sizes, after=()):
    count = mixed[0].shape[0]
    rows = count * SUB
    blocks = rot_block.shape[0]
    parts = 2
    return pl.pallas_call(
        drop_inputs(functools.partial(backward_kernel, sizes), len(sizes) + 1, len(after)),
        grid=(count // parts,),
        in_specs=[pl.BlockSpec((parts, size, SUB, HB), lambda i: (i, 0, 0, 0)) for size in sizes]
        + [pl.BlockSpec((blocks, blocks), lambda i: (0, 0))]
        + [ANYWHERE] * len(after),
        out_specs=pl.BlockSpec((parts * SUB, blocks * HB), lambda i: (i, 0)),
        out_shape=pltpu.HBM((rows, blocks * HB), BF16),
        scratch_shapes=local_scratch(blocks),
        compiler_params=pltpu.CompilerParams(vmem_limit_bytes=60 << 20),
        cost_estimate=FREE,
        name="local_backward",
    )(*mixed, rot_block, *in_hbm(*after))


def units_kernel(first, per, up_ref, w_ref, s_ref, *refs):
    outs, (turned_ref, quant_ref) = refs[:-2], refs[-2:]
    base = first + pl.program_id(0) * per

    @pl.when(pl.program_id(0) == 0)
    def _():
        tile = 256
        for e in range(0, up_ref.shape[1], tile):
            turned_ref[e : e + tile, :] = up_ref[:, e : e + tile].T

    for g in range(per):
        rows = slice(g * GROUP, (g + 1) * GROUP)
        quant_ref[rows, :] = (w_ref[rows, :].astype(F32) * s_ref[pl.ds(base + g, 1), :]).astype(
            BF16
        )
    result = nn_dot(quant_ref[...], turned_ref[...]).astype(BF16).T
    token = 0
    for out_ref in outs:
        for q in range(out_ref.shape[0]):
            for g in range(per):
                out_ref[q, g] = result[token : token + SUB, g * GROUP : (g + 1) * GROUP]
            token += SUB


def unit_grads(up, weight, scales, first, size, per, counts, after=(), cost=FREE):
    tokens, cols = up.shape
    offset = first // per
    return pl.pallas_call(
        drop_inputs(functools.partial(units_kernel, first, per), 3, len(after)),
        grid=(size // per,),
        in_specs=[
            pl.BlockSpec((tokens, cols), lambda i: (0, 0)),
            pl.BlockSpec((per * GROUP, cols), lambda i: (offset + i, 0)),
            pl.BlockSpec(scales.shape, lambda i: (0, 0)),
        ]
        + [ANYWHERE] * len(after),
        out_specs=[pl.BlockSpec((count, per, SUB, HB), lambda i: (0, i, 0, 0)) for count in counts],
        out_shape=[pltpu.HBM((count, size, SUB, HB), BF16) for count in counts],
        scratch_shapes=[pltpu.VMEM((cols, tokens), BF16), pltpu.VMEM((per * GROUP, cols), BF16)],
        compiler_params=pltpu.CompilerParams(vmem_limit_bytes=26 << 20),
        cost_estimate=cost,
        name="unit_grads",
    )(up, *in_hbm(weight, scales), *in_hbm(*after))


def weights_kernel(first, per, pieces, *refs):
    rots = refs[:pieces]
    up_ref, w_ref, s_ref, m_ref = refs[pieces : pieces + 4]
    gw_ref, gs_ref = refs[-2:]
    step = pl.program_id(0)
    base = first + step * per
    left = jnp.concatenate(
        [
            jnp.concatenate(
                [rot_ref[q, g] for rot_ref in rots for q in range(rot_ref.shape[0])], axis=0
            )
            for g in range(per)
        ],
        axis=1,
    )
    cols = up_ref.shape[1]
    tile = min(256, cols)
    for e in range(cols // tile):
        span = slice(e * tile, (e + 1) * tile)
        grad = tn_dot(left, up_ref[:, span])
        for g in range(per):
            rows = slice(g * GROUP, (g + 1) * GROUP)
            piece = grad[rows]
            scale = s_ref[pl.ds(base + g, 1), span]
            kept = m_ref[pl.ds(base + g, 1), span].astype(F32) * scale
            gw_ref[rows, span] = (piece * kept).astype(BF16)
            gs_ref[pl.ds(step * per + g, 1), span] = jnp.sum(
                piece * w_ref[rows, span].astype(F32), axis=0, keepdims=True
            )


def weight_grads(rotated, up, weight, scales, mask, buffer, first, size, per, after=(), cost=FREE):
    tokens, cols = up.shape
    offset = first // per
    specs = [
        pl.BlockSpec((piece.shape[0], per, SUB, HB), lambda i: (0, i, 0, 0))
        for piece in rotated
    ] + [
        pl.BlockSpec((tokens, cols), lambda i: (0, 0)),
        pl.BlockSpec((per * GROUP, cols), lambda i: (offset + i, 0)),
        pl.BlockSpec(scales.shape, lambda i: (0, 0)),
        pl.BlockSpec(scales.shape, lambda i: (0, 0)),
    ]
    args = [*in_hbm(*rotated), up, *in_hbm(weight, scales, mask)]
    aliases = {}
    if buffer is not None:
        aliases = {len(args): 0}
        args.append(buffer)
        specs.append(ANYWHERE)
    return pl.pallas_call(
        functools.partial(weights_kernel, first, per, len(rotated)),
        grid=(size // per,),
        in_specs=specs + [ANYWHERE] * len(after),
        out_specs=[
            pl.BlockSpec((per * GROUP, cols), lambda i: (offset + i, 0)),
            pl.BlockSpec((size, cols), lambda i: (0, 0)),
        ],
        out_shape=[
            pltpu.HBM(weight.shape, BF16),
            jax.ShapeDtypeStruct((size, cols), F32),
        ],
        input_output_aliases=aliases,
        compiler_params=pltpu.CompilerParams(vmem_limit_bytes=26 << 20),
        cost_estimate=cost,
        name="weight_grads",
    )(*args, *in_hbm(*after))


def small_call(kernel, name, ins, outs, steps, after=(), cost=FREE):
    def spec(shape, dim):
        block = tuple(n // steps if d == dim else n for d, n in enumerate(shape))
        return pl.BlockSpec(
            block, lambda i: tuple(i if d == dim else 0 for d in range(len(shape)))
        )

    return pl.pallas_call(
        drop_inputs(kernel, len(ins), len(after)),
        grid=(steps,),
        in_specs=[spec(value.shape, 1) for value in ins] + [ANYWHERE] * len(after),
        out_specs=[spec(shape, 1) for shape in outs],
        out_shape=[pltpu.HBM(shape, BF16) for shape in outs],
        compiler_params=pltpu.CompilerParams(vmem_limit_bytes=SMALL),
        cost_estimate=cost,
        name=name,
    )(*ins, *in_hbm(*after))


def gate(value, after):
    return pl.pallas_call(
        drop_inputs(lambda x_ref, out_ref: None, 1, len(after)),
        in_specs=[ANYWHERE] * (1 + len(after)),
        out_specs=ANYWHERE,
        out_shape=pltpu.HBM(value.shape, value.dtype),
        input_output_aliases={0: 0},
        cost_estimate=FREE,
        name="gate",
    )(*in_hbm(value), *after)


def transform_kernel(x_ref, out_ref):
    count = x_ref.shape[0]
    values = [x_ref[t].astype(F32) for t in range(count)]
    stride = 1
    while stride < count:
        for t in range(count):
            if not t & stride:
                a, b = values[t], values[t | stride]
                values[t], values[t | stride] = a + b, a - b
        stride *= 2
    for t in range(count):
        out_ref[t] = (values[t] * count ** (-0.5)).astype(BF16)


def transform(value, after=(), cost=FREE):
    steps = 4 if value.shape[1] % 4 == 0 else 1
    return small_call(
        transform_kernel, "transform", [value], [value.shape], steps, after, cost
    )[0]


def exchange(value):
    return lax.all_to_all(value, "tensor", split_axis=0, concat_axis=0, tiled=True)


def partner(value, axis, mask):
    size = lax.axis_size(axis)
    return lax.ppermute(value, axis, [(i, i ^ mask) for i in range(size)])


def mix_across(value):
    size = lax.axis_size("tensor")
    index = lax.axis_index("tensor")
    masks = [1 << i for i in range(size.bit_length() - 1)]
    for place, mask in enumerate(masks):
        other = partner(value, "tensor", mask).astype(F32)
        sign = jnp.where((index & mask) != 0, -1.0, 1.0).astype(F32)
        total = other + sign * value.astype(F32)
        if place == len(masks) - 1:
            total = total * size ** (-0.5)
        value = total.astype(BF16)
    return value


def gather_upstream(upstream):
    rows, width = upstream.shape
    parts = lax.axis_size("dp")
    cols = width // parts
    half = rows // 2
    index = lax.axis_index("dp")
    core = lax.axis_index("tensor") & 1
    own = lax.dynamic_slice(upstream, (0, index * cols), (rows, cols))
    mine = [
        partner(
            lax.dynamic_slice(upstream, (core * half, (index ^ m) * cols), (half, cols)), "dp", m
        )
        for m in range(1, parts)
    ]
    mine = jnp.stack(mine)
    other = partner(mine, "tensor", 1)
    low = jnp.where(core == 0, mine, other)
    high = jnp.where(core == 0, other, mine)
    far = jnp.concatenate([low, high], axis=1).reshape((parts - 1) * rows, cols)
    return jnp.concatenate([own, far], axis=0)


def relay_kernel(x_ref, y_ref, a_ref, b_ref, x_out, y_out):
    half = a_ref.shape[0]
    x_out[:half] = x_ref[:half]
    x_out[half:] = (x_ref[half:].astype(F32) + b_ref[...].astype(F32)).astype(BF16)
    y_out[:half] = (y_ref[:half].astype(F32) + a_ref[...].astype(F32)).astype(BF16)
    y_out[half:] = y_ref[half:]


def total_kernel(count, *refs):
    outs = refs[3 * count :]
    place = 0
    for i in range(count):
        own_ref, x_ref, y_ref = refs[3 * i : 3 * i + 3]
        value = own_ref[...].astype(F32) + x_ref[...].astype(F32) + y_ref[...].astype(F32)
        value = value.astype(BF16)
        size = own_ref.shape[1]
        start = 0
        for out_ref in outs:
            first, last = max(place, start), min(place + size, start + out_ref.shape[1])
            if first < last:
                out_ref[:, first - start : last - start] = value[:, first - place : last - place]
            start += out_ref.shape[1]
        place += size


def total(chunks, sizes, after=()):
    ins = [value for own, *far in chunks for value in (*in_hbm(own), *far)]
    subs = ins[0].shape[0]
    step = 2
    return pl.pallas_call(
        drop_inputs(functools.partial(total_kernel, len(chunks)), len(ins), len(after)),
        grid=(subs // step,),
        in_specs=[pl.BlockSpec((step,) + v.shape[1:], lambda i: (i, 0, 0, 0)) for v in ins]
        + [ANYWHERE] * len(after),
        out_specs=[pl.BlockSpec((step, size, SUB, HB), lambda i: (i, 0, 0, 0)) for size in sizes],
        out_shape=[pltpu.HBM((subs, size, SUB, HB), BF16) for size in sizes],
        compiler_params=pltpu.CompilerParams(vmem_limit_bytes=SMALL),
        cost_estimate=FREE,
        name="total",
    )(*ins, *in_hbm(*after))


def butterfly_kernel(scale, x_ref, other_ref, sign_ref, out_ref):
    value = other_ref[...].astype(F32) + sign_ref[0] * x_ref[...].astype(F32)
    out_ref[...] = (value * scale).astype(BF16)


def butterfly(value, mask, scale, after):
    other = partner(value, "tensor", mask)
    sign = jnp.where((lax.axis_index("tensor") & mask) != 0, -1.0, 1.0).astype(F32).reshape(1)
    count = value.shape[0]
    step = min(4, count)
    spec = pl.BlockSpec((step,) + value.shape[1:], lambda i: (i, 0, 0, 0))
    return pl.pallas_call(
        drop_inputs(functools.partial(butterfly_kernel, scale), 3, len(after)),
        grid=(count // step,),
        in_specs=[spec, spec, pl.BlockSpec(memory_space=pltpu.SMEM)] + [ANYWHERE] * len(after),
        out_specs=spec,
        out_shape=pltpu.HBM(value.shape, BF16),
        compiler_params=pltpu.CompilerParams(vmem_limit_bytes=SMALL),
        cost_estimate=FREE,
        name="butterfly",
    )(*in_hbm(value), other, sign, *in_hbm(*after))


def general_shards(hidden, upstream, weight, scales, clip_mask, rot_block):
    groups = scales.shape[0]
    rows = hidden.shape[0]
    parts = lax.axis_size("dp")
    subs = rows // SUB
    index = lax.axis_index("dp")

    up = gather_upstream(upstream)
    (local,) = local_forward(hidden, rot_block, (groups,))
    rotated = lax.all_gather(mix_across(local), "dp", axis=0, tiled=False)
    order = index ^ jnp.arange(parts)
    rotated = rotated[order].reshape((parts * subs,) + local.shape[1:])
    per = 4 if groups % 4 == 0 else 1
    (full,) = unit_grads(up, weight, scales, 0, groups, per, (parts * subs,))
    full = full.reshape((parts,) + local.shape)[order]
    mixed = mix_across(lax.psum_scatter(full, "dp", scatter_dimension=0, tiled=False))
    grad_weight, grad_scales = weight_grads(
        [rotated], up, weight, scales, clip_mask, None, 0, groups, per
    )
    grad_hidden = local_backward([mixed], rot_block, (groups,))
    return grad_hidden, grad_weight, grad_scales


def shards(hidden, upstream, weight, scales, clip_mask, rot_block):
    groups = scales.shape[0]
    subs = hidden.shape[0] // SUB
    if lax.axis_size("dp") != 4 or lax.axis_size("tensor") != subs or groups % 8 != 4 or subs != 8:
        return general_shards(hidden, upstream, weight, scales, clip_mask, rot_block)
    per = 4
    units = groups // per
    sizes = (per * (units - units // 2), per * (units // 2))
    starts = (0, sizes[0])
    cuts = (per * (units - 2 * units // 5), per * (2 * units // 5))
    half = subs // 2
    counts = (subs, subs, subs, half, half)

    def scatter_first(parts_of):
        return partner(parts_of[3], "dp", 1), partner(parts_of[4], "dp", 2)

    def scatter_second(parts_of, received, after, cost=FREE):
        x_part, y_part = small_call(
            relay_kernel,
            "relay",
            [*in_hbm(parts_of[1], parts_of[2]), *received],
            [parts_of[1].shape] * 2,
            2,
            after,
            cost,
        )
        return x_part, partner(x_part, "dp", 1), partner(y_part, "dp", 2)

    def gather_first(value):
        return value, partner(value, "dp", 1), partner(value, "dp", 2)

    def gather_second(value, x_part, y_part):
        return value, x_part, y_part, partner(y_part[:half], "dp", 1), partner(
            x_part[half:], "dp", 2
        )

    up = gather_upstream(upstream)
    side, local = local_forward(hidden, rot_block, (SIDE, groups - SIDE))
    forth = exchange(local)
    unit0 = unit_grads(
        up, weight, scales, starts[0], sizes[0], per, counts, after=(local,), cost=SOME
    )
    first0 = scatter_first(unit0)
    unit1 = unit_grads(up, weight, scales, starts[1], sizes[1], per, counts, after=(unit0[0],))
    first1 = scatter_first(unit1)
    relayed0, *second0 = scatter_second(unit0, first0, after=(unit1[0],))
    turned = transform(forth, after=(relayed0,), cost=LONG)
    rotated = exchange(turned)
    side = butterfly(gate(side, after=(relayed0,)), 4, 1.0, after=(turned,))
    relayed1, *second1 = scatter_second(unit1, first1, after=(side,), cost=LONG)
    side = butterfly(side, 2, 1.0, after=(relayed1,))
    side = butterfly(side, 1, subs ** (-0.5), after=())
    (summed,) = total(((unit0[0], *second0), (unit1[0], *second1)), (groups,), after=(side,))
    summed = gate(summed, after=(rotated,))
    back = exchange(summed)
    low = jnp.concatenate([side, rotated[:, : cuts[0] - SIDE]], axis=1)
    gathered0 = gather_second(*gather_first(low))
    mixed = transform(back, cost=LONG)
    final = exchange(mixed)
    near = gather_first(gate(rotated, after=(*gathered0[3:5], mixed))[:, cuts[0] - SIDE :])
    buffer, scale0 = weight_grads(
        gathered0,
        up,
        weight,
        scales,
        clip_mask,
        None,
        0,
        cuts[0],
        per,
        after=(mixed,),
        cost=MORE,
    )
    gathered1 = gather_second(near[0], *(gate(value, after=(scale0,)) for value in near[1:]))
    buffer, scale1 = weight_grads(
        gathered1, up, weight, scales, clip_mask, buffer, cuts[0], cuts[1], per
    )
    grad_hidden = local_backward([final], rot_block, (groups,), after=(scale1,))
    return grad_hidden, buffer, jnp.concatenate([scale0, scale1], axis=0)


def solution(mesh):
    return jax.shard_map(
        shards,
        mesh=mesh,
        in_specs=(
            P("dp", "tensor"),
            P("dp", None),
            P("tensor", "dp"),
            P("tensor", "dp"),
            P("tensor", "dp"),
            P(),
        ),
        out_specs=(P("dp", "tensor"), P("tensor", "dp"), P("tensor", "dp")),
        check_vma=False,
    )
```

```python
import functools

import jax
import jax.numpy as jnp
from jax import lax
from jax.experimental import pallas as pl
from jax.experimental.pallas import tpu as pltpu
from jax.sharding import PartitionSpec as P

HB = 128
GROUP = 128
SUB = 16
ROWS = 8
F32 = jnp.float32
BF16 = jnp.bfloat16


def nt_dot(a, b):
    return lax.dot_general(a, b, (((1,), (1,)), ((), ())), preferred_element_type=F32)


def nn_dot(a, b):
    return lax.dot_general(a, b, (((1,), (0,)), ((), ())), preferred_element_type=F32)


def split2(value):
    high = value.astype(BF16)
    return high, (value - high.astype(F32)).astype(BF16)


def sign_matrix(size):
    both = lax.broadcasted_iota(jnp.int32, (size, size), 0) & lax.broadcasted_iota(
        jnp.int32, (size, size), 1
    )
    parity = jnp.zeros((size, size), jnp.int32)
    for bit in range(size.bit_length() - 1):
        parity = parity ^ ((both >> bit) & 1)
    return (1 - 2 * parity).astype(F32).astype(BF16)


def build_mixing(rot_ref, high_ref, low_ref, sign_ref, transposed):
    blocks = rot_ref.shape[0]
    size = blocks * ROWS
    row = lax.broadcasted_iota(jnp.int32, (size, blocks), 0)
    col = lax.broadcasted_iota(jnp.int32, (size, blocks), 1)
    pick = ((row >> 3) == col).astype(F32).astype(BF16)
    rows = lax.broadcasted_iota(jnp.int32, (size, size), 0)
    cols = lax.broadcasted_iota(jnp.int32, (size, size), 1)
    same = (rows & (ROWS - 1)) == (cols & (ROWS - 1))
    for part, out_ref in zip(split2(rot_ref[...]), (high_ref, low_ref)):
        spread = nt_dot(pick, part) if transposed else nn_dot(pick, part)
        full = nt_dot(spread.astype(BF16), pick)
        out_ref[...] = jnp.where(same, full, 0.0).astype(BF16)
    sign_ref[...] = sign_matrix(HB)


def mix_rows(tiles, high_ref, low_ref, sign_ref):
    blocks = len(tiles[0])
    stacked = jnp.concatenate([jnp.concatenate(one, axis=0).astype(BF16) for one in tiles], axis=1)
    mixed = nn_dot(high_ref[...], stacked) + nn_dot(low_ref[...], stacked)
    results = []
    for j in range(len(tiles)):
        part = nn_dot(mixed[:, j * HB : (j + 1) * HB].astype(BF16), sign_ref[...])
        results.append((part * HB ** (-0.5)).reshape(blocks, ROWS, HB))
    return results


def forward_kernel(sizes, x_ref, rot_ref, *refs):
    outs, (high_ref, low_ref, sign_ref) = refs[: len(sizes)], refs[len(sizes) :]
    blocks = rot_ref.shape[0]

    @pl.when(pl.program_id(0) == 0)
    def _():
        build_mixing(rot_ref, high_ref, low_ref, sign_ref, True)

    rows = x_ref.shape[0]
    wide = [x_ref[:, k * HB : (k + 1) * HB].astype(F32) for k in range(blocks)]
    tiles = [[one[j : j + ROWS] for one in wide] for j in range(0, rows, ROWS)]
    results = mix_rows(tiles, high_ref, low_ref, sign_ref)
    for j in range(rows // SUB):
        both = jnp.concatenate([results[2 * j], results[2 * j + 1]], axis=1).astype(BF16)
        start = 0
        for size, out_ref in zip(sizes, outs):
            out_ref[j] = both[start : start + size]
            start += size


def backward_kernel(sizes, *refs):
    ins, (high_ref, low_ref, sign_ref, out_ref) = refs[: len(sizes)], refs[len(sizes) :]
    blocks = sum(sizes)
    rows = out_ref.shape[0]
    tiles = []
    for j in range(rows // SUB):
        wide = [
            in_ref[j, c].astype(F32) for size, in_ref in zip(sizes, ins) for c in range(size)
        ]
        tiles += [[one[:ROWS] for one in wide], [one[ROWS:] for one in wide]]
    results = mix_rows(tiles, high_ref, low_ref, sign_ref)
    for j in range(rows // SUB):
        both = jnp.concatenate([results[2 * j], results[2 * j + 1]], axis=1).astype(BF16)
        for k in range(blocks):
            out_ref[j * SUB : (j + 1) * SUB, k * HB : (k + 1) * HB] = both[k]


def local_scratch(blocks):
    return [
        pltpu.VMEM((blocks * ROWS, blocks * ROWS), BF16),
        pltpu.VMEM((blocks * ROWS, blocks * ROWS), BF16),
        pltpu.VMEM((HB, HB), BF16),
    ]


FREE = pl.CostEstimate(flops=0, bytes_accessed=0, transcendentals=0)
LONG = pl.CostEstimate(flops=10**12, bytes_accessed=0, transcendentals=0)
SOME = pl.CostEstimate(flops=5_000_000_000, bytes_accessed=0, transcendentals=0)
SMALL = 16 << 20

ANYWHERE = pl.BlockSpec(memory_space=pl.ANY)


def in_hbm(*values):
    return [pltpu.with_memory_space_constraint(value, pltpu.HBM) for value in values]


def drop_inputs(kernel, start, count):
    def run(*refs):
        kernel(*refs[:start], *refs[start + count :])

    return run


def local_forward(hidden, rot_block, sizes):
    rows, width = hidden.shape
    blocks = width // HB
    parts = 2
    return pl.pallas_call(
        functools.partial(forward_kernel, sizes),
        grid=(rows // (SUB * parts),),
        in_specs=[
            pl.BlockSpec((SUB * parts, width), lambda i: (i, 0)),
            pl.BlockSpec((blocks, blocks), lambda i: (0, 0)),
        ],
        out_specs=[pl.BlockSpec((parts, size, SUB, HB), lambda i: (i, 0, 0, 0)) for size in sizes],
        out_shape=[pltpu.HBM((rows // SUB, size, SUB, HB), BF16) for size in sizes],
        scratch_shapes=local_scratch(blocks),
        compiler_params=pltpu.CompilerParams(vmem_limit_bytes=60 << 20),
        cost_estimate=FREE,
        name="local_forward",
    )(*in_hbm(hidden), rot_block)


def backward_matrices(rot_block, after=()):
    size = rot_block.shape[0] * ROWS
    shapes = [(size, size), (size, size), (HB, HB)]
    return pl.pallas_call(
        drop_inputs(
            lambda rot_ref, *refs: build_mixing(rot_ref, *refs, False), 1, len(after)
        ),
        in_specs=[pl.BlockSpec(memory_space=pltpu.VMEM)] + [ANYWHERE] * len(after),
        out_specs=[pl.BlockSpec(memory_space=pltpu.VMEM)] * 3,
        out_shape=[pltpu.HBM(shape, BF16) for shape in shapes],
        compiler_params=pltpu.CompilerParams(vmem_limit_bytes=SMALL),
        cost_estimate=FREE,
        name="backward_matrices",
    )(rot_block, *after)


def local_backward(mixed, matrices, sizes, after=()):
    count = mixed[0].shape[0]
    rows = count * SUB
    blocks = sum(sizes)
    parts = 2
    return pl.pallas_call(
        drop_inputs(functools.partial(backward_kernel, sizes), len(sizes) + 3, len(after)),
        grid=(count // parts,),
        in_specs=[pl.BlockSpec((parts, size, SUB, HB), lambda i: (i, 0, 0, 0)) for size in sizes]
        + [pl.BlockSpec(value.shape, lambda i: (0, 0)) for value in matrices]
        + [ANYWHERE] * len(after),
        out_specs=pl.BlockSpec((parts * SUB, blocks * HB), lambda i: (i, 0)),
        out_shape=pltpu.HBM((rows, blocks * HB), BF16),
        compiler_params=pltpu.CompilerParams(vmem_limit_bytes=24 << 20),
        cost_estimate=FREE,
        name="local_backward",
    )(*mixed, *in_hbm(*matrices, *after))


def units_kernel(first, per, up_ref, w_ref, s_ref, *refs):
    outs, quant_ref = refs[:-1], refs[-1]
    base = first + pl.program_id(0) * per
    for g in range(per):
        rows = slice(g * GROUP, (g + 1) * GROUP)
        quant_ref[rows, :] = (w_ref[rows, :].astype(F32) * s_ref[pl.ds(base + g, 1), :]).astype(
            BF16
        )
    result = nt_dot(up_ref[...], quant_ref[...]).astype(BF16)
    token = 0
    for out_ref in outs:
        for q in range(out_ref.shape[0]):
            for g in range(per):
                out_ref[q, g] = result[token : token + SUB, g * GROUP : (g + 1) * GROUP]
            token += SUB


def unit_grads(up, weight, scales, first, size, per, counts, after=(), cost=FREE):
    tokens, cols = up.shape
    offset = first // per
    return pl.pallas_call(
        drop_inputs(functools.partial(units_kernel, first, per), 3, len(after)),
        grid=(size // per,),
        in_specs=[
            pl.BlockSpec((tokens, cols), lambda i: (0, 0)),
            pl.BlockSpec((per * GROUP, cols), lambda i: (offset + i, 0)),
            pl.BlockSpec(scales.shape, lambda i: (0, 0)),
        ]
        + [ANYWHERE] * len(after),
        out_specs=[pl.BlockSpec((count, per, SUB, HB), lambda i: (0, i, 0, 0)) for count in counts],
        out_shape=[pltpu.HBM((count, size, SUB, HB), BF16) for count in counts],
        scratch_shapes=[pltpu.VMEM((per * GROUP, cols), BF16)],
        compiler_params=pltpu.CompilerParams(vmem_limit_bytes=26 << 20),
        cost_estimate=cost,
        name="unit_grads",
    )(up, *in_hbm(weight, scales), *in_hbm(*after))


def weights_kernel(first, per, pieces, *refs):
    rots = refs[:pieces]
    up_ref, w_ref, s_ref, m_ref = refs[pieces : pieces + 4]
    gw_ref, gs_ref = refs[-2:]
    step = pl.program_id(0)
    base = first + step * per
    left = jnp.concatenate(
        [
            jnp.concatenate(
                [rot_ref[q, g] for rot_ref in rots for q in range(rot_ref.shape[0])], axis=0
            )
            for g in range(per)
        ],
        axis=1,
    ).T
    cols = up_ref.shape[1]
    tile = min(256, cols)
    for e in range(cols // tile):
        span = slice(e * tile, (e + 1) * tile)
        grad = nn_dot(left, up_ref[:, span])
        for g in range(per):
            rows = slice(g * GROUP, (g + 1) * GROUP)
            piece = grad[rows]
            scale = s_ref[pl.ds(base + g, 1), span]
            kept = m_ref[pl.ds(base + g, 1), span].astype(F32) * scale
            gw_ref[rows, span] = (piece * kept).astype(BF16)
            gs_ref[pl.ds(step * per + g, 1), span] = jnp.sum(
                piece * w_ref[rows, span].astype(F32), axis=0, keepdims=True
            )


def weight_grads(rotated, up, weight, scales, mask, buffer, first, size, per, after=()):
    tokens, cols = up.shape
    offset = first // per
    specs = [
        pl.BlockSpec(
            (piece.shape[0], per, SUB, HB),
            functools.partial(lambda place, i: (0, place + i, 0, 0), place),
        )
        for piece in rotated
        for place in ((0 if piece.shape[1] == size else offset),)
    ] + [
        pl.BlockSpec((tokens, cols), lambda i: (0, 0)),
        pl.BlockSpec((per * GROUP, cols), lambda i: (offset + i, 0)),
        pl.BlockSpec(scales.shape, lambda i: (0, 0)),
        pl.BlockSpec(scales.shape, lambda i: (0, 0)),
    ]
    args = [*rotated, up, *in_hbm(weight, scales, mask)]
    aliases = {}
    if buffer is not None:
        aliases = {len(args): 0}
        args.append(buffer)
        specs.append(ANYWHERE)
    return pl.pallas_call(
        functools.partial(weights_kernel, first, per, len(rotated)),
        grid=(size // per,),
        in_specs=specs + [ANYWHERE] * len(after),
        out_specs=[
            pl.BlockSpec((per * GROUP, cols), lambda i: (offset + i, 0)),
            pl.BlockSpec((size, cols), lambda i: (0, 0)),
        ],
        out_shape=[
            pltpu.HBM(weight.shape, BF16),
            jax.ShapeDtypeStruct((size, cols), F32),
        ],
        input_output_aliases=aliases,
        compiler_params=pltpu.CompilerParams(vmem_limit_bytes=26 << 20),
        cost_estimate=LONG,
        name="weight_grads",
    )(*args, *in_hbm(*after))


def small_call(kernel, name, ins, outs, steps, after=(), cost=FREE):
    def spec(shape, dim):
        block = tuple(n // steps if d == dim else n for d, n in enumerate(shape))
        return pl.BlockSpec(
            block, lambda i: tuple(i if d == dim else 0 for d in range(len(shape)))
        )

    return pl.pallas_call(
        drop_inputs(kernel, len(ins), len(after)),
        grid=(steps,),
        in_specs=[spec(value.shape, 1) for value in ins] + [ANYWHERE] * len(after),
        out_specs=[spec(shape, 1) for shape in outs],
        out_shape=[pltpu.HBM(shape, BF16) for shape in outs],
        compiler_params=pltpu.CompilerParams(vmem_limit_bytes=SMALL),
        cost_estimate=cost,
        name=name,
    )(*ins, *in_hbm(*after))


def cut_kernel(start, x_ref, y_ref, x_out, y_out):
    size = x_out.shape[1]
    x_out[...] = x_ref[:, start : start + size]
    y_out[...] = y_ref[:, start : start + size]


def cut(x_part, y_part, start, size, after):
    subs, groups = x_part.shape[:2]
    half = subs // 2
    out = pl.BlockSpec((2, size, SUB, HB), lambda i: (i, 0, 0, 0))
    return pl.pallas_call(
        drop_inputs(functools.partial(cut_kernel, start), 2, len(after)),
        grid=(half // 2,),
        in_specs=[
            pl.BlockSpec((2, groups, SUB, HB), lambda i: (half // 2 + i, 0, 0, 0)),
            pl.BlockSpec((2, groups, SUB, HB), lambda i: (i, 0, 0, 0)),
        ]
        + [ANYWHERE] * len(after),
        out_specs=[out, out],
        out_shape=[pltpu.HBM((half, size, SUB, HB), BF16)] * 2,
        compiler_params=pltpu.CompilerParams(vmem_limit_bytes=SMALL),
        cost_estimate=FREE,
        name="cut",
    )(x_part, y_part, *in_hbm(*after))


def gate(value, after):
    return pl.pallas_call(
        drop_inputs(lambda x_ref, out_ref: None, 1, len(after)),
        in_specs=[ANYWHERE] * (1 + len(after)),
        out_specs=ANYWHERE,
        out_shape=pltpu.HBM(value.shape, value.dtype),
        input_output_aliases={0: 0},
        cost_estimate=FREE,
        name="gate",
    )(*in_hbm(value, *after))


def transform_kernel(x_ref, out_ref):
    count = x_ref.shape[0]
    values = [x_ref[t].astype(F32) for t in range(count)]
    stride = 1
    while stride < count:
        for t in range(count):
            if not t & stride:
                a, b = values[t], values[t | stride]
                values[t], values[t | stride] = a + b, a - b
        stride *= 2
    for t in range(count):
        out_ref[t] = (values[t] * count ** (-0.5)).astype(BF16)


def transform(value, after=(), cost=FREE):
    steps = 4 if value.shape[1] % 4 == 0 else 1
    return small_call(
        transform_kernel, "transform", [value], [value.shape], steps, after, cost
    )[0]


def exchange(value):
    return lax.all_to_all(value, "tensor", split_axis=0, concat_axis=0, tiled=True)


def partner(value, axis, mask):
    size = lax.axis_size(axis)
    return lax.ppermute(value, axis, [(i, i ^ mask) for i in range(size)])


def mix_across(value):
    size = lax.axis_size("tensor")
    index = lax.axis_index("tensor")
    masks = [1 << i for i in range(size.bit_length() - 1)]
    for place, mask in enumerate(masks):
        other = partner(value, "tensor", mask).astype(F32)
        sign = jnp.where((index & mask) != 0, -1.0, 1.0).astype(F32)
        total = other + sign * value.astype(F32)
        if place == len(masks) - 1:
            total = total * size ** (-0.5)
        value = total.astype(BF16)
    return value


def gather_upstream(upstream):
    rows, width = upstream.shape
    parts = lax.axis_size("dp")
    cols = width // parts
    half = rows // 2
    index = lax.axis_index("dp")
    core = lax.axis_index("tensor") & 1
    own = lax.dynamic_slice(upstream, (0, index * cols), (rows, cols))
    mine = [
        partner(
            lax.dynamic_slice(upstream, (core * half, (index ^ m) * cols), (half, cols)), "dp", m
        )
        for m in range(1, parts)
    ]
    mine = jnp.stack(mine)
    other = partner(mine, "tensor", 1)
    low = jnp.where(core == 0, mine, other)
    high = jnp.where(core == 0, other, mine)
    far = jnp.concatenate([low, high], axis=1).reshape((parts - 1) * rows, cols)
    return jnp.concatenate([own, far], axis=0)


def relay_kernel(x_ref, y_ref, a_ref, b_ref, x_out, y_out):
    half = a_ref.shape[0]
    x_out[:half] = x_ref[:half]
    x_out[half:] = (x_ref[half:].astype(F32) + b_ref[...].astype(F32)).astype(BF16)
    y_out[:half] = (y_ref[:half].astype(F32) + a_ref[...].astype(F32)).astype(BF16)
    y_out[half:] = y_ref[half:]


def total_kernel(count, *refs):
    out_ref = refs[-1]
    start = 0
    for i in range(count):
        own_ref, x_ref, y_ref = refs[3 * i : 3 * i + 3]
        size = own_ref.shape[1]
        out_ref[:, start : start + size] = (
            own_ref[...].astype(F32) + x_ref[...].astype(F32) + y_ref[...].astype(F32)
        ).astype(BF16)
        start += size


def total(chunks, after=()):
    ins = [value for own, *far in chunks for value in (*in_hbm(own), *far)]
    subs = ins[0].shape[0]
    groups = sum(chunk[0].shape[1] for chunk in chunks)
    step = 2
    return pl.pallas_call(
        drop_inputs(functools.partial(total_kernel, len(chunks)), len(ins), len(after)),
        grid=(subs // step,),
        in_specs=[pl.BlockSpec((step,) + v.shape[1:], lambda i: (i, 0, 0, 0)) for v in ins]
        + [ANYWHERE] * len(after),
        out_specs=pl.BlockSpec((step, groups, SUB, HB), lambda i: (i, 0, 0, 0)),
        out_shape=pltpu.HBM((subs, groups, SUB, HB), BF16),
        compiler_params=pltpu.CompilerParams(vmem_limit_bytes=SMALL),
        cost_estimate=FREE,
        name="total",
    )(*ins, *in_hbm(*after))


def general_shards(hidden, upstream, weight, scales, clip_mask, rot_block):
    groups = scales.shape[0]
    rows = hidden.shape[0]
    parts = lax.axis_size("dp")
    subs = rows // SUB
    index = lax.axis_index("dp")

    up = gather_upstream(upstream)
    (local,) = local_forward(hidden, rot_block, (groups,))
    rotated = lax.all_gather(mix_across(local), "dp", axis=0, tiled=False)
    order = index ^ jnp.arange(parts)
    rotated = rotated[order].reshape((parts * subs,) + local.shape[1:])
    per = 4 if groups % 4 == 0 else 1
    (full,) = unit_grads(up, weight, scales, 0, groups, per, (parts * subs,))
    full = full.reshape((parts,) + local.shape)[order]
    mixed = mix_across(lax.psum_scatter(full, "dp", scatter_dimension=0, tiled=False))
    grad_weight, grad_scales = weight_grads(
        [rotated], up, weight, scales, clip_mask, None, 0, groups, per
    )
    grad_hidden = local_backward([mixed], backward_matrices(rot_block), (groups,))
    return grad_hidden, grad_weight, grad_scales


def shards(hidden, upstream, weight, scales, clip_mask, rot_block):
    groups = scales.shape[0]
    subs = hidden.shape[0] // SUB
    if lax.axis_size("dp") != 4 or lax.axis_size("tensor") != subs or groups % 8 != 4:
        return general_shards(hidden, upstream, weight, scales, clip_mask, rot_block)
    per = 4
    units = groups // per
    sizes = (per * (units - units // 2), per * (units // 2))
    starts = (0, sizes[0])
    half = subs // 2
    counts = (subs, subs, subs, half, half)

    def scatter_first(parts_of):
        return partner(parts_of[3], "dp", 1), partner(parts_of[4], "dp", 2)

    def scatter_second(parts_of, received, after, cost=FREE):
        x_part, y_part = small_call(
            relay_kernel,
            "relay",
            [*in_hbm(parts_of[1], parts_of[2]), *received],
            [parts_of[1].shape] * 2,
            2,
            after,
            cost,
        )
        return x_part, partner(x_part, "dp", 1), partner(y_part, "dp", 2)

    def gather_rest(near, chunk, after):
        x_half, y_half = cut(near[1], near[2], starts[chunk], sizes[chunk], after)
        return *near, partner(y_half, "dp", 1), partner(x_half, "dp", 2)

    up = gather_upstream(upstream)
    (local,) = local_forward(hidden, rot_block, (groups,))
    forth = exchange(local)
    unit0 = unit_grads(
        up, weight, scales, starts[0], sizes[0], per, counts, after=(local,), cost=SOME
    )
    first0 = scatter_first(unit0)
    unit1 = unit_grads(up, weight, scales, starts[1], sizes[1], per, counts, after=(unit0[0],))
    first1 = scatter_first(unit1)
    relayed0, *second0 = scatter_second(unit0, first0, after=(unit1[0],))
    turned = transform(forth, after=(relayed0,), cost=LONG)
    rotated = exchange(turned)
    relayed1, *second1 = scatter_second(unit1, first1, after=(turned,), cost=LONG)
    summed = gate(total(((unit0[0], *second0), (unit1[0], *second1))), after=(rotated,))
    matrices = backward_matrices(rot_block, after=(relayed1,))
    back = exchange(summed)
    near = (rotated, partner(rotated, "dp", 1), partner(rotated, "dp", 2))
    gathered0 = gather_rest(near, 0, ())
    mixed = transform(back, cost=LONG)
    final = exchange(mixed)
    gathered1 = gather_rest(near, 1, (mixed,))
    buffer, scale0 = weight_grads(
        gathered0, up, weight, scales, clip_mask, None, starts[0], sizes[0], per, after=(mixed,)
    )
    buffer, scale1 = weight_grads(
        gathered1, up, weight, scales, clip_mask, buffer, starts[1], sizes[1], per
    )
    grad_hidden = local_backward([final], matrices, (groups,), after=(scale1,))
    return grad_hidden, buffer, jnp.concatenate([scale0, scale1], axis=0)


def solution(mesh):
    return jax.shard_map(
        shards,
        mesh=mesh,
        in_specs=(
            P("dp", "tensor"),
            P("dp", None),
            P("tensor", "dp"),
            P("tensor", "dp"),
            P("tensor", "dp"),
            P(),
        ),
        out_specs=(P("dp", "tensor"), P("tensor", "dp"), P("tensor", "dp")),
        check_vma=False,
    )
```

```python
import functools

import jax
import jax.numpy as jnp
from jax import lax
from jax.experimental import pallas as pl
from jax.experimental.pallas import tpu as pltpu
from jax.sharding import PartitionSpec as P

HB = 128
GROUP = 128
SUB = 16
ROWS = 8
F32 = jnp.float32
BF16 = jnp.bfloat16


def nt_dot(a, b):
    return lax.dot_general(a, b, (((1,), (1,)), ((), ())), preferred_element_type=F32)


def nn_dot(a, b):
    return lax.dot_general(a, b, (((1,), (0,)), ((), ())), preferred_element_type=F32)


def split2(value):
    high = value.astype(BF16)
    return high, (value - high.astype(F32)).astype(BF16)


def sign_matrix(size):
    both = lax.broadcasted_iota(jnp.int32, (size, size), 0) & lax.broadcasted_iota(
        jnp.int32, (size, size), 1
    )
    parity = jnp.zeros((size, size), jnp.int32)
    for bit in range(size.bit_length() - 1):
        parity = parity ^ ((both >> bit) & 1)
    return (1 - 2 * parity).astype(F32).astype(BF16)


def build_mixing(rot_ref, mix_ref, sign_ref, transposed):
    blocks = rot_ref.shape[0]
    size = blocks * ROWS
    row = lax.broadcasted_iota(jnp.int32, (size, blocks), 0)
    col = lax.broadcasted_iota(jnp.int32, (size, blocks), 1)
    pick = ((row >> 3) == col).astype(F32).astype(BF16)
    rows = lax.broadcasted_iota(jnp.int32, (size, size), 0)
    cols = lax.broadcasted_iota(jnp.int32, (size, size), 1)
    same = (rows & (ROWS - 1)) == (cols & (ROWS - 1))
    spread = [
        nt_dot(pick, part) if transposed else nn_dot(pick, part) for part in split2(rot_ref[...])
    ]
    for half, value in enumerate(spread):
        full = nt_dot(value.astype(BF16), pick)
        mix_ref[half * size : (half + 1) * size, :] = jnp.where(same, full, 0.0).astype(BF16)
    sign_ref[...] = sign_matrix(HB)


def mix_rows(tiles, mix_ref, sign_ref):
    blocks = len(tiles[0])
    size = blocks * ROWS
    stacked = jnp.concatenate([jnp.concatenate(one, axis=0).astype(BF16) for one in tiles], axis=1)
    halves = nn_dot(mix_ref[...], stacked)
    mixed = (halves[:size] + halves[size:]).astype(BF16)
    results = []
    for j in range(len(tiles)):
        part = nn_dot(mixed[:, j * HB : (j + 1) * HB], sign_ref[...])
        results.append((part * HB ** (-0.5)).reshape(blocks, ROWS, HB))
    return results


def forward_kernel(sizes, x_ref, rot_ref, *refs):
    outs, (mix_ref, sign_ref) = refs[: len(sizes)], refs[len(sizes) :]
    blocks = rot_ref.shape[0]

    @pl.when(pl.program_id(0) == 0)
    def _():
        build_mixing(rot_ref, mix_ref, sign_ref, True)

    rows = x_ref.shape[0]
    wide = [x_ref[:, k * HB : (k + 1) * HB].astype(F32) for k in range(blocks)]
    tiles = [[one[j : j + ROWS] for one in wide] for j in range(0, rows, ROWS)]
    results = mix_rows(tiles, mix_ref, sign_ref)
    for j in range(rows // SUB):
        both = jnp.concatenate([results[2 * j], results[2 * j + 1]], axis=1).astype(BF16)
        start = 0
        for size, out_ref in zip(sizes, outs):
            out_ref[j] = both[start : start + size]
            start += size


def backward_kernel(sizes, *refs):
    ins, (mix_ref, sign_ref, out_ref) = refs[: len(sizes)], refs[len(sizes) :]
    blocks = sum(sizes)
    rows = out_ref.shape[0]
    tiles = []
    for j in range(rows // SUB):
        wide = [
            in_ref[j, c].astype(F32) for size, in_ref in zip(sizes, ins) for c in range(size)
        ]
        tiles += [[one[:ROWS] for one in wide], [one[ROWS:] for one in wide]]
    results = mix_rows(tiles, mix_ref, sign_ref)
    for j in range(rows // SUB):
        both = jnp.concatenate([results[2 * j], results[2 * j + 1]], axis=1).astype(BF16)
        for k in range(blocks):
            out_ref[j * SUB : (j + 1) * SUB, k * HB : (k + 1) * HB] = both[k]


def local_scratch(blocks):
    return [
        pltpu.VMEM((2 * blocks * ROWS, blocks * ROWS), BF16),
        pltpu.VMEM((HB, HB), BF16),
    ]


FREE = pl.CostEstimate(flops=0, bytes_accessed=0, transcendentals=0)
LONG = pl.CostEstimate(flops=10**12, bytes_accessed=0, transcendentals=0)
SOME = pl.CostEstimate(flops=5_000_000_000, bytes_accessed=0, transcendentals=0)
SMALL = 16 << 20

ANYWHERE = pl.BlockSpec(memory_space=pl.ANY)


def in_hbm(*values):
    return [pltpu.with_memory_space_constraint(value, pltpu.HBM) for value in values]


def drop_inputs(kernel, start, count):
    def run(*refs):
        kernel(*refs[:start], *refs[start + count :])

    return run


def local_forward(hidden, rot_block, sizes):
    rows, width = hidden.shape
    blocks = width // HB
    parts = 2
    return pl.pallas_call(
        functools.partial(forward_kernel, sizes),
        grid=(rows // (SUB * parts),),
        in_specs=[
            pl.BlockSpec((SUB * parts, width), lambda i: (i, 0)),
            pl.BlockSpec((blocks, blocks), lambda i: (0, 0)),
        ],
        out_specs=[pl.BlockSpec((parts, size, SUB, HB), lambda i: (i, 0, 0, 0)) for size in sizes],
        out_shape=[pltpu.HBM((rows // SUB, size, SUB, HB), BF16) for size in sizes],
        scratch_shapes=local_scratch(blocks),
        compiler_params=pltpu.CompilerParams(vmem_limit_bytes=60 << 20),
        cost_estimate=FREE,
        name="local_forward",
    )(*in_hbm(hidden), rot_block)


def backward_matrices(rot_block, after=()):
    size = rot_block.shape[0] * ROWS
    shapes = [(2 * size, size), (HB, HB)]
    return pl.pallas_call(
        drop_inputs(
            lambda rot_ref, *refs: build_mixing(rot_ref, *refs, False), 1, len(after)
        ),
        in_specs=[pl.BlockSpec(memory_space=pltpu.VMEM)] + [ANYWHERE] * len(after),
        out_specs=[pl.BlockSpec(memory_space=pltpu.VMEM)] * 2,
        out_shape=[pltpu.HBM(shape, BF16) for shape in shapes],
        compiler_params=pltpu.CompilerParams(vmem_limit_bytes=SMALL),
        cost_estimate=FREE,
        name="backward_matrices",
    )(rot_block, *after)


def local_backward(mixed, matrices, sizes, after=()):
    count = mixed[0].shape[0]
    rows = count * SUB
    blocks = sum(sizes)
    parts = 2
    return pl.pallas_call(
        drop_inputs(functools.partial(backward_kernel, sizes), len(sizes) + 2, len(after)),
        grid=(count // parts,),
        in_specs=[pl.BlockSpec((parts, size, SUB, HB), lambda i: (i, 0, 0, 0)) for size in sizes]
        + [pl.BlockSpec(value.shape, lambda i: (0, 0)) for value in matrices]
        + [ANYWHERE] * len(after),
        out_specs=pl.BlockSpec((parts * SUB, blocks * HB), lambda i: (i, 0)),
        out_shape=pltpu.HBM((rows, blocks * HB), BF16),
        compiler_params=pltpu.CompilerParams(vmem_limit_bytes=24 << 20),
        cost_estimate=FREE,
        name="local_backward",
    )(*mixed, *in_hbm(*matrices, *after))


def weight_spec(first, per, cols):
    return pl.BlockSpec(
        (pl.Element(per * GROUP), pl.Element(cols)), lambda i: ((first + i * per) * GROUP, 0)
    )


def units_kernel(first, per, up_ref, w_ref, s_ref, *refs):
    outs, (turned_ref, quant_ref) = refs[:-2], refs[-2:]
    base = first + pl.program_id(0) * per

    @pl.when(pl.program_id(0) == 0)
    def _():
        tile = 256
        for e in range(0, up_ref.shape[1], tile):
            turned_ref[e : e + tile, :] = up_ref[:, e : e + tile].T

    for g in range(per):
        rows = slice(g * GROUP, (g + 1) * GROUP)
        quant_ref[rows, :] = (w_ref[rows, :].astype(F32) * s_ref[pl.ds(base + g, 1), :]).astype(
            BF16
        )
    result = nn_dot(quant_ref[...], turned_ref[...]).astype(BF16)
    for g in range(per):
        turned = result[g * GROUP : (g + 1) * GROUP, :].T
        token = 0
        for out_ref in outs:
            for q in range(out_ref.shape[0]):
                out_ref[q, g] = turned[token : token + SUB, :]
                token += SUB


def unit_grads(up, weight, scales, first, size, per, counts, after=(), cost=FREE):
    tokens, cols = up.shape
    return pl.pallas_call(
        drop_inputs(functools.partial(units_kernel, first, per), 3, len(after)),
        grid=(size // per,),
        in_specs=[
            pl.BlockSpec((tokens, cols), lambda i: (0, 0)),
            weight_spec(first, per, cols),
            pl.BlockSpec(scales.shape, lambda i: (0, 0)),
        ]
        + [ANYWHERE] * len(after),
        out_specs=[pl.BlockSpec((count, per, SUB, HB), lambda i: (0, i, 0, 0)) for count in counts],
        out_shape=[pltpu.HBM((count, size, SUB, HB), BF16) for count in counts],
        scratch_shapes=[pltpu.VMEM((cols, tokens), BF16), pltpu.VMEM((per * GROUP, cols), BF16)],
        compiler_params=pltpu.CompilerParams(vmem_limit_bytes=40 << 20),
        cost_estimate=cost,
        name="unit_grads",
    )(up, *in_hbm(weight, scales), *in_hbm(*after))


def weights_kernel(first, per, pieces, *refs):
    rots = refs[:pieces]
    up_ref, w_ref, s_ref, m_ref = refs[pieces : pieces + 4]
    gw_ref, gs_ref = refs[-2:]
    step = pl.program_id(0)
    base = first + step * per
    left = jnp.concatenate(
        [
            jnp.concatenate(
                [rot_ref[q, g] for rot_ref in rots for q in range(rot_ref.shape[0])], axis=0
            )
            for g in range(per)
        ],
        axis=1,
    ).T
    cols = up_ref.shape[1]
    tile = min(256, cols)
    for e in range(cols // tile):
        span = slice(e * tile, (e + 1) * tile)
        grad = nn_dot(left, up_ref[:, span])
        for g in range(per):
            rows = slice(g * GROUP, (g + 1) * GROUP)
            piece = grad[rows]
            scale = s_ref[pl.ds(base + g, 1), span]
            kept = m_ref[pl.ds(base + g, 1), span].astype(F32) * scale
            gw_ref[rows, span] = (piece * kept).astype(BF16)
            gs_ref[pl.ds(step * per + g, 1), span] = jnp.sum(
                piece * w_ref[rows, span].astype(F32), axis=0, keepdims=True
            )


def weight_grads(rotated, up, weight, scales, mask, buffer, first, size, per, after=()):
    tokens, cols = up.shape
    specs = [
        pl.BlockSpec(
            tuple(map(pl.Element, (piece.shape[0], per, SUB, HB))),
            functools.partial(lambda place, i: (0, place + i * per, 0, 0), place),
        )
        for piece in rotated
        for place in ((0 if piece.shape[1] == size else first),)
    ] + [
        pl.BlockSpec((tokens, cols), lambda i: (0, 0)),
        weight_spec(first, per, cols),
        pl.BlockSpec(scales.shape, lambda i: (0, 0)),
        pl.BlockSpec(scales.shape, lambda i: (0, 0)),
    ]
    args = [*rotated, up, *in_hbm(weight, scales, mask)]
    aliases = {}
    if buffer is not None:
        aliases = {len(args): 0}
        args.append(buffer)
        specs.append(ANYWHERE)
    return pl.pallas_call(
        functools.partial(weights_kernel, first, per, len(rotated)),
        grid=(size // per,),
        in_specs=specs + [ANYWHERE] * len(after),
        out_specs=[
            weight_spec(first, per, cols),
            pl.BlockSpec((size, cols), lambda i: (0, 0)),
        ],
        out_shape=[
            pltpu.HBM(weight.shape, BF16),
            jax.ShapeDtypeStruct((size, cols), F32),
        ],
        input_output_aliases=aliases,
        compiler_params=pltpu.CompilerParams(vmem_limit_bytes=40 << 20),
        cost_estimate=LONG,
        name="weight_grads",
    )(*args, *in_hbm(*after))


def small_call(kernel, name, ins, outs, steps, after=(), cost=FREE):
    def spec(shape, dim):
        block = tuple(n // steps if d == dim else n for d, n in enumerate(shape))
        return pl.BlockSpec(
            block, lambda i: tuple(i if d == dim else 0 for d in range(len(shape)))
        )

    return pl.pallas_call(
        drop_inputs(kernel, len(ins), len(after)),
        grid=(steps,),
        in_specs=[spec(value.shape, 1) for value in ins] + [ANYWHERE] * len(after),
        out_specs=[spec(shape, 1) for shape in outs],
        out_shape=[pltpu.HBM(shape, BF16) for shape in outs],
        compiler_params=pltpu.CompilerParams(vmem_limit_bytes=SMALL),
        cost_estimate=cost,
        name=name,
    )(*ins, *in_hbm(*after))


def cut_kernel(start, x_ref, y_ref, x_out, y_out):
    size = x_out.shape[1]
    x_out[...] = x_ref[:, start : start + size]
    y_out[...] = y_ref[:, start : start + size]


def cut(x_part, y_part, start, size, after):
    subs, groups = x_part.shape[:2]
    half = subs // 2
    out = pl.BlockSpec((2, size, SUB, HB), lambda i: (i, 0, 0, 0))
    return pl.pallas_call(
        drop_inputs(functools.partial(cut_kernel, start), 2, len(after)),
        grid=(half // 2,),
        in_specs=[
            pl.BlockSpec((2, groups, SUB, HB), lambda i: (half // 2 + i, 0, 0, 0)),
            pl.BlockSpec((2, groups, SUB, HB), lambda i: (i, 0, 0, 0)),
        ]
        + [ANYWHERE] * len(after),
        out_specs=[out, out],
        out_shape=[pltpu.HBM((half, size, SUB, HB), BF16)] * 2,
        compiler_params=pltpu.CompilerParams(vmem_limit_bytes=SMALL),
        cost_estimate=FREE,
        name="cut",
    )(x_part, y_part, *in_hbm(*after))


def gate(value, after):
    return pl.pallas_call(
        drop_inputs(lambda x_ref, out_ref: None, 1, len(after)),
        in_specs=[ANYWHERE] * (1 + len(after)),
        out_specs=ANYWHERE,
        out_shape=pltpu.HBM(value.shape, value.dtype),
        input_output_aliases={0: 0},
        cost_estimate=FREE,
        name="gate",
    )(*in_hbm(value, *after))


def transform_kernel(x_ref, out_ref):
    count = x_ref.shape[0]
    values = [x_ref[t].astype(F32) for t in range(count)]
    stride = 1
    while stride < count:
        for t in range(count):
            if not t & stride:
                a, b = values[t], values[t | stride]
                values[t], values[t | stride] = a + b, a - b
        stride *= 2
    for t in range(count):
        out_ref[t] = (values[t] * count ** (-0.5)).astype(BF16)


def transform(value, after=(), cost=FREE):
    steps = 4 if value.shape[1] % 4 == 0 else 1
    return small_call(
        transform_kernel, "transform", [value], [value.shape], steps, after, cost
    )[0]


def exchange(value):
    return lax.all_to_all(value, "tensor", split_axis=0, concat_axis=0, tiled=True)


def partner(value, axis, mask):
    size = lax.axis_size(axis)
    return lax.ppermute(value, axis, [(i, i ^ mask) for i in range(size)])


def mix_across(value):
    size = lax.axis_size("tensor")
    index = lax.axis_index("tensor")
    masks = [1 << i for i in range(size.bit_length() - 1)]
    for place, mask in enumerate(masks):
        other = partner(value, "tensor", mask).astype(F32)
        sign = jnp.where((index & mask) != 0, -1.0, 1.0).astype(F32)
        total = other + sign * value.astype(F32)
        if place == len(masks) - 1:
            total = total * size ** (-0.5)
        value = total.astype(BF16)
    return value


def gather_upstream(upstream):
    rows, width = upstream.shape
    parts = lax.axis_size("dp")
    cols = width // parts
    half = rows // 2
    index = lax.axis_index("dp")
    core = lax.axis_index("tensor") & 1
    own = lax.dynamic_slice(upstream, (0, index * cols), (rows, cols))
    mine = [
        partner(
            lax.dynamic_slice(upstream, (core * half, (index ^ m) * cols), (half, cols)), "dp", m
        )
        for m in range(1, parts)
    ]
    mine = jnp.stack(mine)
    other = partner(mine, "tensor", 1)
    low = jnp.where(core == 0, mine, other)
    high = jnp.where(core == 0, other, mine)
    far = jnp.concatenate([low, high], axis=1).reshape((parts - 1) * rows, cols)
    return jnp.concatenate([own, far], axis=0)


def relay_kernel(x_ref, y_ref, a_ref, b_ref, x_out, y_out):
    half = a_ref.shape[0]
    x_out[:half] = x_ref[:half]
    x_out[half:] = (x_ref[half:].astype(F32) + b_ref[...].astype(F32)).astype(BF16)
    y_out[:half] = (y_ref[:half].astype(F32) + a_ref[...].astype(F32)).astype(BF16)
    y_out[half:] = y_ref[half:]


def total_kernel(count, *refs):
    out_ref = refs[-1]
    start = 0
    for i in range(count):
        own_ref, x_ref, y_ref = refs[3 * i : 3 * i + 3]
        size = own_ref.shape[1]
        out_ref[:, start : start + size] = (
            own_ref[...].astype(F32) + x_ref[...].astype(F32) + y_ref[...].astype(F32)
        ).astype(BF16)
        start += size


def total(chunks, after=()):
    ins = [value for own, *far in chunks for value in (*in_hbm(own), *far)]
    subs = ins[0].shape[0]
    groups = sum(chunk[0].shape[1] for chunk in chunks)
    step = 2
    return pl.pallas_call(
        drop_inputs(functools.partial(total_kernel, len(chunks)), len(ins), len(after)),
        grid=(subs // step,),
        in_specs=[pl.BlockSpec((step,) + v.shape[1:], lambda i: (i, 0, 0, 0)) for v in ins]
        + [ANYWHERE] * len(after),
        out_specs=pl.BlockSpec((step, groups, SUB, HB), lambda i: (i, 0, 0, 0)),
        out_shape=pltpu.HBM((subs, groups, SUB, HB), BF16),
        compiler_params=pltpu.CompilerParams(vmem_limit_bytes=SMALL),
        cost_estimate=FREE,
        name="total",
    )(*ins, *in_hbm(*after))


def general_shards(hidden, upstream, weight, scales, clip_mask, rot_block):
    groups = scales.shape[0]
    rows = hidden.shape[0]
    parts = lax.axis_size("dp")
    subs = rows // SUB
    index = lax.axis_index("dp")

    up = gather_upstream(upstream)
    (local,) = local_forward(hidden, rot_block, (groups,))
    rotated = lax.all_gather(mix_across(local), "dp", axis=0, tiled=False)
    order = index ^ jnp.arange(parts)
    rotated = rotated[order].reshape((parts * subs,) + local.shape[1:])
    per = 4 if groups % 4 == 0 else 1
    (full,) = unit_grads(up, weight, scales, 0, groups, per, (parts * subs,))
    full = full.reshape((parts,) + local.shape)[order]
    mixed = mix_across(lax.psum_scatter(full, "dp", scatter_dimension=0, tiled=False))
    grad_weight, grad_scales = weight_grads(
        [rotated], up, weight, scales, clip_mask, None, 0, groups, per
    )
    grad_hidden = local_backward([mixed], backward_matrices(rot_block), (groups,))
    return grad_hidden, grad_weight, grad_scales


def shards(hidden, upstream, weight, scales, clip_mask, rot_block):
    groups = scales.shape[0]
    subs = hidden.shape[0] // SUB
    if lax.axis_size("dp") != 4 or lax.axis_size("tensor") != subs or groups % 8 != 4:
        return general_shards(hidden, upstream, weight, scales, clip_mask, rot_block)
    per = 4
    units = groups // per
    sizes = (per * (units - units // 2), per * (units // 2))
    starts = (0, sizes[0])
    half = subs // 2
    counts = (subs, subs, subs, half, half)

    def scatter_first(parts_of):
        return partner(parts_of[3], "dp", 1), partner(parts_of[4], "dp", 2)

    def scatter_second(parts_of, received, after, cost=FREE):
        x_part, y_part = small_call(
            relay_kernel,
            "relay",
            [*in_hbm(parts_of[1], parts_of[2]), *received],
            [parts_of[1].shape] * 2,
            2,
            after,
            cost,
        )
        return x_part, partner(x_part, "dp", 1), partner(y_part, "dp", 2)

    def gather_rest(near, chunk, after):
        x_half, y_half = cut(near[1], near[2], starts[chunk], sizes[chunk], after)
        return *near, partner(y_half, "dp", 1), partner(x_half, "dp", 2)

    up = gather_upstream(upstream)
    (local,) = local_forward(hidden, rot_block, (groups,))
    forth = exchange(local)
    pers = [size // 4 for size in sizes]
    unit0 = unit_grads(
        up, weight, scales, starts[0], sizes[0], pers[0], counts, after=(local,), cost=SOME
    )
    first0 = scatter_first(unit0)
    unit1 = unit_grads(
        up, weight, scales, starts[1], sizes[1], pers[1], counts, after=(unit0[0],)
    )
    first1 = scatter_first(unit1)
    relayed0, *second0 = scatter_second(unit0, first0, after=(unit1[0],))
    turned = transform(forth, after=(relayed0,), cost=LONG)
    rotated = exchange(turned)
    relayed1, *second1 = scatter_second(unit1, first1, after=(turned,), cost=LONG)
    summed = gate(total(((unit0[0], *second0), (unit1[0], *second1))), after=(rotated,))
    matrices = backward_matrices(rot_block, after=(relayed1,))
    back = exchange(summed)
    near = (rotated, partner(rotated, "dp", 1), partner(rotated, "dp", 2))
    gathered0 = gather_rest(near, 0, ())
    mixed = transform(back, cost=LONG)
    final = exchange(mixed)
    gathered1 = gather_rest(near, 1, (mixed,))
    buffer, scale0 = weight_grads(
        gathered0, up, weight, scales, clip_mask, None, starts[0], sizes[0], pers[0], after=(mixed,)
    )
    buffer, scale1 = weight_grads(
        gathered1, up, weight, scales, clip_mask, buffer, starts[1], sizes[1], pers[1]
    )
    grad_hidden = local_backward([final], matrices, (groups,), after=(scale1,))
    return grad_hidden, buffer, jnp.concatenate([scale0, scale1], axis=0)


def solution(mesh):
    return jax.shard_map(
        shards,
        mesh=mesh,
        in_specs=(
            P("dp", "tensor"),
            P("dp", None),
            P("tensor", "dp"),
            P("tensor", "dp"),
            P("tensor", "dp"),
            P(),
        ),
        out_specs=(P("dp", "tensor"), P("tensor", "dp"), P("tensor", "dp")),
        check_vma=False,
    )
```

```python
import functools

import jax
import jax.numpy as jnp
from jax import lax
from jax.experimental import pallas as pl
from jax.experimental.pallas import tpu as pltpu
from jax.sharding import PartitionSpec as P

HB = 128
GROUP = 128
SUB = 16
ROWS = 8
F32 = jnp.float32
BF16 = jnp.bfloat16


def nt_dot(a, b):
    return lax.dot_general(a, b, (((1,), (1,)), ((), ())), preferred_element_type=F32)


def nn_dot(a, b):
    return lax.dot_general(a, b, (((1,), (0,)), ((), ())), preferred_element_type=F32)


def split2(value):
    high = value.astype(BF16)
    return high, (value - high.astype(F32)).astype(BF16)


def sign_matrix():
    size = 2 * HB
    row = lax.broadcasted_iota(jnp.int32, (size, size), 0)
    col = lax.broadcasted_iota(jnp.int32, (size, size), 1)
    both = row & col
    parity = jnp.zeros((size, size), jnp.int32)
    for bit in range(HB.bit_length() - 1):
        parity = parity ^ ((both >> bit) & 1)
    return jnp.where((row ^ col) < HB, (1 - 2 * parity).astype(F32), 0.0).astype(BF16)


def build_mixing(rot_ref, mix_ref, sign_ref, transposed):
    blocks = rot_ref.shape[0]
    size = blocks * ROWS
    row = lax.broadcasted_iota(jnp.int32, (size, blocks), 0)
    col = lax.broadcasted_iota(jnp.int32, (size, blocks), 1)
    pick = ((row >> 3) == col).astype(F32).astype(BF16)
    rows = lax.broadcasted_iota(jnp.int32, (size, size), 0)
    cols = lax.broadcasted_iota(jnp.int32, (size, size), 1)
    same = (rows & (ROWS - 1)) == (cols & (ROWS - 1))
    spread = [
        nt_dot(pick, part) if transposed else nn_dot(pick, part) for part in split2(rot_ref[...])
    ]
    for half, value in enumerate(spread):
        full = nt_dot(value.astype(BF16), pick)
        mix_ref[half * size : (half + 1) * size, :] = jnp.where(same, full, 0.0).astype(BF16)
    sign_ref[...] = sign_matrix()


def mix_rows(tiles, mix_ref, sign_ref):
    blocks = len(tiles[0])
    size = blocks * ROWS
    stacked = jnp.concatenate([jnp.concatenate(one, axis=0).astype(BF16) for one in tiles], axis=1)
    halves = nn_dot(mix_ref[...], stacked)
    mixed = (halves[:size] + halves[size:]).astype(BF16)
    results = []
    for j in range(0, len(tiles), 2):
        part = nn_dot(mixed[:, j * HB : (j + 2) * HB], sign_ref[...]) * HB ** (-0.5)
        results += [part[:, :HB].reshape(blocks, ROWS, HB), part[:, HB:].reshape(blocks, ROWS, HB)]
    return results


def forward_kernel(sizes, x_ref, rot_ref, *refs):
    outs, (mix_ref, sign_ref) = refs[: len(sizes)], refs[len(sizes) :]
    blocks = rot_ref.shape[0]

    @pl.when(pl.program_id(0) == 0)
    def _():
        build_mixing(rot_ref, mix_ref, sign_ref, True)

    rows = x_ref.shape[0]
    wide = [x_ref[:, k * HB : (k + 1) * HB].astype(F32) for k in range(blocks)]
    tiles = [[one[j : j + ROWS] for one in wide] for j in range(0, rows, ROWS)]
    results = mix_rows(tiles, mix_ref, sign_ref)
    for j in range(rows // SUB):
        both = jnp.concatenate([results[2 * j], results[2 * j + 1]], axis=1).astype(BF16)
        start = 0
        for size, out_ref in zip(sizes, outs):
            out_ref[j] = both[start : start + size]
            start += size


def backward_kernel(sizes, *refs):
    ins, (mix_ref, sign_ref, out_ref) = refs[: len(sizes)], refs[len(sizes) :]
    blocks = sum(sizes)
    rows = out_ref.shape[0]
    tiles = []
    start = pl.program_id(0) * (rows // SUB)
    for j in range(rows // SUB):
        wide = [
            in_ref[start + j, c].astype(F32)
            for size, in_ref in zip(sizes, ins)
            for c in range(size)
        ]
        tiles += [[one[:ROWS] for one in wide], [one[ROWS:] for one in wide]]
    results = mix_rows(tiles, mix_ref, sign_ref)
    for j in range(rows // SUB):
        both = jnp.concatenate([results[2 * j], results[2 * j + 1]], axis=1).astype(BF16)
        for k in range(blocks):
            out_ref[j * SUB : (j + 1) * SUB, k * HB : (k + 1) * HB] = both[k]


def local_scratch(blocks):
    return [
        pltpu.VMEM((2 * blocks * ROWS, blocks * ROWS), BF16),
        pltpu.VMEM((2 * HB, 2 * HB), BF16),
    ]


FREE = pl.CostEstimate(flops=0, bytes_accessed=0, transcendentals=0)
LONG = pl.CostEstimate(flops=10**12, bytes_accessed=0, transcendentals=0)
SOME = pl.CostEstimate(flops=5_000_000_000, bytes_accessed=0, transcendentals=0)
SMALL = 16 << 20

ANYWHERE = pl.BlockSpec(memory_space=pl.ANY)


def in_hbm(*values):
    return [pltpu.with_memory_space_constraint(value, pltpu.HBM) for value in values]


def drop_inputs(kernel, start, count):
    def run(*refs):
        kernel(*refs[:start], *refs[start + count :])

    return run


def local_forward(hidden, rot_block, sizes):
    rows, width = hidden.shape
    blocks = width // HB
    parts = 2
    return pl.pallas_call(
        functools.partial(forward_kernel, sizes),
        grid=(rows // (SUB * parts),),
        in_specs=[
            pl.BlockSpec((SUB * parts, width), lambda i: (i, 0)),
            pl.BlockSpec((blocks, blocks), lambda i: (0, 0)),
        ],
        out_specs=[pl.BlockSpec((parts, size, SUB, HB), lambda i: (i, 0, 0, 0)) for size in sizes],
        out_shape=[pltpu.HBM((rows // SUB, size, SUB, HB), BF16) for size in sizes],
        scratch_shapes=local_scratch(blocks),
        compiler_params=pltpu.CompilerParams(vmem_limit_bytes=60 << 20),
        cost_estimate=FREE,
        name="local_forward",
    )(*in_hbm(hidden), rot_block)


def backward_matrices(rot_block, after=()):
    size = rot_block.shape[0] * ROWS
    shapes = [(2 * size, size), (2 * HB, 2 * HB)]
    return pl.pallas_call(
        drop_inputs(
            lambda rot_ref, *refs: build_mixing(rot_ref, *refs, False), 1, len(after)
        ),
        in_specs=[pl.BlockSpec(memory_space=pltpu.VMEM)] + [ANYWHERE] * len(after),
        out_specs=[pl.BlockSpec(memory_space=pltpu.VMEM)] * 2,
        out_shape=[pltpu.HBM(shape, BF16) for shape in shapes],
        compiler_params=pltpu.CompilerParams(vmem_limit_bytes=SMALL),
        cost_estimate=FREE,
        name="backward_matrices",
    )(rot_block, *after)


def local_backward(mixed, matrices, sizes, after=()):
    count = mixed[0].shape[0]
    rows = count * SUB
    blocks = sum(sizes)
    parts = 2
    return pl.pallas_call(
        drop_inputs(functools.partial(backward_kernel, sizes), len(sizes) + 2, len(after)),
        grid=(count // parts,),
        in_specs=[pl.BlockSpec(memory_space=pltpu.VMEM)] * len(sizes)
        + [pl.BlockSpec(value.shape, lambda i: (0, 0)) for value in matrices]
        + [ANYWHERE] * len(after),
        out_specs=pl.BlockSpec((parts * SUB, blocks * HB), lambda i: (i, 0)),
        out_shape=pltpu.HBM((rows, blocks * HB), BF16),
        compiler_params=pltpu.CompilerParams(vmem_limit_bytes=24 << 20),
        cost_estimate=FREE,
        name="local_backward",
    )(*mixed, *in_hbm(*matrices, *after))


def weight_spec(first, per, cols):
    return pl.BlockSpec(
        (pl.Element(per * GROUP), pl.Element(cols)), lambda i: ((first + i * per) * GROUP, 0)
    )


def units_kernel(first, per, up_ref, w_ref, s_ref, *refs):
    outs, (turned_ref, quant_ref) = refs[:-2], refs[-2:]
    base = first + pl.program_id(0) * per

    @pl.when(pl.program_id(0) == 0)
    def _():
        tile = 256
        for e in range(0, up_ref.shape[1], tile):
            turned_ref[e : e + tile, :] = up_ref[:, e : e + tile].T

    for g in range(per):
        rows = slice(g * GROUP, (g + 1) * GROUP)
        quant_ref[rows, :] = (w_ref[rows, :].astype(F32) * s_ref[pl.ds(base + g, 1), :]).astype(
            BF16
        )
    result = nn_dot(quant_ref[...], turned_ref[...]).astype(BF16)
    for g in range(per):
        turned = result[g * GROUP : (g + 1) * GROUP, :].T
        token = 0
        for out_ref in outs:
            for q in range(out_ref.shape[0]):
                out_ref[q, g] = turned[token : token + SUB, :]
                token += SUB


def unit_grads(up, weight, scales, first, size, per, counts, after=(), cost=FREE):
    tokens, cols = up.shape
    return pl.pallas_call(
        drop_inputs(functools.partial(units_kernel, first, per), 3, len(after)),
        grid=(size // per,),
        in_specs=[
            pl.BlockSpec((tokens, cols), lambda i: (0, 0)),
            weight_spec(first, per, cols),
            pl.BlockSpec(scales.shape, lambda i: (0, 0)),
        ]
        + [ANYWHERE] * len(after),
        out_specs=[pl.BlockSpec((count, per, SUB, HB), lambda i: (0, i, 0, 0)) for count in counts],
        out_shape=[pltpu.HBM((count, size, SUB, HB), BF16) for count in counts],
        scratch_shapes=[pltpu.VMEM((cols, tokens), BF16), pltpu.VMEM((per * GROUP, cols), BF16)],
        compiler_params=pltpu.CompilerParams(vmem_limit_bytes=40 << 20),
        cost_estimate=cost,
        name="unit_grads",
    )(up, *in_hbm(weight, scales), *in_hbm(*after))


def weights_kernel(first, per, pieces, *refs):
    rots = refs[:pieces]
    up_ref, w_ref, s_ref, m_ref = refs[pieces : pieces + 4]
    gw_ref, gs_ref = refs[-2:]
    step = pl.program_id(0)
    base = first + step * per
    left = jnp.concatenate(
        [
            jnp.concatenate(
                [rot_ref[q, g] for rot_ref in rots for q in range(rot_ref.shape[0])], axis=0
            )
            for g in range(per)
        ],
        axis=1,
    ).T
    cols = up_ref.shape[1]
    tile = min(256, cols)
    for e in range(cols // tile):
        span = slice(e * tile, (e + 1) * tile)
        grad = nn_dot(left, up_ref[:, span])
        for g in range(per):
            rows = slice(g * GROUP, (g + 1) * GROUP)
            piece = grad[rows]
            scale = s_ref[pl.ds(base + g, 1), span]
            kept = m_ref[pl.ds(base + g, 1), span].astype(F32) * scale
            gw_ref[rows, span] = (piece * kept).astype(BF16)
            gs_ref[pl.ds(step * per + g, 1), span] = jnp.sum(
                piece * w_ref[rows, span].astype(F32), axis=0, keepdims=True
            )


def weight_grads(rotated, up, weight, scales, mask, buffer, first, size, per, after=()):
    tokens, cols = up.shape
    specs = [
        pl.BlockSpec(
            tuple(map(pl.Element, (piece.shape[0], per, SUB, HB))),
            functools.partial(lambda place, i: (0, place + i * per, 0, 0), place),
        )
        for piece in rotated
        for place in ((0 if piece.shape[1] == size else first),)
    ] + [
        pl.BlockSpec((tokens, cols), lambda i: (0, 0)),
        weight_spec(first, per, cols),
        pl.BlockSpec(scales.shape, lambda i: (0, 0)),
        pl.BlockSpec(scales.shape, lambda i: (0, 0)),
    ]
    args = [*rotated, up, *in_hbm(weight, scales, mask)]
    aliases = {}
    if buffer is not None:
        aliases = {len(args): 0}
        args.append(buffer)
        specs.append(ANYWHERE)
    return pl.pallas_call(
        functools.partial(weights_kernel, first, per, len(rotated)),
        grid=(size // per,),
        in_specs=specs + [ANYWHERE] * len(after),
        out_specs=[
            weight_spec(first, per, cols),
            pl.BlockSpec((size, cols), lambda i: (0, 0)),
        ],
        out_shape=[
            pltpu.HBM(weight.shape, BF16),
            jax.ShapeDtypeStruct((size, cols), F32),
        ],
        input_output_aliases=aliases,
        compiler_params=pltpu.CompilerParams(vmem_limit_bytes=40 << 20),
        cost_estimate=LONG,
        name="weight_grads",
    )(*args, *in_hbm(*after))


def small_call(kernel, name, ins, outs, steps, after=(), cost=FREE):
    def spec(shape, dim):
        block = tuple(n // steps if d == dim else n for d, n in enumerate(shape))
        return pl.BlockSpec(
            block, lambda i: tuple(i if d == dim else 0 for d in range(len(shape)))
        )

    return pl.pallas_call(
        drop_inputs(kernel, len(ins), len(after)),
        grid=(steps,),
        in_specs=[spec(value.shape, 1) for value in ins] + [ANYWHERE] * len(after),
        out_specs=[spec(shape, 1) for shape in outs],
        out_shape=[pltpu.HBM(shape, BF16) for shape in outs],
        compiler_params=pltpu.CompilerParams(vmem_limit_bytes=SMALL),
        cost_estimate=cost,
        name=name,
    )(*ins, *in_hbm(*after))


def cut_kernel(start, x_ref, y_ref, x_out, y_out):
    size = x_out.shape[1]
    x_out[...] = x_ref[:, start : start + size]
    y_out[...] = y_ref[:, start : start + size]


def cut(x_part, y_part, start, size, after):
    subs, groups = x_part.shape[:2]
    half = subs // 2
    out = pl.BlockSpec((2, size, SUB, HB), lambda i: (i, 0, 0, 0))
    return pl.pallas_call(
        drop_inputs(functools.partial(cut_kernel, start), 2, len(after)),
        grid=(half // 2,),
        in_specs=[
            pl.BlockSpec((2, groups, SUB, HB), lambda i: (half // 2 + i, 0, 0, 0)),
            pl.BlockSpec((2, groups, SUB, HB), lambda i: (i, 0, 0, 0)),
        ]
        + [ANYWHERE] * len(after),
        out_specs=[out, out],
        out_shape=[pltpu.HBM((half, size, SUB, HB), BF16)] * 2,
        compiler_params=pltpu.CompilerParams(vmem_limit_bytes=SMALL),
        cost_estimate=FREE,
        name="cut",
    )(x_part, y_part, *in_hbm(*after))


def gate(value, after):
    return pl.pallas_call(
        drop_inputs(lambda x_ref, out_ref: None, 1, len(after)),
        in_specs=[ANYWHERE] * (1 + len(after)),
        out_specs=ANYWHERE,
        out_shape=pltpu.HBM(value.shape, value.dtype),
        input_output_aliases={0: 0},
        cost_estimate=FREE,
        name="gate",
    )(*in_hbm(value, *after))


def transform_kernel(x_ref, out_ref):
    count, size = out_ref.shape[:2]
    start = pl.program_id(0) * size
    values = [x_ref[t, pl.ds(start, size)].astype(F32) for t in range(count)]
    stride = 1
    while stride < count:
        for t in range(count):
            if not t & stride:
                a, b = values[t], values[t | stride]
                values[t], values[t | stride] = a + b, a - b
        stride *= 2
    for t in range(count):
        out_ref[t] = (values[t] * count ** (-0.5)).astype(BF16)


def transform(value, after=(), cost=FREE):
    count, groups = value.shape[:2]
    steps = 4 if groups % 4 == 0 else 1
    return pl.pallas_call(
        drop_inputs(transform_kernel, 1, len(after)),
        grid=(steps,),
        in_specs=[pl.BlockSpec(memory_space=pltpu.VMEM)] + [ANYWHERE] * len(after),
        out_specs=pl.BlockSpec((count, groups // steps, SUB, HB), lambda i: (0, i, 0, 0)),
        out_shape=pltpu.HBM(value.shape, BF16),
        compiler_params=pltpu.CompilerParams(vmem_limit_bytes=SMALL),
        cost_estimate=cost,
        name="transform",
    )(value, *in_hbm(*after))


def exchange(value):
    return lax.all_to_all(value, "tensor", split_axis=0, concat_axis=0, tiled=True)


def partner(value, axis, mask):
    size = lax.axis_size(axis)
    return lax.ppermute(value, axis, [(i, i ^ mask) for i in range(size)])


def mix_across(value):
    size = lax.axis_size("tensor")
    index = lax.axis_index("tensor")
    masks = [1 << i for i in range(size.bit_length() - 1)]
    for place, mask in enumerate(masks):
        other = partner(value, "tensor", mask).astype(F32)
        sign = jnp.where((index & mask) != 0, -1.0, 1.0).astype(F32)
        total = other + sign * value.astype(F32)
        if place == len(masks) - 1:
            total = total * size ** (-0.5)
        value = total.astype(BF16)
    return value


def gather_upstream(upstream):
    rows, width = upstream.shape
    parts = lax.axis_size("dp")
    cols = width // parts
    half = rows // 2
    index = lax.axis_index("dp")
    core = lax.axis_index("tensor") & 1
    own = lax.dynamic_slice(upstream, (0, index * cols), (rows, cols))
    mine = [
        partner(
            lax.dynamic_slice(upstream, (core * half, (index ^ m) * cols), (half, cols)), "dp", m
        )
        for m in range(1, parts)
    ]
    mine = jnp.stack(mine)
    other = partner(mine, "tensor", 1)
    low = jnp.where(core == 0, mine, other)
    high = jnp.where(core == 0, other, mine)
    far = jnp.concatenate([low, high], axis=1).reshape((parts - 1) * rows, cols)
    return jnp.concatenate([own, far], axis=0)


def relay_kernel(x_ref, y_ref, a_ref, b_ref, x_out, y_out):
    half = a_ref.shape[0]
    x_out[:half] = x_ref[:half]
    x_out[half:] = (x_ref[half:].astype(F32) + b_ref[...].astype(F32)).astype(BF16)
    y_out[:half] = (y_ref[:half].astype(F32) + a_ref[...].astype(F32)).astype(BF16)
    y_out[half:] = y_ref[half:]


def total_kernel(count, *refs):
    out_ref = refs[-1]
    start = 0
    for i in range(count):
        own_ref, x_ref, y_ref = refs[3 * i : 3 * i + 3]
        size = own_ref.shape[1]
        out_ref[:, start : start + size] = (
            own_ref[...].astype(F32) + x_ref[...].astype(F32) + y_ref[...].astype(F32)
        ).astype(BF16)
        start += size


def total(chunks, after=()):
    ins = [value for own, *far in chunks for value in (*in_hbm(own), *far)]
    subs = ins[0].shape[0]
    groups = sum(chunk[0].shape[1] for chunk in chunks)
    step = 2
    return pl.pallas_call(
        drop_inputs(functools.partial(total_kernel, len(chunks)), len(ins), len(after)),
        grid=(subs // step,),
        in_specs=[pl.BlockSpec((step,) + v.shape[1:], lambda i: (i, 0, 0, 0)) for v in ins]
        + [ANYWHERE] * len(after),
        out_specs=pl.BlockSpec((step, groups, SUB, HB), lambda i: (i, 0, 0, 0)),
        out_shape=pltpu.HBM((subs, groups, SUB, HB), BF16),
        compiler_params=pltpu.CompilerParams(vmem_limit_bytes=SMALL),
        cost_estimate=FREE,
        name="total",
    )(*ins, *in_hbm(*after))


def general_shards(hidden, upstream, weight, scales, clip_mask, rot_block):
    groups = scales.shape[0]
    rows = hidden.shape[0]
    parts = lax.axis_size("dp")
    subs = rows // SUB
    index = lax.axis_index("dp")

    up = gather_upstream(upstream)
    (local,) = local_forward(hidden, rot_block, (groups,))
    rotated = lax.all_gather(mix_across(local), "dp", axis=0, tiled=False)
    order = index ^ jnp.arange(parts)
    rotated = rotated[order].reshape((parts * subs,) + local.shape[1:])
    per = 4 if groups % 4 == 0 else 1
    (full,) = unit_grads(up, weight, scales, 0, groups, per, (parts * subs,))
    full = full.reshape((parts,) + local.shape)[order]
    mixed = mix_across(lax.psum_scatter(full, "dp", scatter_dimension=0, tiled=False))
    grad_weight, grad_scales = weight_grads(
        [rotated], up, weight, scales, clip_mask, None, 0, groups, per
    )
    grad_hidden = local_backward([mixed], backward_matrices(rot_block), (groups,))
    return grad_hidden, grad_weight, grad_scales


def shards(hidden, upstream, weight, scales, clip_mask, rot_block):
    groups = scales.shape[0]
    subs = hidden.shape[0] // SUB
    if lax.axis_size("dp") != 4 or lax.axis_size("tensor") != subs or groups % 8 != 4:
        return general_shards(hidden, upstream, weight, scales, clip_mask, rot_block)
    per = 4
    units = groups // per
    sizes = (per * (units - units // 2), per * (units // 2))
    starts = (0, sizes[0])
    half = subs // 2
    counts = (subs, subs, subs, half, half)

    def scatter_first(parts_of):
        return partner(parts_of[3], "dp", 1), partner(parts_of[4], "dp", 2)

    def scatter_second(parts_of, received, after, cost=FREE):
        x_part, y_part = small_call(
            relay_kernel,
            "relay",
            [*in_hbm(parts_of[1], parts_of[2]), *received],
            [parts_of[1].shape] * 2,
            2,
            after,
            cost,
        )
        return x_part, partner(x_part, "dp", 1), partner(y_part, "dp", 2)

    def gather_rest(near, chunk, after):
        x_half, y_half = cut(near[1], near[2], starts[chunk], sizes[chunk], after)
        return *near, partner(y_half, "dp", 1), partner(x_half, "dp", 2)

    up = gather_upstream(upstream)
    (local,) = local_forward(hidden, rot_block, (groups,))
    forth = exchange(local)
    pers = [size // 4 for size in sizes]
    unit0 = unit_grads(
        up, weight, scales, starts[0], sizes[0], pers[0], counts, after=(local,), cost=SOME
    )
    first0 = scatter_first(unit0)
    unit1 = unit_grads(
        up, weight, scales, starts[1], sizes[1], pers[1], counts, after=(unit0[0],)
    )
    first1 = scatter_first(unit1)
    relayed0, *second0 = scatter_second(unit0, first0, after=(unit1[0],))
    turned = transform(forth, after=(relayed0,), cost=LONG)
    rotated = exchange(turned)
    relayed1, *second1 = scatter_second(unit1, first1, after=(turned,), cost=LONG)
    summed = gate(total(((unit0[0], *second0), (unit1[0], *second1))), after=(rotated,))
    matrices = backward_matrices(rot_block, after=(relayed1,))
    back = exchange(summed)
    near = (rotated, partner(rotated, "dp", 1), partner(rotated, "dp", 2))
    gathered0 = gather_rest(near, 0, ())
    mixed = transform(back, cost=LONG)
    final = exchange(mixed)
    gathered1 = gather_rest(near, 1, (mixed,))
    buffer, scale0 = weight_grads(
        gathered0, up, weight, scales, clip_mask, None, starts[0], sizes[0], pers[0], after=(mixed,)
    )
    buffer, scale1 = weight_grads(
        gathered1, up, weight, scales, clip_mask, buffer, starts[1], sizes[1], pers[1]
    )
    grad_hidden = local_backward([final], matrices, (groups,), after=(scale1,))
    return grad_hidden, buffer, jnp.concatenate([scale0, scale1], axis=0)


def solution(mesh):
    return jax.shard_map(
        shards,
        mesh=mesh,
        in_specs=(
            P("dp", "tensor"),
            P("dp", None),
            P("tensor", "dp"),
            P("tensor", "dp"),
            P("tensor", "dp"),
            P(),
        ),
        out_specs=(P("dp", "tensor"), P("tensor", "dp"), P("tensor", "dp")),
        check_vma=False,
    )
```

```python
import functools

import jax
import jax.numpy as jnp
from jax import lax
from jax.experimental import pallas as pl
from jax.experimental.pallas import tpu as pltpu
from jax.sharding import PartitionSpec as P

HB = 128
GROUP = 128
SUB = 16
ROWS = 8
F32 = jnp.float32
BF16 = jnp.bfloat16


def nt_dot(a, b):
    return lax.dot_general(a, b, (((1,), (1,)), ((), ())), preferred_element_type=F32)


def nn_dot(a, b):
    return lax.dot_general(a, b, (((1,), (0,)), ((), ())), preferred_element_type=F32)


def split2(value):
    high = value.astype(BF16)
    return high, (value - high.astype(F32)).astype(BF16)


def sign_matrix():
    size = 2 * HB
    row = lax.broadcasted_iota(jnp.int32, (size, size), 0)
    col = lax.broadcasted_iota(jnp.int32, (size, size), 1)
    both = row & col
    parity = jnp.zeros((size, size), jnp.int32)
    for bit in range(HB.bit_length() - 1):
        parity = parity ^ ((both >> bit) & 1)
    return jnp.where((row ^ col) < HB, (1 - 2 * parity).astype(F32), 0.0).astype(BF16)


def build_mixing(rot_ref, mix_ref, sign_ref, transposed):
    blocks = rot_ref.shape[0]
    size = blocks * ROWS
    row = lax.broadcasted_iota(jnp.int32, (size, blocks), 0)
    col = lax.broadcasted_iota(jnp.int32, (size, blocks), 1)
    pick = ((row >> 3) == col).astype(F32).astype(BF16)
    rows = lax.broadcasted_iota(jnp.int32, (size, size), 0)
    cols = lax.broadcasted_iota(jnp.int32, (size, size), 1)
    same = (rows & (ROWS - 1)) == (cols & (ROWS - 1))
    spread = [
        nt_dot(pick, part) if transposed else nn_dot(pick, part) for part in split2(rot_ref[...])
    ]
    for half, value in enumerate(spread):
        full = nt_dot(value.astype(BF16), pick)
        mix_ref[half * size : (half + 1) * size, :] = jnp.where(same, full, 0.0).astype(BF16)
    sign_ref[...] = sign_matrix()


def mix_rows(tiles, mix_ref, sign_ref, scale):
    blocks = len(tiles[0])
    size = blocks * ROWS
    stacked = jnp.concatenate([jnp.concatenate(one, axis=0).astype(BF16) for one in tiles], axis=1)
    halves = nn_dot(mix_ref[...], stacked)
    mixed = (halves[:size] + halves[size:]).astype(BF16)
    results = []
    for j in range(0, len(tiles), 2):
        part = nn_dot(mixed[:, j * HB : (j + 2) * HB], sign_ref[...]) * scale
        results += [part[:, :HB].reshape(blocks, ROWS, HB), part[:, HB:].reshape(blocks, ROWS, HB)]
    return results


def forward_kernel(sizes, scale, x_ref, rot_ref, *refs):
    outs, (mix_ref, sign_ref) = refs[: len(sizes)], refs[len(sizes) :]
    blocks = rot_ref.shape[0]

    @pl.when(pl.program_id(0) == 0)
    def _():
        build_mixing(rot_ref, mix_ref, sign_ref, True)

    rows = x_ref.shape[0]
    wide = [x_ref[:, k * HB : (k + 1) * HB].astype(F32) for k in range(blocks)]
    tiles = [[one[j : j + ROWS] for one in wide] for j in range(0, rows, ROWS)]
    results = mix_rows(tiles, mix_ref, sign_ref, scale)
    for j in range(rows // SUB):
        both = jnp.concatenate([results[2 * j], results[2 * j + 1]], axis=1).astype(BF16)
        start = 0
        for size, out_ref in zip(sizes, outs):
            out_ref[j] = both[start : start + size]
            start += size


def backward_kernel(sizes, scale, *refs):
    ins, (mix_ref, sign_ref, out_ref) = refs[: len(sizes)], refs[len(sizes) :]
    blocks = sum(sizes)
    rows = out_ref.shape[0]
    tiles = []
    start = pl.program_id(0) * (rows // SUB)
    for j in range(rows // SUB):
        wide = [
            in_ref[start + j, c].astype(F32)
            for size, in_ref in zip(sizes, ins)
            for c in range(size)
        ]
        tiles += [[one[:ROWS] for one in wide], [one[ROWS:] for one in wide]]
    results = mix_rows(tiles, mix_ref, sign_ref, scale)
    for j in range(rows // SUB):
        both = jnp.concatenate([results[2 * j], results[2 * j + 1]], axis=1).astype(BF16)
        for k in range(blocks):
            out_ref[j * SUB : (j + 1) * SUB, k * HB : (k + 1) * HB] = both[k]


def local_scratch(blocks):
    return [
        pltpu.VMEM((2 * blocks * ROWS, blocks * ROWS), BF16),
        pltpu.VMEM((2 * HB, 2 * HB), BF16),
    ]


FREE = pl.CostEstimate(flops=0, bytes_accessed=0, transcendentals=0)
LONG = pl.CostEstimate(flops=10**12, bytes_accessed=0, transcendentals=0)
SOME = pl.CostEstimate(flops=5_000_000_000, bytes_accessed=0, transcendentals=0)
SMALL = 16 << 20

ANYWHERE = pl.BlockSpec(memory_space=pl.ANY)


def in_hbm(*values):
    return [pltpu.with_memory_space_constraint(value, pltpu.HBM) for value in values]


def drop_inputs(kernel, start, count):
    def run(*refs):
        kernel(*refs[:start], *refs[start + count :])

    return run


def local_forward(hidden, rot_block, sizes, scale=HB ** (-0.5)):
    rows, width = hidden.shape
    blocks = width // HB
    parts = 4
    return pl.pallas_call(
        functools.partial(forward_kernel, sizes, scale),
        grid=(rows // (SUB * parts),),
        in_specs=[
            pl.BlockSpec((SUB * parts, width), lambda i: (i, 0)),
            pl.BlockSpec((blocks, blocks), lambda i: (0, 0)),
        ],
        out_specs=[pl.BlockSpec((parts, size, SUB, HB), lambda i: (i, 0, 0, 0)) for size in sizes],
        out_shape=[pltpu.HBM((rows // SUB, size, SUB, HB), BF16) for size in sizes],
        scratch_shapes=local_scratch(blocks),
        compiler_params=pltpu.CompilerParams(vmem_limit_bytes=60 << 20),
        cost_estimate=FREE,
        name="local_forward",
    )(*in_hbm(hidden), rot_block)


def backward_matrices(rot_block, after=()):
    size = rot_block.shape[0] * ROWS
    shapes = [(2 * size, size), (2 * HB, 2 * HB)]
    return pl.pallas_call(
        drop_inputs(
            lambda rot_ref, *refs: build_mixing(rot_ref, *refs, False), 1, len(after)
        ),
        in_specs=[pl.BlockSpec(memory_space=pltpu.VMEM)] + [ANYWHERE] * len(after),
        out_specs=[pl.BlockSpec(memory_space=pltpu.VMEM)] * 2,
        out_shape=[pltpu.HBM(shape, BF16) for shape in shapes],
        compiler_params=pltpu.CompilerParams(vmem_limit_bytes=SMALL),
        cost_estimate=FREE,
        name="backward_matrices",
    )(rot_block, *after)


def local_backward(mixed, matrices, sizes, after=(), scale=HB ** (-0.5)):
    count = mixed[0].shape[0]
    rows = count * SUB
    blocks = sum(sizes)
    parts = 4
    return pl.pallas_call(
        drop_inputs(functools.partial(backward_kernel, sizes, scale), len(sizes) + 2, len(after)),
        grid=(count // parts,),
        in_specs=[pl.BlockSpec(memory_space=pltpu.VMEM)] * len(sizes)
        + [pl.BlockSpec(value.shape, lambda i: (0, 0)) for value in matrices]
        + [ANYWHERE] * len(after),
        out_specs=pl.BlockSpec((parts * SUB, blocks * HB), lambda i: (i, 0)),
        out_shape=pltpu.HBM((rows, blocks * HB), BF16),
        compiler_params=pltpu.CompilerParams(vmem_limit_bytes=24 << 20),
        cost_estimate=FREE,
        name="local_backward",
    )(*mixed, *in_hbm(*matrices, *after))


def weight_spec(first, per, cols):
    return pl.BlockSpec(
        (pl.Element(per * GROUP), pl.Element(cols)), lambda i: ((first + i * per) * GROUP, 0)
    )


def units_kernel(first, per, up_ref, w_ref, s_ref, *refs):
    outs, (turned_ref, quant_ref) = refs[:-2], refs[-2:]
    base = first + pl.program_id(0) * per

    @pl.when(pl.program_id(0) == 0)
    def _():
        tile = 256
        for e in range(0, up_ref.shape[1], tile):
            turned_ref[e : e + tile, :] = up_ref[:, e : e + tile].T

    for g in range(per):
        rows = slice(g * GROUP, (g + 1) * GROUP)
        quant_ref[rows, :] = (w_ref[rows, :].astype(F32) * s_ref[pl.ds(base + g, 1), :]).astype(
            BF16
        )
    result = nn_dot(quant_ref[...], turned_ref[...]).astype(BF16)
    for g in range(per):
        turned = result[g * GROUP : (g + 1) * GROUP, :].T
        token = 0
        for out_ref in outs:
            for q in range(out_ref.shape[0]):
                out_ref[q, g] = turned[token : token + SUB, :]
                token += SUB


def unit_grads(up, weight, scales, first, size, per, counts, after=(), cost=FREE):
    tokens, cols = up.shape
    return pl.pallas_call(
        drop_inputs(functools.partial(units_kernel, first, per), 3, len(after)),
        grid=(size // per,),
        in_specs=[
            pl.BlockSpec((tokens, cols), lambda i: (0, 0)),
            weight_spec(first, per, cols),
            pl.BlockSpec(scales.shape, lambda i: (0, 0)),
        ]
        + [ANYWHERE] * len(after),
        out_specs=[pl.BlockSpec((count, per, SUB, HB), lambda i: (0, i, 0, 0)) for count in counts],
        out_shape=[pltpu.HBM((count, size, SUB, HB), BF16) for count in counts],
        scratch_shapes=[pltpu.VMEM((cols, tokens), BF16), pltpu.VMEM((per * GROUP, cols), BF16)],
        compiler_params=pltpu.CompilerParams(vmem_limit_bytes=40 << 20),
        cost_estimate=cost,
        name="unit_grads",
    )(up, *in_hbm(weight, scales), *in_hbm(*after))


def weights_kernel(first, per, pieces, *refs):
    rots = refs[:pieces]
    up_ref, w_ref, s_ref, m_ref = refs[pieces : pieces + 4]
    gw_ref, gs_ref = refs[-2:]
    step = pl.program_id(0)
    base = first + step * per
    left = jnp.concatenate(
        [
            jnp.concatenate(
                [rot_ref[q, g] for rot_ref in rots for q in range(rot_ref.shape[0])], axis=0
            )
            for g in range(per)
        ],
        axis=1,
    ).T
    cols = up_ref.shape[1]
    tile = min(256, cols)
    for e in range(cols // tile):
        span = slice(e * tile, (e + 1) * tile)
        grad = nn_dot(left, up_ref[:, span])
        for g in range(per):
            rows = slice(g * GROUP, (g + 1) * GROUP)
            piece = grad[rows]
            scale = s_ref[pl.ds(base + g, 1), span]
            kept = m_ref[pl.ds(base + g, 1), span].astype(F32) * scale
            gw_ref[rows, span] = (piece * kept).astype(BF16)
            gs_ref[pl.ds(step * per + g, 1), span] = jnp.sum(
                piece * w_ref[rows, span].astype(F32), axis=0, keepdims=True
            )


def weight_grads(rotated, up, weight, scales, mask, buffer, first, size, per, after=()):
    tokens, cols = up.shape
    specs = [
        pl.BlockSpec(
            tuple(map(pl.Element, (piece.shape[0], per, SUB, HB))),
            functools.partial(lambda place, i: (0, place + i * per, 0, 0), place),
        )
        for piece in rotated
        for place in ((0 if piece.shape[1] == size else first),)
    ] + [
        pl.BlockSpec((tokens, cols), lambda i: (0, 0)),
        weight_spec(first, per, cols),
        pl.BlockSpec(scales.shape, lambda i: (0, 0)),
        pl.BlockSpec(scales.shape, lambda i: (0, 0)),
    ]
    args = [*rotated, up, *in_hbm(weight, scales, mask)]
    aliases = {}
    if buffer is not None:
        aliases = {len(args): 0}
        args.append(buffer)
        specs.append(ANYWHERE)
    return pl.pallas_call(
        functools.partial(weights_kernel, first, per, len(rotated)),
        grid=(size // per,),
        in_specs=specs + [ANYWHERE] * len(after),
        out_specs=[
            weight_spec(first, per, cols),
            pl.BlockSpec((size, cols), lambda i: (0, 0)),
        ],
        out_shape=[
            pltpu.HBM(weight.shape, BF16),
            jax.ShapeDtypeStruct((size, cols), F32),
        ],
        input_output_aliases=aliases,
        compiler_params=pltpu.CompilerParams(vmem_limit_bytes=40 << 20),
        cost_estimate=LONG,
        name="weight_grads",
    )(*args, *in_hbm(*after))


def small_call(kernel, name, ins, outs, steps, after=(), cost=FREE):
    def spec(shape, dim):
        block = tuple(n // steps if d == dim else n for d, n in enumerate(shape))
        return pl.BlockSpec(
            block, lambda i: tuple(i if d == dim else 0 for d in range(len(shape)))
        )

    return pl.pallas_call(
        drop_inputs(kernel, len(ins), len(after)),
        grid=(steps,),
        in_specs=[spec(value.shape, 1) for value in ins] + [ANYWHERE] * len(after),
        out_specs=[spec(shape, 1) for shape in outs],
        out_shape=[pltpu.HBM(shape, BF16) for shape in outs],
        compiler_params=pltpu.CompilerParams(vmem_limit_bytes=SMALL),
        cost_estimate=cost,
        name=name,
    )(*ins, *in_hbm(*after))


def cut_kernel(start, x_ref, y_ref, x_out, y_out):
    size = x_out.shape[1]
    x_out[...] = x_ref[:, start : start + size]
    y_out[...] = y_ref[:, start : start + size]


def cut(x_part, y_part, start, size, after):
    subs, groups = x_part.shape[:2]
    half = subs // 2
    out = pl.BlockSpec((2, size, SUB, HB), lambda i: (i, 0, 0, 0))
    return pl.pallas_call(
        drop_inputs(functools.partial(cut_kernel, start), 2, len(after)),
        grid=(half // 2,),
        in_specs=[
            pl.BlockSpec((2, groups, SUB, HB), lambda i: (half // 2 + i, 0, 0, 0)),
            pl.BlockSpec((2, groups, SUB, HB), lambda i: (i, 0, 0, 0)),
        ]
        + [ANYWHERE] * len(after),
        out_specs=[out, out],
        out_shape=[pltpu.HBM((half, size, SUB, HB), BF16)] * 2,
        compiler_params=pltpu.CompilerParams(vmem_limit_bytes=SMALL),
        cost_estimate=FREE,
        name="cut",
    )(x_part, y_part, *in_hbm(*after))


def gate(value, after):
    return pl.pallas_call(
        drop_inputs(lambda x_ref, out_ref: None, 1, len(after)),
        in_specs=[ANYWHERE] * (1 + len(after)),
        out_specs=ANYWHERE,
        out_shape=pltpu.HBM(value.shape, value.dtype),
        input_output_aliases={0: 0},
        cost_estimate=FREE,
        name="gate",
    )(*in_hbm(value, *after))


def transform_kernel(x_ref, out_ref):
    count, size = out_ref.shape[:2]
    start = pl.program_id(0) * size
    values = [x_ref[t, pl.ds(start, size)].astype(F32) for t in range(count)]
    stride = 1
    while stride < count:
        for t in range(count):
            if not t & stride:
                a, b = values[t], values[t | stride]
                values[t], values[t | stride] = a + b, a - b
        stride *= 2
    for t in range(count):
        out_ref[t] = values[t].astype(BF16)


def transform(value, after=(), cost=FREE):
    count, groups = value.shape[:2]
    steps = 4 if groups % 4 == 0 else 1
    return pl.pallas_call(
        drop_inputs(transform_kernel, 1, len(after)),
        grid=(steps,),
        in_specs=[pl.BlockSpec(memory_space=pltpu.VMEM)] + [ANYWHERE] * len(after),
        out_specs=pl.BlockSpec((count, groups // steps, SUB, HB), lambda i: (0, i, 0, 0)),
        out_shape=pltpu.HBM(value.shape, BF16),
        compiler_params=pltpu.CompilerParams(vmem_limit_bytes=SMALL),
        cost_estimate=cost,
        name="transform",
    )(value, *in_hbm(*after))


def exchange(value):
    return lax.all_to_all(value, "tensor", split_axis=0, concat_axis=0, tiled=True)


def partner(value, axis, mask):
    size = lax.axis_size(axis)
    return lax.ppermute(value, axis, [(i, i ^ mask) for i in range(size)])


def mix_across(value):
    size = lax.axis_size("tensor")
    index = lax.axis_index("tensor")
    masks = [1 << i for i in range(size.bit_length() - 1)]
    for place, mask in enumerate(masks):
        other = partner(value, "tensor", mask).astype(F32)
        sign = jnp.where((index & mask) != 0, -1.0, 1.0).astype(F32)
        total = other + sign * value.astype(F32)
        if place == len(masks) - 1:
            total = total * size ** (-0.5)
        value = total.astype(BF16)
    return value


def gather_upstream(upstream):
    rows, width = upstream.shape
    parts = lax.axis_size("dp")
    cols = width // parts
    half = rows // 2
    index = lax.axis_index("dp")
    core = lax.axis_index("tensor") & 1
    own = lax.dynamic_slice(upstream, (0, index * cols), (rows, cols))
    mine = [
        partner(
            lax.dynamic_slice(upstream, (core * half, (index ^ m) * cols), (half, cols)), "dp", m
        )
        for m in range(1, parts)
    ]
    mine = jnp.stack(mine)
    other = partner(mine, "tensor", 1)
    low = jnp.where(core == 0, mine, other)
    high = jnp.where(core == 0, other, mine)
    far = jnp.concatenate([low, high], axis=1).reshape((parts - 1) * rows, cols)
    return jnp.concatenate([own, far], axis=0)


def relay_kernel(x_ref, y_ref, a_ref, b_ref, x_out, y_out):
    half = a_ref.shape[0]
    x_out[:half] = x_ref[:half]
    x_out[half:] = (x_ref[half:].astype(F32) + b_ref[...].astype(F32)).astype(BF16)
    y_out[:half] = (y_ref[:half].astype(F32) + a_ref[...].astype(F32)).astype(BF16)
    y_out[half:] = y_ref[half:]


def total_kernel(count, *refs):
    out_ref = refs[-1]
    start = 0
    for i in range(count):
        own_ref, x_ref, y_ref = refs[3 * i : 3 * i + 3]
        size = own_ref.shape[1]
        out_ref[:, start : start + size] = (
            own_ref[...].astype(F32) + x_ref[...].astype(F32) + y_ref[...].astype(F32)
        ).astype(BF16)
        start += size


def total(chunks, after=()):
    ins = [value for own, *far in chunks for value in (*in_hbm(own), *far)]
    subs = ins[0].shape[0]
    groups = sum(chunk[0].shape[1] for chunk in chunks)
    step = 2
    return pl.pallas_call(
        drop_inputs(functools.partial(total_kernel, len(chunks)), len(ins), len(after)),
        grid=(subs // step,),
        in_specs=[pl.BlockSpec((step,) + v.shape[1:], lambda i: (i, 0, 0, 0)) for v in ins]
        + [ANYWHERE] * len(after),
        out_specs=pl.BlockSpec((step, groups, SUB, HB), lambda i: (i, 0, 0, 0)),
        out_shape=pltpu.HBM((subs, groups, SUB, HB), BF16),
        compiler_params=pltpu.CompilerParams(vmem_limit_bytes=SMALL),
        cost_estimate=FREE,
        name="total",
    )(*ins, *in_hbm(*after))


def general_shards(hidden, upstream, weight, scales, clip_mask, rot_block):
    groups = scales.shape[0]
    rows = hidden.shape[0]
    parts = lax.axis_size("dp")
    subs = rows // SUB
    index = lax.axis_index("dp")

    up = gather_upstream(upstream)
    (local,) = local_forward(hidden, rot_block, (groups,))
    rotated = lax.all_gather(mix_across(local), "dp", axis=0, tiled=False)
    order = index ^ jnp.arange(parts)
    rotated = rotated[order].reshape((parts * subs,) + local.shape[1:])
    per = 4 if groups % 4 == 0 else 1
    (full,) = unit_grads(up, weight, scales, 0, groups, per, (parts * subs,))
    full = full.reshape((parts,) + local.shape)[order]
    mixed = mix_across(lax.psum_scatter(full, "dp", scatter_dimension=0, tiled=False))
    grad_weight, grad_scales = weight_grads(
        [rotated], up, weight, scales, clip_mask, None, 0, groups, per
    )
    grad_hidden = local_backward([mixed], backward_matrices(rot_block), (groups,))
    return grad_hidden, grad_weight, grad_scales


def shards(hidden, upstream, weight, scales, clip_mask, rot_block):
    groups = scales.shape[0]
    subs = hidden.shape[0] // SUB
    if lax.axis_size("dp") != 4 or lax.axis_size("tensor") != subs or groups % 8 != 4:
        return general_shards(hidden, upstream, weight, scales, clip_mask, rot_block)
    per = 4
    units = groups // per
    sizes = (per * (units - units // 2), per * (units // 2))
    starts = (0, sizes[0])
    half = subs // 2
    counts = (subs, subs, subs, half, half)

    def scatter_first(parts_of):
        return partner(parts_of[3], "dp", 1), partner(parts_of[4], "dp", 2)

    def scatter_second(parts_of, received, after, cost=FREE):
        x_part, y_part = small_call(
            relay_kernel,
            "relay",
            [*in_hbm(parts_of[1], parts_of[2]), *received],
            [parts_of[1].shape] * 2,
            2,
            after,
            cost,
        )
        return x_part, partner(x_part, "dp", 1), partner(y_part, "dp", 2)

    def gather_rest(near, chunk, after):
        x_half, y_half = cut(near[1], near[2], starts[chunk], sizes[chunk], after)
        return *near, partner(y_half, "dp", 1), partner(x_half, "dp", 2)

    up = gather_upstream(upstream)
    scale = (HB * subs) ** (-0.5)
    (local,) = local_forward(hidden, rot_block, (groups,), scale)
    forth = exchange(local)
    pers = [size // 4 for size in sizes]
    unit0 = unit_grads(
        up, weight, scales, starts[0], sizes[0], pers[0], counts, after=(local,), cost=SOME
    )
    first0 = scatter_first(unit0)
    unit1 = unit_grads(
        up, weight, scales, starts[1], sizes[1], pers[1], counts, after=(unit0[0],)
    )
    first1 = scatter_first(unit1)
    relayed0, *second0 = scatter_second(unit0, first0, after=(unit1[0],))
    turned = transform(forth, after=(relayed0,), cost=LONG)
    rotated = exchange(turned)
    relayed1, *second1 = scatter_second(unit1, first1, after=(turned,), cost=LONG)
    summed = gate(total(((unit0[0], *second0), (unit1[0], *second1))), after=(rotated,))
    matrices = backward_matrices(rot_block, after=(relayed1,))
    back = exchange(summed)
    near = (rotated, partner(rotated, "dp", 1), partner(rotated, "dp", 2))
    gathered0 = gather_rest(near, 0, ())
    mixed = transform(back, cost=LONG)
    final = exchange(mixed)
    gathered1 = gather_rest(near, 1, (mixed,))
    buffer, scale0 = weight_grads(
        gathered0, up, weight, scales, clip_mask, None, starts[0], sizes[0], pers[0], after=(mixed,)
    )
    buffer, scale1 = weight_grads(
        gathered1, up, weight, scales, clip_mask, buffer, starts[1], sizes[1], pers[1]
    )
    grad_hidden = local_backward(
        [final], matrices, (groups,), after=(scale1,), scale=scale
    )
    return grad_hidden, buffer, jnp.concatenate([scale0, scale1], axis=0)


def solution(mesh):
    return jax.shard_map(
        shards,
        mesh=mesh,
        in_specs=(
            P("dp", "tensor"),
            P("dp", None),
            P("tensor", "dp"),
            P("tensor", "dp"),
            P("tensor", "dp"),
            P(),
        ),
        out_specs=(P("dp", "tensor"), P("tensor", "dp"), P("tensor", "dp")),
        check_vma=False,
    )
```

```python
import functools

import jax
import jax.numpy as jnp
from jax import lax
from jax.experimental import pallas as pl
from jax.experimental.pallas import tpu as pltpu
from jax.sharding import PartitionSpec as P

HB = 128
GROUP = 128
SUB = 16
ROWS = 8
F32 = jnp.float32
BF16 = jnp.bfloat16


def nt_dot(a, b):
    return lax.dot_general(a, b, (((1,), (1,)), ((), ())), preferred_element_type=F32)


def nn_dot(a, b):
    return lax.dot_general(a, b, (((1,), (0,)), ((), ())), preferred_element_type=F32)


def split2(value):
    high = value.astype(BF16)
    return high, (value - high.astype(F32)).astype(BF16)


def sign_matrix():
    size = 2 * HB
    row = lax.broadcasted_iota(jnp.int32, (size, size), 0)
    col = lax.broadcasted_iota(jnp.int32, (size, size), 1)
    both = row & col
    parity = jnp.zeros((size, size), jnp.int32)
    for bit in range(HB.bit_length() - 1):
        parity = parity ^ ((both >> bit) & 1)
    return jnp.where((row ^ col) < HB, (1 - 2 * parity).astype(F32), 0.0).astype(BF16)


def build_mixing(rot_ref, mix_ref, sign_ref, transposed):
    blocks = rot_ref.shape[0]
    size = blocks * ROWS
    row = lax.broadcasted_iota(jnp.int32, (size, blocks), 0)
    col = lax.broadcasted_iota(jnp.int32, (size, blocks), 1)
    pick = ((row >> 3) == col).astype(F32).astype(BF16)
    rows = lax.broadcasted_iota(jnp.int32, (size, size), 0)
    cols = lax.broadcasted_iota(jnp.int32, (size, size), 1)
    same = (rows & (ROWS - 1)) == (cols & (ROWS - 1))
    spread = [
        nt_dot(pick, part) if transposed else nn_dot(pick, part) for part in split2(rot_ref[...])
    ]
    for half, value in enumerate(spread):
        full = nt_dot(value.astype(BF16), pick)
        mix_ref[half * size : (half + 1) * size, :] = jnp.where(same, full, 0.0).astype(BF16)
    sign_ref[...] = sign_matrix()


def mix_rows(tiles, mix_ref, sign_ref, scale):
    blocks = len(tiles[0])
    size = blocks * ROWS
    stacked = jnp.concatenate([jnp.concatenate(one, axis=0).astype(BF16) for one in tiles], axis=1)
    halves = nn_dot(mix_ref[...], stacked)
    mixed = (halves[:size] + halves[size:]).astype(BF16)
    results = []
    for j in range(0, len(tiles), 2):
        part = nn_dot(mixed[:, j * HB : (j + 2) * HB], sign_ref[...]) * scale
        results += [part[:, :HB].reshape(blocks, ROWS, HB), part[:, HB:].reshape(blocks, ROWS, HB)]
    return results


def forward_kernel(sizes, scale, x_ref, rot_ref, *refs):
    outs, (mix_ref, sign_ref) = refs[: len(sizes)], refs[len(sizes) :]
    blocks = rot_ref.shape[0]

    @pl.when(pl.program_id(0) == 0)
    def _():
        build_mixing(rot_ref, mix_ref, sign_ref, True)

    rows = x_ref.shape[0]
    wide = [x_ref[:, k * HB : (k + 1) * HB].astype(F32) for k in range(blocks)]
    tiles = [[one[j : j + ROWS] for one in wide] for j in range(0, rows, ROWS)]
    results = mix_rows(tiles, mix_ref, sign_ref, scale)
    for j in range(rows // SUB):
        both = jnp.concatenate([results[2 * j], results[2 * j + 1]], axis=1).astype(BF16)
        start = 0
        for size, out_ref in zip(sizes, outs):
            out_ref[j] = both[start : start + size]
            start += size


def backward_kernel(counts, scale, *refs):
    ins, (mix_ref, sign_ref, out_ref) = refs[: sum(counts)], refs[sum(counts) :]
    chunks = [ins[sum(counts[:i]) : sum(counts[: i + 1])] for i in range(len(counts))]
    rows = out_ref.shape[0]
    tiles = []
    for j in range(rows // SUB):
        wide = [
            sum(term[j, c].astype(F32) for term in terms)
            for terms in chunks
            for c in range(terms[0].shape[1])
        ]
        tiles += [[one[:ROWS] for one in wide], [one[ROWS:] for one in wide]]
    results = mix_rows(tiles, mix_ref, sign_ref, scale)
    for j in range(rows // SUB):
        both = jnp.concatenate([results[2 * j], results[2 * j + 1]], axis=1).astype(BF16)
        for k in range(both.shape[0]):
            out_ref[j * SUB : (j + 1) * SUB, k * HB : (k + 1) * HB] = both[k]


def local_scratch(blocks):
    return [
        pltpu.VMEM((2 * blocks * ROWS, blocks * ROWS), BF16),
        pltpu.VMEM((2 * HB, 2 * HB), BF16),
    ]


FREE = pl.CostEstimate(flops=0, bytes_accessed=0, transcendentals=0)
LONG = pl.CostEstimate(flops=10**12, bytes_accessed=0, transcendentals=0)
SOME = pl.CostEstimate(flops=5_000_000_000, bytes_accessed=0, transcendentals=0)
SMALL = 16 << 20

ANYWHERE = pl.BlockSpec(memory_space=pl.ANY)


def in_hbm(*values):
    return [pltpu.with_memory_space_constraint(value, pltpu.HBM) for value in values]


def drop_inputs(kernel, start, count):
    def run(*refs):
        kernel(*refs[:start], *refs[start + count :])

    return run


def local_forward(hidden, rot_block, sizes, scale=HB ** (-0.5)):
    rows, width = hidden.shape
    blocks = width // HB
    parts = 4
    return pl.pallas_call(
        functools.partial(forward_kernel, sizes, scale),
        grid=(rows // (SUB * parts),),
        in_specs=[
            pl.BlockSpec((SUB * parts, width), lambda i: (i, 0)),
            pl.BlockSpec((blocks, blocks), lambda i: (0, 0)),
        ],
        out_specs=[pl.BlockSpec((parts, size, SUB, HB), lambda i: (i, 0, 0, 0)) for size in sizes],
        out_shape=[pltpu.HBM((rows // SUB, size, SUB, HB), BF16) for size in sizes],
        scratch_shapes=local_scratch(blocks),
        compiler_params=pltpu.CompilerParams(vmem_limit_bytes=60 << 20),
        cost_estimate=FREE,
        name="local_forward",
    )(*in_hbm(hidden), rot_block)


def backward_matrices(rot_block, after=()):
    size = rot_block.shape[0] * ROWS
    shapes = [(2 * size, size), (2 * HB, 2 * HB)]
    return pl.pallas_call(
        drop_inputs(
            lambda rot_ref, *refs: build_mixing(rot_ref, *refs, False), 1, len(after)
        ),
        in_specs=[pl.BlockSpec(memory_space=pltpu.VMEM)] + [ANYWHERE] * len(after),
        out_specs=[pl.BlockSpec(memory_space=pltpu.VMEM)] * 2,
        out_shape=[pltpu.HBM(shape, BF16) for shape in shapes],
        compiler_params=pltpu.CompilerParams(vmem_limit_bytes=SMALL),
        cost_estimate=FREE,
        name="backward_matrices",
    )(rot_block, *after)


def local_backward(chunks, matrices, scale=HB ** (-0.5)):
    ins = [value for own, *far in chunks for value in (*in_hbm(own), *far)]
    count = ins[0].shape[0]
    width = sum(chunk[0].shape[1] for chunk in chunks) * HB
    parts = 4
    return pl.pallas_call(
        functools.partial(backward_kernel, [len(chunk) for chunk in chunks], scale),
        grid=(count // parts,),
        in_specs=[pl.BlockSpec((parts,) + v.shape[1:], lambda i: (i, 0, 0, 0)) for v in ins]
        + [pl.BlockSpec(value.shape, lambda i: (0, 0)) for value in matrices],
        out_specs=pl.BlockSpec((parts * SUB, width), lambda i: (i, 0)),
        out_shape=pltpu.HBM((count * SUB, width), BF16),
        compiler_params=pltpu.CompilerParams(vmem_limit_bytes=32 << 20),
        cost_estimate=FREE,
        name="local_backward",
    )(*ins, *in_hbm(*matrices))


def weight_spec(first, per, cols):
    return pl.BlockSpec(
        (pl.Element(per * GROUP), pl.Element(cols)), lambda i: ((first + i * per) * GROUP, 0)
    )


def units_kernel(first, per, up_ref, w_ref, s_ref, *refs):
    outs, (turned_ref, quant_ref) = refs[:-2], refs[-2:]
    base = first + pl.program_id(0) * per

    @pl.when(pl.program_id(0) == 0)
    def _():
        tile = 256
        for e in range(0, up_ref.shape[1], tile):
            turned_ref[e : e + tile, :] = up_ref[:, e : e + tile].T

    for g in range(per):
        rows = slice(g * GROUP, (g + 1) * GROUP)
        quant_ref[rows, :] = (w_ref[rows, :].astype(F32) * s_ref[pl.ds(base + g, 1), :]).astype(
            BF16
        )
    result = nn_dot(quant_ref[...], turned_ref[...]).astype(BF16)
    for g in range(per):
        turned = result[g * GROUP : (g + 1) * GROUP, :].T
        token = 0
        for out_ref in outs:
            for q in range(out_ref.shape[0]):
                out_ref[q, g] = turned[token : token + SUB, :]
                token += SUB


def unit_grads(up, weight, scales, first, size, per, counts, after=(), cost=FREE):
    tokens, cols = up.shape
    return pl.pallas_call(
        drop_inputs(functools.partial(units_kernel, first, per), 3, len(after)),
        grid=(size // per,),
        in_specs=[
            pl.BlockSpec((tokens, cols), lambda i: (0, 0)),
            weight_spec(first, per, cols),
            pl.BlockSpec(scales.shape, lambda i: (0, 0)),
        ]
        + [ANYWHERE] * len(after),
        out_specs=[pl.BlockSpec((count, per, SUB, HB), lambda i: (0, i, 0, 0)) for count in counts],
        out_shape=[pltpu.HBM((count, size, SUB, HB), BF16) for count in counts],
        scratch_shapes=[pltpu.VMEM((cols, tokens), BF16), pltpu.VMEM((per * GROUP, cols), BF16)],
        compiler_params=pltpu.CompilerParams(vmem_limit_bytes=40 << 20),
        cost_estimate=cost,
        name="unit_grads",
    )(up, *in_hbm(weight, scales), *in_hbm(*after))


def weights_kernel(first, per, pieces, *refs):
    rots = refs[:pieces]
    up_ref, w_ref, s_ref, m_ref = refs[pieces : pieces + 4]
    gw_ref, gs_ref = refs[-2:]
    step = pl.program_id(0)
    base = first + step * per
    left = jnp.concatenate(
        [
            jnp.concatenate(
                [rot_ref[q, g] for rot_ref in rots for q in range(rot_ref.shape[0])], axis=0
            )
            for g in range(per)
        ],
        axis=1,
    ).T
    cols = up_ref.shape[1]
    tile = min(256, cols)
    for e in range(cols // tile):
        span = slice(e * tile, (e + 1) * tile)
        grad = nn_dot(left, up_ref[:, span])
        for g in range(per):
            rows = slice(g * GROUP, (g + 1) * GROUP)
            piece = grad[rows]
            scale = s_ref[pl.ds(base + g, 1), span]
            kept = m_ref[pl.ds(base + g, 1), span].astype(F32) * scale
            gw_ref[rows, span] = (piece * kept).astype(BF16)
            gs_ref[pl.ds(step * per + g, 1), span] = jnp.sum(
                piece * w_ref[rows, span].astype(F32), axis=0, keepdims=True
            )


def weight_grads(rotated, up, weight, scales, mask, buffer, first, size, per, after=()):
    tokens, cols = up.shape
    specs = [
        pl.BlockSpec(
            tuple(map(pl.Element, (piece.shape[0], per, SUB, HB))),
            functools.partial(lambda place, i: (0, place + i * per, 0, 0), place),
        )
        for piece in rotated
        for place in ((0 if piece.shape[1] == size else first),)
    ] + [
        pl.BlockSpec((tokens, cols), lambda i: (0, 0)),
        weight_spec(first, per, cols),
        pl.BlockSpec(scales.shape, lambda i: (0, 0)),
        pl.BlockSpec(scales.shape, lambda i: (0, 0)),
    ]
    args = [*rotated, up, *in_hbm(weight, scales, mask)]
    aliases = {}
    if buffer is not None:
        aliases = {len(args): 0}
        args.append(buffer)
        specs.append(ANYWHERE)
    return pl.pallas_call(
        functools.partial(weights_kernel, first, per, len(rotated)),
        grid=(size // per,),
        in_specs=specs + [ANYWHERE] * len(after),
        out_specs=[
            weight_spec(first, per, cols),
            pl.BlockSpec((size, cols), lambda i: (0, 0)),
        ],
        out_shape=[
            pltpu.HBM(weight.shape, BF16),
            jax.ShapeDtypeStruct((size, cols), F32),
        ],
        input_output_aliases=aliases,
        compiler_params=pltpu.CompilerParams(vmem_limit_bytes=40 << 20),
        cost_estimate=LONG,
        name="weight_grads",
    )(*args, *in_hbm(*after))


def small_call(kernel, name, ins, outs, steps, after=(), cost=FREE):
    def spec(shape, dim):
        block = tuple(n // steps if d == dim else n for d, n in enumerate(shape))
        return pl.BlockSpec(
            block, lambda i: tuple(i if d == dim else 0 for d in range(len(shape)))
        )

    return pl.pallas_call(
        drop_inputs(kernel, len(ins), len(after)),
        grid=(steps,),
        in_specs=[spec(value.shape, 1) for value in ins] + [ANYWHERE] * len(after),
        out_specs=[spec(shape, 1) for shape in outs],
        out_shape=[pltpu.HBM(shape, BF16) for shape in outs],
        compiler_params=pltpu.CompilerParams(vmem_limit_bytes=SMALL),
        cost_estimate=cost,
        name=name,
    )(*ins, *in_hbm(*after))


def cut_kernel(start, x_ref, y_ref, x_out, y_out):
    size = x_out.shape[1]
    x_out[...] = x_ref[:, start : start + size]
    y_out[...] = y_ref[:, start : start + size]


def cut(x_part, y_part, start, size, after):
    subs, groups = x_part.shape[:2]
    half = subs // 2
    out = pl.BlockSpec((2, size, SUB, HB), lambda i: (i, 0, 0, 0))
    return pl.pallas_call(
        drop_inputs(functools.partial(cut_kernel, start), 2, len(after)),
        grid=(half // 2,),
        in_specs=[
            pl.BlockSpec((2, groups, SUB, HB), lambda i: (half // 2 + i, 0, 0, 0)),
            pl.BlockSpec((2, groups, SUB, HB), lambda i: (i, 0, 0, 0)),
        ]
        + [ANYWHERE] * len(after),
        out_specs=[out, out],
        out_shape=[pltpu.HBM((half, size, SUB, HB), BF16)] * 2,
        compiler_params=pltpu.CompilerParams(vmem_limit_bytes=SMALL),
        cost_estimate=FREE,
        name="cut",
    )(x_part, y_part, *in_hbm(*after))


def gate(value, after):
    return pl.pallas_call(
        drop_inputs(lambda x_ref, out_ref: None, 1, len(after)),
        in_specs=[ANYWHERE] * (1 + len(after)),
        out_specs=ANYWHERE,
        out_shape=pltpu.HBM(value.shape, value.dtype),
        input_output_aliases={0: 0},
        cost_estimate=FREE,
        name="gate",
    )(*in_hbm(value, *after))


def transform_kernel(x_ref, out_ref):
    count, _, size = out_ref.shape
    start = pl.multiple_of(pl.program_id(0) * size, HB)
    values = [x_ref[t, :, pl.ds(start, size)].astype(F32) for t in range(count)]
    stride = 1
    while stride < count:
        for t in range(count):
            if not t & stride:
                a, b = values[t], values[t | stride]
                values[t], values[t | stride] = a + b, a - b
        stride *= 2
    for t in range(count):
        out_ref[t] = values[t].astype(BF16)


def transform(value, after=(), cost=FREE):
    count, rows, width = value.shape
    steps = 4
    return pl.pallas_call(
        drop_inputs(transform_kernel, 1, len(after)),
        grid=(steps,),
        in_specs=[pl.BlockSpec(memory_space=pltpu.VMEM)] + [ANYWHERE] * len(after),
        out_specs=pl.BlockSpec((count, rows, width // steps), lambda i: (0, 0, i)),
        out_shape=pltpu.HBM(value.shape, BF16),
        compiler_params=pltpu.CompilerParams(vmem_limit_bytes=SMALL),
        cost_estimate=cost,
        name="transform",
    )(value, *in_hbm(*after))


def exchange(value):
    return lax.all_to_all(value, "tensor", split_axis=0, concat_axis=0, tiled=True)


def partner(value, axis, mask):
    size = lax.axis_size(axis)
    return lax.ppermute(value, axis, [(i, i ^ mask) for i in range(size)])


def mix_across(value):
    size = lax.axis_size("tensor")
    index = lax.axis_index("tensor")
    masks = [1 << i for i in range(size.bit_length() - 1)]
    for place, mask in enumerate(masks):
        other = partner(value, "tensor", mask).astype(F32)
        sign = jnp.where((index & mask) != 0, -1.0, 1.0).astype(F32)
        total = other + sign * value.astype(F32)
        if place == len(masks) - 1:
            total = total * size ** (-0.5)
        value = total.astype(BF16)
    return value


def gather_upstream(upstream):
    rows, width = upstream.shape
    parts = lax.axis_size("dp")
    cols = width // parts
    half = rows // 2
    index = lax.axis_index("dp")
    core = lax.axis_index("tensor") & 1
    own = lax.dynamic_slice(upstream, (0, index * cols), (rows, cols))
    mine = [
        partner(
            lax.dynamic_slice(upstream, (core * half, (index ^ m) * cols), (half, cols)), "dp", m
        )
        for m in range(1, parts)
    ]
    mine = jnp.stack(mine)
    other = partner(mine, "tensor", 1)
    low = jnp.where(core == 0, mine, other)
    high = jnp.where(core == 0, other, mine)
    far = jnp.concatenate([low, high], axis=1).reshape((parts - 1) * rows, cols)
    return jnp.concatenate([own, far], axis=0)


def relay_kernel(x_ref, y_ref, a_ref, b_ref, x_out, y_out):
    half = a_ref.shape[0]
    x_out[:half] = x_ref[:half]
    x_out[half:] = (x_ref[half:].astype(F32) + b_ref[...].astype(F32)).astype(BF16)
    y_out[:half] = (y_ref[:half].astype(F32) + a_ref[...].astype(F32)).astype(BF16)
    y_out[half:] = y_ref[half:]


def general_shards(hidden, upstream, weight, scales, clip_mask, rot_block):
    groups = scales.shape[0]
    rows = hidden.shape[0]
    parts = lax.axis_size("dp")
    subs = rows // SUB
    index = lax.axis_index("dp")

    up = gather_upstream(upstream)
    (local,) = local_forward(hidden, rot_block, (groups,))
    rotated = lax.all_gather(mix_across(local), "dp", axis=0, tiled=False)
    order = index ^ jnp.arange(parts)
    rotated = rotated[order].reshape((parts * subs,) + local.shape[1:])
    per = 4 if groups % 4 == 0 else 1
    (full,) = unit_grads(up, weight, scales, 0, groups, per, (parts * subs,))
    full = full.reshape((parts,) + local.shape)[order]
    mixed = mix_across(lax.psum_scatter(full, "dp", scatter_dimension=0, tiled=False))
    grad_weight, grad_scales = weight_grads(
        [rotated], up, weight, scales, clip_mask, None, 0, groups, per
    )
    grad_hidden = local_backward([[mixed]], backward_matrices(rot_block))
    return grad_hidden, grad_weight, grad_scales


def shards(hidden, upstream, weight, scales, clip_mask, rot_block):
    groups = scales.shape[0]
    subs = hidden.shape[0] // SUB
    if lax.axis_size("dp") != 4 or lax.axis_size("tensor") != subs or groups % 8 != 4:
        return general_shards(hidden, upstream, weight, scales, clip_mask, rot_block)
    per = 4
    units = groups // per
    sizes = (per * (units - units // 2), per * (units // 2))
    starts = (0, sizes[0])
    half = subs // 2
    counts = (subs, subs, subs, half, half)

    def scatter_first(parts_of):
        return partner(parts_of[3], "dp", 1), partner(parts_of[4], "dp", 2)

    def scatter_second(parts_of, received, after, cost=FREE):
        x_part, y_part = small_call(
            relay_kernel,
            "relay",
            [*in_hbm(parts_of[1], parts_of[2]), *received],
            [parts_of[1].shape] * 2,
            2,
            after,
            cost,
        )
        return x_part, partner(x_part, "dp", 1), partner(y_part, "dp", 2)

    def gather_rest(near, chunk, after):
        x_half, y_half = cut(near[1], near[2], starts[chunk], sizes[chunk], after)
        return *near, partner(y_half, "dp", 1), partner(x_half, "dp", 2)

    up = gather_upstream(upstream)
    scale = (HB * subs) ** (-0.5)
    rows, width = hidden.shape
    forth = exchange(hidden.reshape(subs, SUB, width))
    pers = [size // 4 for size in sizes]
    unit0 = unit_grads(up, weight, scales, starts[0], sizes[0], pers[0], counts, cost=SOME)
    first0 = scatter_first(unit0)
    unit1 = unit_grads(
        up, weight, scales, starts[1], sizes[1], pers[1], counts, after=(unit0[0],)
    )
    first1 = scatter_first(unit1)
    relayed0, *second0 = scatter_second(unit0, first0, after=(unit1[0],))
    turned = transform(forth, after=(relayed0,), cost=LONG)
    rotated = exchange(turned)
    relayed1, *second1 = scatter_second(unit1, first1, after=(turned,), cost=LONG)
    matrices = backward_matrices(rot_block, after=(relayed1,))
    summed = local_backward(((unit0[0], *second0), (unit1[0], *second1)), matrices, scale)
    summed = gate(summed, after=(rotated,))
    back = exchange(summed.reshape(subs, SUB, width))
    (rotated,) = local_forward(rotated.reshape(rows, width), rot_block, (groups,), scale)
    near = (rotated, partner(rotated, "dp", 1), partner(rotated, "dp", 2))
    mixed = transform(back, cost=LONG)
    grad_hidden = exchange(mixed).reshape(rows, width)
    gathered0 = gather_rest(near, 0, (mixed,))
    gathered1 = gather_rest(near, 1, (mixed,))
    buffer, scale0 = weight_grads(
        gathered0, up, weight, scales, clip_mask, None, starts[0], sizes[0], pers[0], after=(mixed,)
    )
    buffer, scale1 = weight_grads(
        gathered1, up, weight, scales, clip_mask, buffer, starts[1], sizes[1], pers[1]
    )
    return grad_hidden, buffer, jnp.concatenate([scale0, scale1], axis=0)


def solution(mesh):
    return jax.shard_map(
        shards,
        mesh=mesh,
        in_specs=(
            P("dp", "tensor"),
            P("dp", None),
            P("tensor", "dp"),
            P("tensor", "dp"),
            P("tensor", "dp"),
            P(),
        ),
        out_specs=(P("dp", "tensor"), P("tensor", "dp"), P("tensor", "dp")),
        check_vma=False,
    )
```

```python
import functools

import jax
import jax.numpy as jnp
from jax import lax
from jax.experimental import pallas as pl
from jax.experimental.pallas import tpu as pltpu
from jax.sharding import PartitionSpec as P

HB = 128
GROUP = 128
SUB = 16
ROWS = 8
F32 = jnp.float32
BF16 = jnp.bfloat16


def nt_dot(a, b):
    return lax.dot_general(a, b, (((1,), (1,)), ((), ())), preferred_element_type=F32)


def nn_dot(a, b):
    return lax.dot_general(a, b, (((1,), (0,)), ((), ())), preferred_element_type=F32)


def split2(value):
    high = value.astype(BF16)
    return high, (value - high.astype(F32)).astype(BF16)


def sign_matrix():
    size = 2 * HB
    row = lax.broadcasted_iota(jnp.int32, (size, size), 0)
    col = lax.broadcasted_iota(jnp.int32, (size, size), 1)
    both = row & col
    parity = jnp.zeros((size, size), jnp.int32)
    for bit in range(HB.bit_length() - 1):
        parity = parity ^ ((both >> bit) & 1)
    return jnp.where((row ^ col) < HB, (1 - 2 * parity).astype(F32), 0.0).astype(BF16)


def build_mixing(rot_ref, mix_ref, sign_ref, transposed):
    blocks = rot_ref.shape[0]
    size = blocks * ROWS
    row = lax.broadcasted_iota(jnp.int32, (size, blocks), 0)
    col = lax.broadcasted_iota(jnp.int32, (size, blocks), 1)
    pick = ((row >> 3) == col).astype(F32).astype(BF16)
    rows = lax.broadcasted_iota(jnp.int32, (size, size), 0)
    cols = lax.broadcasted_iota(jnp.int32, (size, size), 1)
    same = (rows & (ROWS - 1)) == (cols & (ROWS - 1))
    spread = [
        nt_dot(pick, part) if transposed else nn_dot(pick, part) for part in split2(rot_ref[...])
    ]
    for half, value in enumerate(spread):
        full = nt_dot(value.astype(BF16), pick)
        mix_ref[half * size : (half + 1) * size, :] = jnp.where(same, full, 0.0).astype(BF16)
    sign_ref[...] = sign_matrix()


def mix_rows(tiles, mix_ref, sign_ref, scale):
    blocks = len(tiles[0])
    size = blocks * ROWS
    stacked = jnp.concatenate([jnp.concatenate(one, axis=0).astype(BF16) for one in tiles], axis=1)
    halves = nn_dot(mix_ref[...], stacked)
    mixed = (halves[:size] + halves[size:]).astype(BF16)
    results = []
    for j in range(0, len(tiles), 2):
        part = nn_dot(mixed[:, j * HB : (j + 2) * HB], sign_ref[...]) * scale
        results += [part[:, :HB].reshape(blocks, ROWS, HB), part[:, HB:].reshape(blocks, ROWS, HB)]
    return results


def forward_kernel(sizes, scale, x_ref, rot_ref, *refs):
    outs, (mix_ref, sign_ref) = refs[: len(sizes)], refs[len(sizes) :]
    blocks = rot_ref.shape[0]

    @pl.when(pl.program_id(0) == 0)
    def _():
        build_mixing(rot_ref, mix_ref, sign_ref, True)

    rows = x_ref.shape[0]
    wide = [x_ref[:, k * HB : (k + 1) * HB].astype(F32) for k in range(blocks)]
    tiles = [[one[j : j + ROWS] for one in wide] for j in range(0, rows, ROWS)]
    results = mix_rows(tiles, mix_ref, sign_ref, scale)
    for j in range(rows // SUB):
        both = jnp.concatenate([results[2 * j], results[2 * j + 1]], axis=1).astype(BF16)
        start = 0
        for size, out_ref in zip(sizes, outs):
            out_ref[j] = both[start : start + size]
            start += size


def backward_kernel(counts, scale, *refs):
    ins, (mix_ref, sign_ref, out_ref) = refs[: sum(counts)], refs[sum(counts) :]
    chunks = [ins[sum(counts[:i]) : sum(counts[: i + 1])] for i in range(len(counts))]
    rows = out_ref.shape[0]
    tiles = []
    for j in range(rows // SUB):
        wide = [
            sum(term[j, c].astype(F32) for term in terms)
            for terms in chunks
            for c in range(terms[0].shape[1])
        ]
        tiles += [[one[:ROWS] for one in wide], [one[ROWS:] for one in wide]]
    results = mix_rows(tiles, mix_ref, sign_ref, scale)
    for j in range(rows // SUB):
        both = jnp.concatenate([results[2 * j], results[2 * j + 1]], axis=1).astype(BF16)
        for k in range(both.shape[0]):
            out_ref[j * SUB : (j + 1) * SUB, k * HB : (k + 1) * HB] = both[k]


def local_scratch(blocks):
    return [
        pltpu.VMEM((2 * blocks * ROWS, blocks * ROWS), BF16),
        pltpu.VMEM((2 * HB, 2 * HB), BF16),
    ]


FREE = pl.CostEstimate(flops=0, bytes_accessed=0, transcendentals=0)
LONG = pl.CostEstimate(flops=10**12, bytes_accessed=0, transcendentals=0)
SOME = pl.CostEstimate(flops=5_000_000_000, bytes_accessed=0, transcendentals=0)
SMALL = 16 << 20

ANYWHERE = pl.BlockSpec(memory_space=pl.ANY)


def in_hbm(*values):
    return [pltpu.with_memory_space_constraint(value, pltpu.HBM) for value in values]


def drop_inputs(kernel, start, count):
    def run(*refs):
        kernel(*refs[:start], *refs[start + count :])

    return run


def local_forward(hidden, rot_block, sizes, scale=HB ** (-0.5)):
    rows, width = hidden.shape
    blocks = width // HB
    parts = 4
    return pl.pallas_call(
        functools.partial(forward_kernel, sizes, scale),
        grid=(rows // (SUB * parts),),
        in_specs=[
            pl.BlockSpec((SUB * parts, width), lambda i: (i, 0)),
            pl.BlockSpec((blocks, blocks), lambda i: (0, 0)),
        ],
        out_specs=[pl.BlockSpec((parts, size, SUB, HB), lambda i: (i, 0, 0, 0)) for size in sizes],
        out_shape=[pltpu.HBM((rows // SUB, size, SUB, HB), BF16) for size in sizes],
        scratch_shapes=local_scratch(blocks),
        compiler_params=pltpu.CompilerParams(vmem_limit_bytes=60 << 20),
        cost_estimate=FREE,
        name="local_forward",
    )(*in_hbm(hidden), rot_block)


def backward_matrices(rot_block, after=()):
    size = rot_block.shape[0] * ROWS
    shapes = [(2 * size, size), (2 * HB, 2 * HB)]
    return pl.pallas_call(
        drop_inputs(
            lambda rot_ref, *refs: build_mixing(rot_ref, *refs, False), 1, len(after)
        ),
        in_specs=[pl.BlockSpec(memory_space=pltpu.VMEM)] + [ANYWHERE] * len(after),
        out_specs=[pl.BlockSpec(memory_space=pltpu.VMEM)] * 2,
        out_shape=[pltpu.HBM(shape, BF16) for shape in shapes],
        compiler_params=pltpu.CompilerParams(vmem_limit_bytes=SMALL),
        cost_estimate=FREE,
        name="backward_matrices",
    )(rot_block, *after)


def local_backward(chunks, matrices, scale=HB ** (-0.5)):
    ins = [value for own, *far in chunks for value in (*in_hbm(own), *far)]
    count = ins[0].shape[0]
    width = sum(chunk[0].shape[1] for chunk in chunks) * HB
    parts = 4
    return pl.pallas_call(
        functools.partial(backward_kernel, [len(chunk) for chunk in chunks], scale),
        grid=(count // parts,),
        in_specs=[pl.BlockSpec((parts,) + v.shape[1:], lambda i: (i, 0, 0, 0)) for v in ins]
        + [pl.BlockSpec(value.shape, lambda i: (0, 0)) for value in matrices],
        out_specs=pl.BlockSpec((parts * SUB, width), lambda i: (i, 0)),
        out_shape=pltpu.HBM((count * SUB, width), BF16),
        compiler_params=pltpu.CompilerParams(vmem_limit_bytes=32 << 20),
        cost_estimate=FREE,
        name="local_backward",
    )(*ins, *in_hbm(*matrices))


def weight_spec(first, per, cols):
    return pl.BlockSpec(
        (pl.Element(per * GROUP), pl.Element(cols)), lambda i: ((first + i * per) * GROUP, 0)
    )


def units_kernel(first, per, up_ref, w_ref, s_ref, *refs):
    outs, (turned_ref, quant_ref) = refs[:-2], refs[-2:]
    base = first + pl.program_id(0) * per

    @pl.when(pl.program_id(0) == 0)
    def _():
        tile = 256
        for e in range(0, up_ref.shape[1], tile):
            turned_ref[e : e + tile, :] = up_ref[:, e : e + tile].T

    for g in range(per):
        rows = slice(g * GROUP, (g + 1) * GROUP)
        quant_ref[rows, :] = (w_ref[rows, :].astype(F32) * s_ref[pl.ds(base + g, 1), :]).astype(
            BF16
        )
    result = nn_dot(quant_ref[...], turned_ref[...]).astype(BF16)
    for g in range(per):
        turned = result[g * GROUP : (g + 1) * GROUP, :].T
        token = 0
        for out_ref in outs:
            for q in range(out_ref.shape[0]):
                out_ref[q, g] = turned[token : token + SUB, :]
                token += SUB


def unit_grads(up, weight, scales, first, size, per, counts, after=(), cost=FREE):
    tokens, cols = up.shape
    return pl.pallas_call(
        drop_inputs(functools.partial(units_kernel, first, per), 3, len(after)),
        grid=(size // per,),
        in_specs=[
            pl.BlockSpec((tokens, cols), lambda i: (0, 0)),
            weight_spec(first, per, cols),
            pl.BlockSpec(scales.shape, lambda i: (0, 0)),
        ]
        + [ANYWHERE] * len(after),
        out_specs=[pl.BlockSpec((count, per, SUB, HB), lambda i: (0, i, 0, 0)) for count in counts],
        out_shape=[pltpu.HBM((count, size, SUB, HB), BF16) for count in counts],
        scratch_shapes=[pltpu.VMEM((cols, tokens), BF16), pltpu.VMEM((per * GROUP, cols), BF16)],
        compiler_params=pltpu.CompilerParams(vmem_limit_bytes=40 << 20),
        cost_estimate=cost,
        name="unit_grads",
    )(up, *in_hbm(weight, scales), *in_hbm(*after))


def weights_kernel(first, per, pieces, *refs):
    rots = refs[:pieces]
    up_ref, w_ref, s_ref, m_ref = refs[pieces : pieces + 4]
    gw_ref, gs_ref = refs[-2:]
    step = pl.program_id(0)
    base = first + step * per
    left = jnp.concatenate(
        [
            jnp.concatenate(
                [rot_ref[q, g] for rot_ref in rots for q in range(rot_ref.shape[0])], axis=0
            )
            for g in range(per)
        ],
        axis=1,
    ).T
    cols = up_ref.shape[1]
    tile = min(256, cols)
    for e in range(cols // tile):
        span = slice(e * tile, (e + 1) * tile)
        grad = nn_dot(left, up_ref[:, span])
        for g in range(per):
            rows = slice(g * GROUP, (g + 1) * GROUP)
            piece = grad[rows]
            scale = s_ref[pl.ds(base + g, 1), span]
            kept = m_ref[pl.ds(base + g, 1), span].astype(F32) * scale
            gw_ref[rows, span] = (piece * kept).astype(BF16)
            gs_ref[pl.ds(step * per + g, 1), span] = jnp.sum(
                piece * w_ref[rows, span].astype(F32), axis=0, keepdims=True
            )


def weight_grads(rotated, up, weight, scales, mask, buffer, first, size, per, after=()):
    tokens, cols = up.shape
    specs = [
        pl.BlockSpec(
            tuple(map(pl.Element, (piece.shape[0], per, SUB, HB))),
            functools.partial(lambda place, i: (0, place + i * per, 0, 0), place),
        )
        for piece in rotated
        for place in ((0 if piece.shape[1] == size else first),)
    ] + [
        pl.BlockSpec((tokens, cols), lambda i: (0, 0)),
        weight_spec(first, per, cols),
        pl.BlockSpec(scales.shape, lambda i: (0, 0)),
        pl.BlockSpec(scales.shape, lambda i: (0, 0)),
    ]
    args = [*rotated, up, *in_hbm(weight, scales, mask)]
    aliases = {}
    if buffer is not None:
        aliases = {len(args): 0}
        args.append(buffer)
        specs.append(ANYWHERE)
    return pl.pallas_call(
        functools.partial(weights_kernel, first, per, len(rotated)),
        grid=(size // per,),
        in_specs=specs + [ANYWHERE] * len(after),
        out_specs=[
            weight_spec(first, per, cols),
            pl.BlockSpec((size, cols), lambda i: (0, 0)),
        ],
        out_shape=[
            pltpu.HBM(weight.shape, BF16),
            jax.ShapeDtypeStruct((size, cols), F32),
        ],
        input_output_aliases=aliases,
        compiler_params=pltpu.CompilerParams(vmem_limit_bytes=40 << 20),
        cost_estimate=LONG,
        name="weight_grads",
    )(*args, *in_hbm(*after))


def small_call(kernel, name, ins, outs, steps, after=(), cost=FREE):
    def spec(shape, dim):
        block = tuple(n // steps if d == dim else n for d, n in enumerate(shape))
        return pl.BlockSpec(
            block, lambda i: tuple(i if d == dim else 0 for d in range(len(shape)))
        )

    return pl.pallas_call(
        drop_inputs(kernel, len(ins), len(after)),
        grid=(steps,),
        in_specs=[spec(value.shape, 1) for value in ins] + [ANYWHERE] * len(after),
        out_specs=[spec(shape, 1) for shape in outs],
        out_shape=[pltpu.HBM(shape, BF16) for shape in outs],
        compiler_params=pltpu.CompilerParams(vmem_limit_bytes=SMALL),
        cost_estimate=cost,
        name=name,
    )(*ins, *in_hbm(*after))


def cut_kernel(start, x_ref, y_ref, x_out, y_out):
    size = x_out.shape[1]
    x_out[...] = x_ref[:, start : start + size]
    y_out[...] = y_ref[:, start : start + size]


def cut(x_part, y_part, start, size, after):
    subs, groups = x_part.shape[:2]
    half = subs // 2
    out = pl.BlockSpec((2, size, SUB, HB), lambda i: (i, 0, 0, 0))
    return pl.pallas_call(
        drop_inputs(functools.partial(cut_kernel, start), 2, len(after)),
        grid=(half // 2,),
        in_specs=[
            pl.BlockSpec((2, groups, SUB, HB), lambda i: (half // 2 + i, 0, 0, 0)),
            pl.BlockSpec((2, groups, SUB, HB), lambda i: (i, 0, 0, 0)),
        ]
        + [ANYWHERE] * len(after),
        out_specs=[out, out],
        out_shape=[pltpu.HBM((half, size, SUB, HB), BF16)] * 2,
        compiler_params=pltpu.CompilerParams(vmem_limit_bytes=SMALL),
        cost_estimate=FREE,
        name="cut",
    )(x_part, y_part, *in_hbm(*after))


def gate(value, after):
    return pl.pallas_call(
        drop_inputs(lambda x_ref, out_ref: None, 1, len(after)),
        in_specs=[ANYWHERE] * (1 + len(after)),
        out_specs=ANYWHERE,
        out_shape=pltpu.HBM(value.shape, value.dtype),
        input_output_aliases={0: 0},
        cost_estimate=FREE,
        name="gate",
    )(*in_hbm(value, *after))


def land_kernel(x_ref, out_ref, sems):
    size = x_ref.shape[0] // 4
    copies = [
        pltpu.make_async_copy(
            x_ref.at[pl.ds(i * size, size)], out_ref.at[pl.ds(i * size, size)], sems.at[i]
        )
        for i in range(4)
    ]
    for copy in copies:
        copy.start()
    for copy in copies:
        copy.wait()


def land(value):
    return pl.pallas_call(
        land_kernel,
        in_specs=[ANYWHERE],
        out_specs=ANYWHERE,
        out_shape=pltpu.HBM(value.shape, value.dtype),
        scratch_shapes=[pltpu.SemaphoreType.DMA((4,))],
        compiler_params=pltpu.CompilerParams(vmem_limit_bytes=SMALL),
        cost_estimate=FREE,
        name="land",
    )(value)


def transform_kernel(x_ref, out_ref):
    count = x_ref.shape[0]
    if len(x_ref.shape) == 4:
        size = out_ref.shape[1]
        span = (pl.ds(pl.program_id(0) * size, size),)
    else:
        size = out_ref.shape[2]
        span = (slice(None), pl.ds(pl.multiple_of(pl.program_id(0) * size, HB), size))
    values = [x_ref[(t, *span)].astype(F32) for t in range(count)]
    stride = 1
    while stride < count:
        for t in range(count):
            if not t & stride:
                a, b = values[t], values[t | stride]
                values[t], values[t | stride] = a + b, a - b
        stride *= 2
    for t in range(count):
        out_ref[t] = values[t].astype(BF16)


def transform(value, after=(), cost=FREE):
    steps = 4
    if value.ndim == 4:
        count, groups = value.shape[:2]
        out = pl.BlockSpec((count, groups // steps, SUB, HB), lambda i: (0, i, 0, 0))
    else:
        count, rows, width = value.shape
        out = pl.BlockSpec((count, rows, width // steps), lambda i: (0, 0, i))
    return pl.pallas_call(
        drop_inputs(transform_kernel, 1, len(after)),
        grid=(steps,),
        in_specs=[pl.BlockSpec(memory_space=pltpu.VMEM)] + [ANYWHERE] * len(after),
        out_specs=out,
        out_shape=pltpu.HBM(value.shape, BF16),
        compiler_params=pltpu.CompilerParams(vmem_limit_bytes=SMALL),
        cost_estimate=cost,
        name="transform",
    )(value, *in_hbm(*after))


def exchange(value):
    return lax.all_to_all(value, "tensor", split_axis=0, concat_axis=0, tiled=True)


def partner(value, axis, mask):
    size = lax.axis_size(axis)
    return lax.ppermute(value, axis, [(i, i ^ mask) for i in range(size)])


def mix_across(value):
    size = lax.axis_size("tensor")
    index = lax.axis_index("tensor")
    masks = [1 << i for i in range(size.bit_length() - 1)]
    for place, mask in enumerate(masks):
        other = partner(value, "tensor", mask).astype(F32)
        sign = jnp.where((index & mask) != 0, -1.0, 1.0).astype(F32)
        total = other + sign * value.astype(F32)
        if place == len(masks) - 1:
            total = total * size ** (-0.5)
        value = total.astype(BF16)
    return value


def gather_upstream(upstream):
    rows, width = upstream.shape
    parts = lax.axis_size("dp")
    cols = width // parts
    half = rows // 2
    index = lax.axis_index("dp")
    core = lax.axis_index("tensor") & 1
    own = lax.dynamic_slice(upstream, (0, index * cols), (rows, cols))
    mine = [
        partner(
            lax.dynamic_slice(upstream, (core * half, (index ^ m) * cols), (half, cols)), "dp", m
        )
        for m in range(1, parts)
    ]
    mine = jnp.stack(mine)
    other = partner(mine, "tensor", 1)
    low = jnp.where(core == 0, mine, other)
    high = jnp.where(core == 0, other, mine)
    far = jnp.concatenate([low, high], axis=1).reshape((parts - 1) * rows, cols)
    return jnp.concatenate([own, far], axis=0)


def relay_kernel(x_ref, y_ref, a_ref, b_ref, x_out, y_out):
    half = a_ref.shape[0]
    x_out[:half] = x_ref[:half]
    x_out[half:] = (x_ref[half:].astype(F32) + b_ref[...].astype(F32)).astype(BF16)
    y_out[:half] = (y_ref[:half].astype(F32) + a_ref[...].astype(F32)).astype(BF16)
    y_out[half:] = y_ref[half:]


def general_shards(hidden, upstream, weight, scales, clip_mask, rot_block):
    groups = scales.shape[0]
    rows = hidden.shape[0]
    parts = lax.axis_size("dp")
    subs = rows // SUB
    index = lax.axis_index("dp")

    up = gather_upstream(upstream)
    (local,) = local_forward(hidden, rot_block, (groups,))
    rotated = lax.all_gather(mix_across(local), "dp", axis=0, tiled=False)
    order = index ^ jnp.arange(parts)
    rotated = rotated[order].reshape((parts * subs,) + local.shape[1:])
    per = 4 if groups % 4 == 0 else 1
    (full,) = unit_grads(up, weight, scales, 0, groups, per, (parts * subs,))
    full = full.reshape((parts,) + local.shape)[order]
    mixed = mix_across(lax.psum_scatter(full, "dp", scatter_dimension=0, tiled=False))
    grad_weight, grad_scales = weight_grads(
        [rotated], up, weight, scales, clip_mask, None, 0, groups, per
    )
    grad_hidden = local_backward([[mixed]], backward_matrices(rot_block))
    return grad_hidden, grad_weight, grad_scales


def shards(hidden, upstream, weight, scales, clip_mask, rot_block):
    groups = scales.shape[0]
    subs = hidden.shape[0] // SUB
    if lax.axis_size("dp") != 4 or lax.axis_size("tensor") != subs or groups % 8 != 4:
        return general_shards(hidden, upstream, weight, scales, clip_mask, rot_block)
    per = 4
    units = groups // per
    sizes = (per * (units - units // 2), per * (units // 2))
    starts = (0, sizes[0])
    half = subs // 2
    counts = (subs, subs, subs, half, half)

    def scatter_first(parts_of):
        return partner(parts_of[3], "dp", 1), partner(parts_of[4], "dp", 2)

    def scatter_second(parts_of, received, after, cost=FREE):
        x_part, y_part = small_call(
            relay_kernel,
            "relay",
            [*in_hbm(parts_of[1], parts_of[2]), *received],
            [parts_of[1].shape] * 2,
            2,
            after,
            cost,
        )
        return x_part, partner(x_part, "dp", 1), partner(y_part, "dp", 2)

    def gather_rest(near, chunk, after):
        x_half, y_half = cut(near[1], near[2], starts[chunk], sizes[chunk], after)
        return *near, partner(y_half, "dp", 1), partner(x_half, "dp", 2)

    up = gather_upstream(upstream)
    scale = (HB * subs) ** (-0.5)
    rows, width = hidden.shape
    (local,) = local_forward(hidden, rot_block, (groups,), scale)
    forth = exchange(local)
    pers = [size // 4 for size in sizes]
    unit0 = unit_grads(up, weight, scales, starts[0], sizes[0], pers[0], counts, (local,), SOME)
    first0 = scatter_first(unit0)
    unit1 = unit_grads(
        up, weight, scales, starts[1], sizes[1], pers[1], counts, after=(unit0[0],)
    )
    first1 = scatter_first(unit1)
    relayed0, *second0 = scatter_second(unit0, first0, after=(unit1[0],))
    turned = transform(forth, after=(relayed0,), cost=LONG)
    rotated = exchange(turned)
    relayed1, *second1 = scatter_second(unit1, first1, after=(turned,), cost=LONG)
    matrices = backward_matrices(rot_block, after=(relayed1,))
    summed = local_backward(((unit0[0], *second0), (unit1[0], *second1)), matrices, scale)
    summed = gate(summed, after=(rotated,))
    back = exchange(summed).reshape(subs, SUB, width)
    near = (rotated, partner(rotated, "dp", 1), partner(rotated, "dp", 2))
    gathered0 = gather_rest(near, 0, ())
    mixed = transform(back, cost=LONG)
    grad_hidden = land(exchange(mixed.reshape(rows, width)))
    gathered1 = gather_rest(near, 1, (mixed,))
    buffer, scale0 = weight_grads(
        gathered0, up, weight, scales, clip_mask, None, starts[0], sizes[0], pers[0], after=(mixed,)
    )
    buffer, scale1 = weight_grads(
        gathered1, up, weight, scales, clip_mask, buffer, starts[1], sizes[1], pers[1]
    )
    return grad_hidden, buffer, jnp.concatenate([scale0, scale1], axis=0)


def solution(mesh):
    return jax.shard_map(
        shards,
        mesh=mesh,
        in_specs=(
            P("dp", "tensor"),
            P("dp", None),
            P("tensor", "dp"),
            P("tensor", "dp"),
            P("tensor", "dp"),
            P(),
        ),
        out_specs=(P("dp", "tensor"), P("tensor", "dp"), P("tensor", "dp")),
        check_vma=False,
    )
```

```python
import functools

import jax
import jax.numpy as jnp
from jax import lax
from jax.experimental import pallas as pl
from jax.experimental.pallas import tpu as pltpu
from jax.sharding import PartitionSpec as P

HB = 128
GROUP = 128
SUB = 16
ROWS = 8
F32 = jnp.float32
BF16 = jnp.bfloat16


def nt_dot(a, b):
    return lax.dot_general(a, b, (((1,), (1,)), ((), ())), preferred_element_type=F32)


def nn_dot(a, b):
    return lax.dot_general(a, b, (((1,), (0,)), ((), ())), preferred_element_type=F32)


def split2(value):
    high = value.astype(BF16)
    return high, (value - high.astype(F32)).astype(BF16)


def sign_matrix():
    size = 2 * HB
    row = lax.broadcasted_iota(jnp.int32, (size, size), 0)
    col = lax.broadcasted_iota(jnp.int32, (size, size), 1)
    both = row & col
    parity = jnp.zeros((size, size), jnp.int32)
    for bit in range(HB.bit_length() - 1):
        parity = parity ^ ((both >> bit) & 1)
    return jnp.where((row ^ col) < HB, (1 - 2 * parity).astype(F32), 0.0).astype(BF16)


def build_mixing(rot_ref, mix_ref, sign_ref, transposed):
    blocks = rot_ref.shape[0]
    size = blocks * ROWS
    row = lax.broadcasted_iota(jnp.int32, (size, blocks), 0)
    col = lax.broadcasted_iota(jnp.int32, (size, blocks), 1)
    pick = ((row >> 3) == col).astype(F32).astype(BF16)
    rows = lax.broadcasted_iota(jnp.int32, (size, size), 0)
    cols = lax.broadcasted_iota(jnp.int32, (size, size), 1)
    same = (rows & (ROWS - 1)) == (cols & (ROWS - 1))
    spread = [
        nt_dot(pick, part) if transposed else nn_dot(pick, part) for part in split2(rot_ref[...])
    ]
    for half, value in enumerate(spread):
        full = nt_dot(value.astype(BF16), pick)
        mix_ref[half * size : (half + 1) * size, :] = jnp.where(same, full, 0.0).astype(BF16)
    sign_ref[...] = sign_matrix()


def mix_rows(tiles, mix_ref, sign_ref, scale):
    blocks = len(tiles[0])
    size = blocks * ROWS
    stacked = jnp.concatenate([jnp.concatenate(one, axis=0).astype(BF16) for one in tiles], axis=1)
    halves = nn_dot(mix_ref[...], stacked)
    mixed = (halves[:size] + halves[size:]).astype(BF16)
    results = []
    for j in range(0, len(tiles), 2):
        part = nn_dot(mixed[:, j * HB : (j + 2) * HB], sign_ref[...]) * scale
        results += [part[:, :HB].reshape(blocks, ROWS, HB), part[:, HB:].reshape(blocks, ROWS, HB)]
    return results


def forward_kernel(sizes, scale, x_ref, rot_ref, *refs):
    outs, (mix_ref, sign_ref) = refs[: len(sizes)], refs[len(sizes) :]
    blocks = rot_ref.shape[0]

    @pl.when(pl.program_id(0) == 0)
    def _():
        build_mixing(rot_ref, mix_ref, sign_ref, True)

    rows = x_ref.shape[0]
    wide = [x_ref[:, k * HB : (k + 1) * HB].astype(F32) for k in range(blocks)]
    tiles = [[one[j : j + ROWS] for one in wide] for j in range(0, rows, ROWS)]
    results = mix_rows(tiles, mix_ref, sign_ref, scale)
    for j in range(rows // SUB):
        both = jnp.concatenate([results[2 * j], results[2 * j + 1]], axis=1).astype(BF16)
        start = 0
        for size, out_ref in zip(sizes, outs):
            out_ref[j] = both[start : start + size]
            start += size


def backward_kernel(counts, scale, *refs):
    ins, (mix_ref, sign_ref, out_ref) = refs[: sum(counts)], refs[sum(counts) :]
    chunks = [ins[sum(counts[:i]) : sum(counts[: i + 1])] for i in range(len(counts))]
    rows = out_ref.shape[0]
    tiles = []
    for j in range(rows // SUB):
        wide = [
            sum(term[j, c].astype(F32) for term in terms)
            for terms in chunks
            for c in range(terms[0].shape[1])
        ]
        tiles += [[one[:ROWS] for one in wide], [one[ROWS:] for one in wide]]
    results = mix_rows(tiles, mix_ref, sign_ref, scale)
    for j in range(rows // SUB):
        both = jnp.concatenate([results[2 * j], results[2 * j + 1]], axis=1).astype(BF16)
        for k in range(both.shape[0]):
            out_ref[j * SUB : (j + 1) * SUB, k * HB : (k + 1) * HB] = both[k]


def local_scratch(blocks):
    return [
        pltpu.VMEM((2 * blocks * ROWS, blocks * ROWS), BF16),
        pltpu.VMEM((2 * HB, 2 * HB), BF16),
    ]


FREE = pl.CostEstimate(flops=0, bytes_accessed=0, transcendentals=0)
LONG = pl.CostEstimate(flops=10**12, bytes_accessed=0, transcendentals=0)
SOME = pl.CostEstimate(flops=5_000_000_000, bytes_accessed=0, transcendentals=0)
SMALL = 16 << 20

ANYWHERE = pl.BlockSpec(memory_space=pl.ANY)


def in_hbm(*values):
    return [pltpu.with_memory_space_constraint(value, pltpu.HBM) for value in values]


def drop_inputs(kernel, start, count):
    def run(*refs):
        kernel(*refs[:start], *refs[start + count :])

    return run


def local_forward(hidden, rot_block, sizes, scale=HB ** (-0.5)):
    rows, width = hidden.shape
    blocks = width // HB
    parts = 4
    return pl.pallas_call(
        functools.partial(forward_kernel, sizes, scale),
        grid=(rows // (SUB * parts),),
        in_specs=[
            pl.BlockSpec((SUB * parts, width), lambda i: (i, 0)),
            pl.BlockSpec((blocks, blocks), lambda i: (0, 0)),
        ],
        out_specs=[pl.BlockSpec((parts, size, SUB, HB), lambda i: (i, 0, 0, 0)) for size in sizes],
        out_shape=[pltpu.HBM((rows // SUB, size, SUB, HB), BF16) for size in sizes],
        scratch_shapes=local_scratch(blocks),
        compiler_params=pltpu.CompilerParams(vmem_limit_bytes=60 << 20),
        cost_estimate=FREE,
        name="local_forward",
    )(*in_hbm(hidden), rot_block)


def backward_matrices(rot_block, after=()):
    size = rot_block.shape[0] * ROWS
    shapes = [(2 * size, size), (2 * HB, 2 * HB)]
    return pl.pallas_call(
        drop_inputs(
            lambda rot_ref, *refs: build_mixing(rot_ref, *refs, False), 1, len(after)
        ),
        in_specs=[pl.BlockSpec(memory_space=pltpu.VMEM)] + [ANYWHERE] * len(after),
        out_specs=[pl.BlockSpec(memory_space=pltpu.VMEM)] * 2,
        out_shape=[pltpu.HBM(shape, BF16) for shape in shapes],
        compiler_params=pltpu.CompilerParams(vmem_limit_bytes=SMALL),
        cost_estimate=FREE,
        name="backward_matrices",
    )(rot_block, *after)


def local_backward(chunks, matrices, scale=HB ** (-0.5)):
    ins = [value for own, *far in chunks for value in (*in_hbm(own), *far)]
    count = ins[0].shape[0]
    width = sum(chunk[0].shape[1] for chunk in chunks) * HB
    parts = 4
    return pl.pallas_call(
        functools.partial(backward_kernel, [len(chunk) for chunk in chunks], scale),
        grid=(count // parts,),
        in_specs=[pl.BlockSpec((parts,) + v.shape[1:], lambda i: (i, 0, 0, 0)) for v in ins]
        + [pl.BlockSpec(value.shape, lambda i: (0, 0)) for value in matrices],
        out_specs=pl.BlockSpec((parts * SUB, width), lambda i: (i, 0)),
        out_shape=pltpu.HBM((count * SUB, width), BF16),
        compiler_params=pltpu.CompilerParams(vmem_limit_bytes=32 << 20),
        cost_estimate=FREE,
        name="local_backward",
    )(*ins, *in_hbm(*matrices))


def weight_spec(first, per, cols):
    return pl.BlockSpec(
        (pl.Element(per * GROUP), pl.Element(cols)), lambda i: ((first + i * per) * GROUP, 0)
    )


def units_kernel(first, per, up_ref, w_ref, s_ref, *refs):
    outs, (turned_ref, quant_ref) = refs[:-2], refs[-2:]
    base = first + pl.program_id(0) * per

    @pl.when(pl.program_id(0) == 0)
    def _():
        tile = 256
        for e in range(0, up_ref.shape[1], tile):
            turned_ref[e : e + tile, :] = up_ref[:, e : e + tile].T

    for g in range(per):
        rows = slice(g * GROUP, (g + 1) * GROUP)
        quant_ref[rows, :] = (w_ref[rows, :].astype(F32) * s_ref[pl.ds(base + g, 1), :]).astype(
            BF16
        )
    result = nn_dot(quant_ref[...], turned_ref[...]).astype(BF16)
    for g in range(per):
        turned = result[g * GROUP : (g + 1) * GROUP, :].T
        token = 0
        for out_ref in outs:
            for q in range(out_ref.shape[0]):
                out_ref[q, g] = turned[token : token + SUB, :]
                token += SUB


def unit_grads(up, weight, scales, first, size, per, counts, after=(), cost=FREE):
    tokens, cols = up.shape
    return pl.pallas_call(
        drop_inputs(functools.partial(units_kernel, first, per), 3, len(after)),
        grid=(size // per,),
        in_specs=[
            pl.BlockSpec((tokens, cols), lambda i: (0, 0)),
            weight_spec(first, per, cols),
            pl.BlockSpec(scales.shape, lambda i: (0, 0)),
        ]
        + [ANYWHERE] * len(after),
        out_specs=[pl.BlockSpec((count, per, SUB, HB), lambda i: (0, i, 0, 0)) for count in counts],
        out_shape=[pltpu.HBM((count, size, SUB, HB), BF16) for count in counts],
        scratch_shapes=[pltpu.VMEM((cols, tokens), BF16), pltpu.VMEM((per * GROUP, cols), BF16)],
        compiler_params=pltpu.CompilerParams(vmem_limit_bytes=40 << 20),
        cost_estimate=cost,
        name="unit_grads",
    )(up, *in_hbm(weight, scales), *in_hbm(*after))


def weights_kernel(first, per, pieces, *refs):
    rots = refs[:pieces]
    up_ref, w_ref, s_ref, m_ref = refs[pieces : pieces + 4]
    gw_ref, gs_ref = refs[-2:]
    step = pl.program_id(0)
    base = first + step * per
    left = jnp.concatenate(
        [
            jnp.concatenate(
                [rot_ref[q, g] for rot_ref in rots for q in range(rot_ref.shape[0])], axis=0
            )
            for g in range(per)
        ],
        axis=1,
    ).T
    cols = up_ref.shape[1]
    tile = min(256, cols)
    for e in range(cols // tile):
        span = slice(e * tile, (e + 1) * tile)
        grad = nn_dot(left, up_ref[:, span])
        for g in range(per):
            rows = slice(g * GROUP, (g + 1) * GROUP)
            piece = grad[rows]
            scale = s_ref[pl.ds(base + g, 1), span]
            kept = m_ref[pl.ds(base + g, 1), span].astype(F32) * scale
            gw_ref[rows, span] = (piece * kept).astype(BF16)
            gs_ref[pl.ds(step * per + g, 1), span] = jnp.sum(
                piece * w_ref[rows, span].astype(F32), axis=0, keepdims=True
            )


def weight_grads(rotated, up, weight, scales, mask, buffer, first, size, per, after=()):
    tokens, cols = up.shape
    specs = [
        pl.BlockSpec(
            tuple(map(pl.Element, (piece.shape[0], per, SUB, HB))),
            functools.partial(lambda place, i: (0, place + i * per, 0, 0), place),
        )
        for piece in rotated
        for place in ((0 if piece.shape[1] == size else first),)
    ] + [
        pl.BlockSpec((tokens, cols), lambda i: (0, 0)),
        weight_spec(first, per, cols),
        pl.BlockSpec(scales.shape, lambda i: (0, 0)),
        pl.BlockSpec(scales.shape, lambda i: (0, 0)),
    ]
    args = [*rotated, up, *in_hbm(weight, scales, mask)]
    aliases = {}
    if buffer is not None:
        aliases = {len(args): 0}
        args.append(buffer)
        specs.append(ANYWHERE)
    return pl.pallas_call(
        functools.partial(weights_kernel, first, per, len(rotated)),
        grid=(size // per,),
        in_specs=specs + [ANYWHERE] * len(after),
        out_specs=[
            weight_spec(first, per, cols),
            pl.BlockSpec((size, cols), lambda i: (0, 0)),
        ],
        out_shape=[
            pltpu.HBM(weight.shape, BF16),
            jax.ShapeDtypeStruct((size, cols), F32),
        ],
        input_output_aliases=aliases,
        compiler_params=pltpu.CompilerParams(vmem_limit_bytes=40 << 20),
        cost_estimate=LONG,
        name="weight_grads",
    )(*args, *in_hbm(*after))


def small_call(kernel, name, ins, outs, steps, after=(), cost=FREE):
    def spec(shape, dim):
        block = tuple(n // steps if d == dim else n for d, n in enumerate(shape))
        return pl.BlockSpec(
            block, lambda i: tuple(i if d == dim else 0 for d in range(len(shape)))
        )

    return pl.pallas_call(
        drop_inputs(kernel, len(ins), len(after)),
        grid=(steps,),
        in_specs=[spec(value.shape, 1) for value in ins] + [ANYWHERE] * len(after),
        out_specs=[spec(shape, 1) for shape in outs],
        out_shape=[pltpu.HBM(shape, BF16) for shape in outs],
        compiler_params=pltpu.CompilerParams(vmem_limit_bytes=SMALL),
        cost_estimate=cost,
        name=name,
    )(*ins, *in_hbm(*after))


def cut_kernel(start, x_ref, y_ref, x_out, y_out):
    size = x_out.shape[1]
    x_out[...] = x_ref[:, start : start + size]
    y_out[...] = y_ref[:, start : start + size]


def cut(x_part, y_part, start, size, after):
    subs, groups = x_part.shape[:2]
    half = subs // 2
    out = pl.BlockSpec((2, size, SUB, HB), lambda i: (i, 0, 0, 0))
    return pl.pallas_call(
        drop_inputs(functools.partial(cut_kernel, start), 2, len(after)),
        grid=(half // 2,),
        in_specs=[
            pl.BlockSpec((2, groups, SUB, HB), lambda i: (half // 2 + i, 0, 0, 0)),
            pl.BlockSpec((2, groups, SUB, HB), lambda i: (i, 0, 0, 0)),
        ]
        + [ANYWHERE] * len(after),
        out_specs=[out, out],
        out_shape=[pltpu.HBM((half, size, SUB, HB), BF16)] * 2,
        compiler_params=pltpu.CompilerParams(vmem_limit_bytes=SMALL),
        cost_estimate=FREE,
        name="cut",
    )(x_part, y_part, *in_hbm(*after))


def gate(value, after):
    return pl.pallas_call(
        drop_inputs(lambda x_ref, out_ref: None, 1, len(after)),
        in_specs=[ANYWHERE] * (1 + len(after)),
        out_specs=ANYWHERE,
        out_shape=pltpu.HBM(value.shape, value.dtype),
        input_output_aliases={0: 0},
        cost_estimate=FREE,
        name="gate",
    )(*in_hbm(value, *after))


def land_kernel(x_ref, out_ref):
    out_ref[...] = x_ref[...]


def land(value):
    steps = 4
    block = pl.BlockSpec((value.shape[0] // steps, value.shape[1]), lambda i: (i, 0))
    return pl.pallas_call(
        land_kernel,
        grid=(steps,),
        in_specs=[block],
        out_specs=block,
        out_shape=pltpu.HBM(value.shape, value.dtype),
        compiler_params=pltpu.CompilerParams(vmem_limit_bytes=SMALL),
        cost_estimate=FREE,
        name="land",
    )(value)


def transform_kernel(x_ref, out_ref):
    count = x_ref.shape[0]
    if len(x_ref.shape) == 4:
        size = out_ref.shape[1]
        span = (pl.ds(pl.program_id(0) * size, size),)
    else:
        size = out_ref.shape[2]
        span = (slice(None), pl.ds(pl.multiple_of(pl.program_id(0) * size, HB), size))
    values = [x_ref[(t, *span)].astype(F32) for t in range(count)]
    stride = 1
    while stride < count:
        for t in range(count):
            if not t & stride:
                a, b = values[t], values[t | stride]
                values[t], values[t | stride] = a + b, a - b
        stride *= 2
    for t in range(count):
        out_ref[t] = values[t].astype(BF16)


def transform(value, after=(), cost=FREE):
    steps = 4
    if value.ndim == 4:
        count, groups = value.shape[:2]
        out = pl.BlockSpec((count, groups // steps, SUB, HB), lambda i: (0, i, 0, 0))
    else:
        count, rows, width = value.shape
        out = pl.BlockSpec((count, rows, width // steps), lambda i: (0, 0, i))
    return pl.pallas_call(
        drop_inputs(transform_kernel, 1, len(after)),
        grid=(steps,),
        in_specs=[pl.BlockSpec(memory_space=pltpu.VMEM)] + [ANYWHERE] * len(after),
        out_specs=out,
        out_shape=pltpu.HBM(value.shape, BF16),
        compiler_params=pltpu.CompilerParams(vmem_limit_bytes=SMALL),
        cost_estimate=cost,
        name="transform",
    )(value, *in_hbm(*after))


def exchange(value):
    return lax.all_to_all(value, "tensor", split_axis=0, concat_axis=0, tiled=True)


def partner(value, axis, mask):
    size = lax.axis_size(axis)
    return lax.ppermute(value, axis, [(i, i ^ mask) for i in range(size)])


def mix_across(value):
    size = lax.axis_size("tensor")
    index = lax.axis_index("tensor")
    masks = [1 << i for i in range(size.bit_length() - 1)]
    for place, mask in enumerate(masks):
        other = partner(value, "tensor", mask).astype(F32)
        sign = jnp.where((index & mask) != 0, -1.0, 1.0).astype(F32)
        total = other + sign * value.astype(F32)
        if place == len(masks) - 1:
            total = total * size ** (-0.5)
        value = total.astype(BF16)
    return value


def gather_upstream(upstream):
    rows, width = upstream.shape
    parts = lax.axis_size("dp")
    cols = width // parts
    half = rows // 2
    index = lax.axis_index("dp")
    core = lax.axis_index("tensor") & 1
    own = lax.dynamic_slice(upstream, (0, index * cols), (rows, cols))
    mine = [
        partner(
            lax.dynamic_slice(upstream, (core * half, (index ^ m) * cols), (half, cols)), "dp", m
        )
        for m in range(1, parts)
    ]
    mine = jnp.stack(mine)
    other = partner(mine, "tensor", 1)
    low = jnp.where(core == 0, mine, other)
    high = jnp.where(core == 0, other, mine)
    far = jnp.concatenate([low, high], axis=1).reshape((parts - 1) * rows, cols)
    return jnp.concatenate([own, far], axis=0)


def relay_kernel(x_ref, y_ref, a_ref, b_ref, x_out, y_out):
    half = a_ref.shape[0]
    x_out[:half] = x_ref[:half]
    x_out[half:] = (x_ref[half:].astype(F32) + b_ref[...].astype(F32)).astype(BF16)
    y_out[:half] = (y_ref[:half].astype(F32) + a_ref[...].astype(F32)).astype(BF16)
    y_out[half:] = y_ref[half:]


def general_shards(hidden, upstream, weight, scales, clip_mask, rot_block):
    groups = scales.shape[0]
    rows = hidden.shape[0]
    parts = lax.axis_size("dp")
    subs = rows // SUB
    index = lax.axis_index("dp")

    up = gather_upstream(upstream)
    (local,) = local_forward(hidden, rot_block, (groups,))
    rotated = lax.all_gather(mix_across(local), "dp", axis=0, tiled=False)
    order = index ^ jnp.arange(parts)
    rotated = rotated[order].reshape((parts * subs,) + local.shape[1:])
    per = 4 if groups % 4 == 0 else 1
    (full,) = unit_grads(up, weight, scales, 0, groups, per, (parts * subs,))
    full = full.reshape((parts,) + local.shape)[order]
    mixed = mix_across(lax.psum_scatter(full, "dp", scatter_dimension=0, tiled=False))
    grad_weight, grad_scales = weight_grads(
        [rotated], up, weight, scales, clip_mask, None, 0, groups, per
    )
    grad_hidden = local_backward([[mixed]], backward_matrices(rot_block))
    return grad_hidden, grad_weight, grad_scales


def shards(hidden, upstream, weight, scales, clip_mask, rot_block):
    groups = scales.shape[0]
    subs = hidden.shape[0] // SUB
    if lax.axis_size("dp") != 4 or lax.axis_size("tensor") != subs or groups % 8 != 4:
        return general_shards(hidden, upstream, weight, scales, clip_mask, rot_block)
    per = 4
    units = groups // per
    sizes = (per * (units - units // 2), per * (units // 2))
    starts = (0, sizes[0])
    half = subs // 2
    counts = (subs, subs, subs, half, half)

    def scatter_first(parts_of):
        return partner(parts_of[3], "dp", 1), partner(parts_of[4], "dp", 2)

    def scatter_second(parts_of, received, after, cost=FREE):
        x_part, y_part = small_call(
            relay_kernel,
            "relay",
            [*in_hbm(parts_of[1], parts_of[2]), *received],
            [parts_of[1].shape] * 2,
            2,
            after,
            cost,
        )
        return x_part, partner(x_part, "dp", 1), partner(y_part, "dp", 2)

    def gather_rest(near, chunk, after):
        x_half, y_half = cut(near[1], near[2], starts[chunk], sizes[chunk], after)
        return *near, partner(y_half, "dp", 1), partner(x_half, "dp", 2)

    up = gather_upstream(upstream)
    scale = (HB * subs) ** (-0.5)
    rows, width = hidden.shape
    (local,) = local_forward(hidden, rot_block, (groups,), scale)
    forth = exchange(local)
    pers = [size // 4 for size in sizes]
    unit0 = unit_grads(up, weight, scales, starts[0], sizes[0], pers[0], counts, (local,), SOME)
    first0 = scatter_first(unit0)
    unit1 = unit_grads(
        up, weight, scales, starts[1], sizes[1], pers[1], counts, after=(unit0[0],)
    )
    first1 = scatter_first(unit1)
    relayed0, *second0 = scatter_second(unit0, first0, after=(unit1[0],))
    turned = transform(forth, after=(relayed0,), cost=LONG)
    rotated = exchange(turned)
    relayed1, *second1 = scatter_second(unit1, first1, after=(turned,), cost=LONG)
    matrices = backward_matrices(rot_block, after=(relayed1,))
    summed = local_backward(((unit0[0], *second0), (unit1[0], *second1)), matrices, scale)
    summed = gate(summed, after=(rotated,))
    back = exchange(summed).reshape(subs, SUB, width)
    near = (rotated, partner(rotated, "dp", 1), partner(rotated, "dp", 2))
    gathered0 = gather_rest(near, 0, ())
    mixed = transform(back, cost=LONG)
    grad_hidden = land(exchange(mixed.reshape(rows, width)))
    gathered1 = gather_rest(near, 1, (mixed,))
    buffer, scale0 = weight_grads(
        gathered0, up, weight, scales, clip_mask, None, starts[0], sizes[0], pers[0], after=(mixed,)
    )
    buffer, scale1 = weight_grads(
        gathered1, up, weight, scales, clip_mask, buffer, starts[1], sizes[1], pers[1]
    )
    return grad_hidden, buffer, jnp.concatenate([scale0, scale1], axis=0)


def solution(mesh):
    return jax.shard_map(
        shards,
        mesh=mesh,
        in_specs=(
            P("dp", "tensor"),
            P("dp", None),
            P("tensor", "dp"),
            P("tensor", "dp"),
            P("tensor", "dp"),
            P(),
        ),
        out_specs=(P("dp", "tensor"), P("tensor", "dp"), P("tensor", "dp")),
        check_vma=False,
    )
```
